32 devices in a mesh: ctx: 16 (over z, y, x), wt: 2 (over core).
Axes of the slice: x: 2, y: 2, z: 4, core: 2. Of those that a mesh axis runs over, the one named last changes fastest.
Arguments:
- tokens: bfloat16 [4096, 2048], P('ctx'), may hold values from -6 to 6
- layer_input: bfloat16 [4096, 256], P('ctx'), may hold values from -6 to 6
- out_grad: bfloat16 [4096, 2048], P('ctx'), may hold values from -6 to 6
- block_device: int32 [1, 16], replicated, may hold values from 0 to 15, each once within a row
- adapter_pick: int32 [1, 8], replicated, may hold values from 0 to 7, as said below
- norm_gains: bfloat16 [6, 2048], replicated, may hold values from 0.25 to 1.75
- head_norm_gains: bfloat16 [2, 256], replicated, may hold values from 0.25 to 1.75
- query_weight: bfloat16 [2048, 2048], P('ctx', 'wt'), may hold values from -0.125 to 0.125
- key_matrix: bfloat16 [2048, 512], P('ctx', 'wt'), may hold values from -0.125 to 0.125
- value_matrix: bfloat16 [2048, 512], P('ctx', 'wt'), may hold values from -0.125 to 0.125
- gate_weight: bfloat16 [2048, 8192], P('ctx', 'wt'), may hold values from -0.125 to 0.125
- up_weight: bfloat16 [2048, 8192], P('ctx', 'wt'), may hold values from -0.125 to 0.125
- out_weight: bfloat16 [2048, 2048], P('wt', 'ctx'), may hold values from -0.125 to 0.125
- down_weight: bfloat16 [8192, 2048], P('wt', 'ctx'), may hold values from -0.0625 to 0.0625
- laurel_left: bfloat16 [2048, 64], replicated, may hold values from -0.125 to 0.125
- laurel_right: bfloat16 [64, 2048], replicated, may hold values from -0.75 to 0.75
- layer_gate: bfloat16 [2048, 256], replicated, may hold values from -0.125 to 0.125
- layer_lift: bfloat16 [256, 2048], replicated, may hold values from -0.375 to 0.375
- query_shrink: bfloat16 [128, 2048], replicated, may hold values from -0.125 to 0.125
- key_shrink: bfloat16 [128, 2048], replicated, may hold values from -0.125 to 0.125
- value_shrink: bfloat16 [128, 2048], replicated, may hold values from -0.125 to 0.125
- gate_shrink: bfloat16 [128, 2048], replicated, may hold values from -0.125 to 0.125
- up_shrink: bfloat16 [128, 2048], replicated, may hold values from -0.125 to 0.125
- out_shrink: bfloat16 [128, 2048], P(None, 'wt'), may hold values from -0.125 to 0.125
- down_shrink: bfloat16 [128, 8192], P(None, 'wt'), may hold values from -0.0625 to 0.0625
- query_expand: bfloat16 [128, 2048], P(None, 'wt'), may hold values from -1.5 to 1.5
- key_widen_maps: bfloat16 [128, 512], P(None, 'wt'), may hold values from -1.5 to 1.5
- value_widen_maps: bfloat16 [128, 512], P(None, 'wt'), may hold values from -1.5 to 1.5
- gate_expand: bfloat16 [128, 8192], P(None, 'wt'), may hold values from -1.5 to 1.5
- up_expand: bfloat16 [128, 8192], P(None, 'wt'), may hold values from -1.5 to 1.5
- out_expand: bfloat16 [128, 2048], replicated, may hold values from -1.5 to 1.5
- down_expand: bfloat16 [128, 2048], replicated, may hold values from -1.5 to 1.5
Outputs:
- layer_output: bfloat16 [4096, 2048], P('ctx')
- input_grad: float32 [4096, 2048], P('ctx')
- layer_input_grad: float32 [4096, 256], P('ctx')
- query_shrink_grad: float32 [128, 2048], P(('ctx', 'wt'))
- key_shrink_grad: float32 [128, 2048], P(('ctx', 'wt'))
- value_shrink_grad: float32 [128, 2048], P(('ctx', 'wt'))
- gate_shrink_grad: float32 [128, 2048], P(('ctx', 'wt'))
- up_shrink_grad: float32 [128, 2048], P(('ctx', 'wt'))
- out_shrink_grad: float32 [128, 2048], P('ctx', 'wt')
- down_shrink_grad: float32 [128, 8192], P('ctx', 'wt')
- query_expand_grad: float32 [128, 2048], P('ctx', 'wt')
- key_expand_grad: float32 [128, 512], P('ctx', 'wt')
- value_expand_grad: float32 [128, 512], P('ctx', 'wt')
- gate_expand_grad: float32 [128, 8192], P('ctx', 'wt')
- up_expand_grad: float32 [128, 8192], P('ctx', 'wt')
- out_expand_grad: float32 [128, 2048], P(('ctx', 'wt'))
- down_expand_grad: float32 [128, 2048], P(('ctx', 'wt'))
The draws below stay inside these ranges and needn't reach their ends.
Inputs may be any that keep to these rules, and one draw needn't show every extreme that they name: Each row of block_device names every index along ctx once: block b of group g (its tokens b * 256 to b * 256 + 255) is held by index block_device[g, b]. `adapter_pick`: column c names the adapter of continuation c + 1 of the group; the continuations of one group have different adapters.
All inputs are finite; a program needn't handle non-finite values.
Results may differ from the reference program's by a relative error of at most 0.019.
Values may be sent and summed in bfloat16 or wider, within the bound.
No kernel may reach another device: no remote copies, remote signals or barrier semaphores. Data moves between devices by JAX's collectives and lax.ppermute only.
A program may use at most 256 MiB of HBM per device.

```python
import math
import jax
import jax.numpy as jnp
from jax import lax

MODEL_WIDTH = 2048
QUERY_HEADS = 8
KEY_VALUE_HEADS = 2
HEAD_SIZE = 256
FF = 8192
LR = 64
PLE = 256
ADAPTER_COUNT = 8
ADAPTER_RANK = 16
PROMPT = 2048
CONT = 256
NCONT = 8
TOK_DEV = 256
GTOK = 4096
GROUPS = 1
BLOCK = 256
TOKENS = 4096
N_CTX = 16


def draw_adapter_pick(key, part):
    key = jax.random.fold_in(key, 5)
    group_keys = jax.random.split(key, GROUPS)
    orders = jax.vmap(lambda single: jax.random.permutation(single, ADAPTER_COUNT))(group_keys)
    return orders[:, :NCONT].astype(jnp.int32)


def steps_of(rng, extent, cuts, smallest, top_value):
    def one(position, parts):
        steps = jax.random.uniform(jax.random.fold_in(jax.random.fold_in(rng, 6), position), (parts,), jnp.float32, smallest / len(cuts), top_value / len(cuts))
        return jnp.repeat(jnp.exp(steps), extent[position] // parts).reshape((-1,) + (1,) * (len(extent) - position - 1))

    gain = one(*cuts[0])
    for cut in cuts[1:]:
        gain = gain * one(*cut)
    return gain


def centred(stream_key, shape, scale, reach, cuts=(), kind=jnp.bfloat16):
    gain = steps_of(stream_key, shape, cuts, -0.22, 0.18) if cuts else 1.0
    array = jax.random.normal(stream_key, shape, jnp.float32) * scale * gain
    return jnp.minimum(jnp.maximum(array, -reach), reach).astype(kind)


def setup_inputs(seed: int = 0) -> dict:
    key_of = jax.random.split(jax.random.key(seed), 33)
    return {
        "tokens": centred(key_of[0], (TOKENS, MODEL_WIDTH), 1.0, 6.0, ((0, 16),)),
        "layer_input": centred(key_of[1], (TOKENS, PLE), 1.0, 6.0, ((0, 16),)),
        "out_grad": centred(key_of[2], (TOKENS, MODEL_WIDTH), 1.0, 6.0, ((0, 16),)),
        "block_device": jax.vmap(lambda own: jax.random.permutation(own, N_CTX))(jax.random.split(key_of[3], GROUPS)).reshape((GROUPS, N_CTX)).astype(jnp.int32),
        "adapter_pick": draw_adapter_pick(jax.random.fold_in(key_of[32], 71), 0),
        "norm_gains": jnp.clip(1.0 + 0.15 * jax.random.normal(key_of[5], (6, MODEL_WIDTH), jnp.float32), 0.25, 1.75).astype(jnp.bfloat16),
        "head_norm_gains": jnp.clip(1.0 + 0.15 * jax.random.normal(key_of[6], (2, HEAD_SIZE), jnp.float32), 0.25, 1.75).astype(jnp.bfloat16),
        "query_weight": centred(key_of[7], (MODEL_WIDTH, QUERY_HEADS * HEAD_SIZE), MODEL_WIDTH ** -0.5, 0.125, ((0, 16), (1, 2))),
        "key_matrix": centred(key_of[8], (MODEL_WIDTH, KEY_VALUE_HEADS * HEAD_SIZE), MODEL_WIDTH ** -0.5, 0.125, ((0, 16), (1, 2))),
        "value_matrix": centred(key_of[9], (MODEL_WIDTH, KEY_VALUE_HEADS * HEAD_SIZE), MODEL_WIDTH ** -0.5, 0.125, ((0, 16), (1, 2))),
        "gate_weight": centred(key_of[10], (MODEL_WIDTH, FF), MODEL_WIDTH ** -0.5, 0.125, ((0, 16), (1, 2))),
        "up_weight": centred(key_of[11], (MODEL_WIDTH, FF), MODEL_WIDTH ** -0.5, 0.125, ((0, 16), (1, 2))),
        "out_weight": centred(key_of[12], (QUERY_HEADS * HEAD_SIZE, MODEL_WIDTH), (QUERY_HEADS * HEAD_SIZE) ** -0.5, 0.125, ((0, 2), (1, 16))),
        "down_weight": centred(key_of[13], (FF, MODEL_WIDTH), FF ** -0.5, 0.0625, ((0, 2), (1, 16))),
        "laurel_left": centred(key_of[14], (MODEL_WIDTH, LR), MODEL_WIDTH ** -0.5, 0.125),
        "laurel_right": centred(key_of[15], (LR, MODEL_WIDTH), LR ** -0.5, 0.75),
        "layer_gate": centred(key_of[16], (MODEL_WIDTH, PLE), MODEL_WIDTH ** -0.5, 0.125),
        "layer_lift": centred(key_of[17], (PLE, MODEL_WIDTH), PLE ** -0.5, 0.375),
        "query_shrink": centred(key_of[18], (ADAPTER_COUNT * ADAPTER_RANK, MODEL_WIDTH), MODEL_WIDTH ** -0.5, 0.125),
        "key_shrink": centred(key_of[19], (ADAPTER_COUNT * ADAPTER_RANK, MODEL_WIDTH), MODEL_WIDTH ** -0.5, 0.125),
        "value_shrink": centred(key_of[20], (ADAPTER_COUNT * ADAPTER_RANK, MODEL_WIDTH), MODEL_WIDTH ** -0.5, 0.125),
        "gate_shrink": centred(key_of[21], (ADAPTER_COUNT * ADAPTER_RANK, MODEL_WIDTH), MODEL_WIDTH ** -0.5, 0.125),
        "up_shrink": centred(key_of[22], (ADAPTER_COUNT * ADAPTER_RANK, MODEL_WIDTH), MODEL_WIDTH ** -0.5, 0.125),
        "out_shrink": centred(key_of[23], (ADAPTER_COUNT * ADAPTER_RANK, QUERY_HEADS * HEAD_SIZE), (QUERY_HEADS * HEAD_SIZE) ** -0.5, 0.125, ((1, 2),)),
        "down_shrink": centred(key_of[24], (ADAPTER_COUNT * ADAPTER_RANK, FF), FF ** -0.5, 0.0625, ((1, 2),)),
        "query_expand": centred(key_of[25], (ADAPTER_COUNT * ADAPTER_RANK, QUERY_HEADS * HEAD_SIZE), ADAPTER_RANK ** -0.5, 1.5, ((1, 2),)),
        "key_widen_maps": centred(key_of[26], (ADAPTER_COUNT * ADAPTER_RANK, KEY_VALUE_HEADS * HEAD_SIZE), ADAPTER_RANK ** -0.5, 1.5, ((1, 2),)),
        "value_widen_maps": centred(key_of[27], (ADAPTER_COUNT * ADAPTER_RANK, KEY_VALUE_HEADS * HEAD_SIZE), ADAPTER_RANK ** -0.5, 1.5, ((1, 2),)),
        "gate_expand": centred(key_of[28], (ADAPTER_COUNT * ADAPTER_RANK, FF), ADAPTER_RANK ** -0.5, 1.5, ((1, 2),)),
        "up_expand": centred(key_of[29], (ADAPTER_COUNT * ADAPTER_RANK, FF), ADAPTER_RANK ** -0.5, 1.5, ((1, 2),)),
        "out_expand": centred(key_of[30], (ADAPTER_COUNT * ADAPTER_RANK, MODEL_WIDTH), ADAPTER_RANK ** -0.5, 1.5),
        "down_expand": centred(key_of[31], (ADAPTER_COUNT * ADAPTER_RANK, MODEL_WIDTH), ADAPTER_RANK ** -0.5, 1.5),
    }


@jax.custom_vjp
def rank_reduced(v):
    return lax.optimization_barrier(v.astype(jnp.bfloat16)).astype(jnp.float32)

@jax.custom_vjp
def low_back(v):
    return v

def low_keep(v):
    return (rank_reduced(v), None)

def low_pass(kept, grad):
    return (grad,)

def back_keep(v):
    return (v, None)

def back_low(kept, grad):
    return (rank_reduced(grad),)
rank_reduced.defvjp(low_keep, low_pass)
low_back.defvjp(back_keep, back_low)
EPS = 1e-06
THETA = 1000000.0
FLOOR = -1e+30
ROOT_HALF = 0.5 ** 0.5
HIGHEST = lax.Precision.HIGHEST

def precise(left_side, right_side):
    return jnp.dot(left_side, right_side, precision=HIGHEST)

def normalized(inputs, norm_gain):
    return inputs * lax.rsqrt(lax.optimization_barrier(jnp.mean(inputs * inputs, axis=-1, keepdims=True)) + EPS) * norm_gain

def rotary_applied(inputs, rotary_angles):
    half_width = inputs.shape[-1] // 2
    cosine = jnp.cos(rotary_angles)[:, None, :]
    sine_term = jnp.sin(rotary_angles)[:, None, :]
    first_half = inputs[..., :half_width]
    second_half = inputs[..., half_width:]
    return jnp.concatenate([first_half * cosine - second_half * sine_term, second_half * cosine + first_half * sine_term], axis=-1)

def segment_of(positions):
    return jnp.where(positions < PROMPT, 0, 1 + (positions - PROMPT) // CONT).astype(jnp.int32)

def attention(queries, key_rows, value_rows):
    row_count_total = queries.shape[0]
    group_portion = QUERY_HEADS // KEY_VALUE_HEADS
    width = math.gcd(row_count_total, 512)
    key_places = jnp.arange(row_count_total, dtype=jnp.int32)
    key_segments = segment_of(key_places)
    keys_wide = jnp.repeat(key_rows, group_portion, axis=1)
    values_wide = jnp.repeat(value_rows, group_portion, axis=1)
    starts = jnp.arange(row_count_total // width, dtype=jnp.int32) * width

    def one_block(members):
        query_block, start_at = members
        query_places = start_at + jnp.arange(width, dtype=jnp.int32)
        visible = (key_places[None, :] <= query_places[:, None]) & ((key_segments[None, :] == 0) | (key_segments[None, :] == segment_of(query_places)[:, None]))
        scores = low_back(jnp.einsum('qhd,khd->hqk', query_block, keys_wide, precision=HIGHEST))
        scores = jnp.where(visible[None], scores, FLOOR)
        row_max = lax.optimization_barrier(jnp.max(scores, axis=-1, keepdims=True))
        exponent = jnp.exp(scores - row_max)
        chances = rank_reduced(exponent / lax.optimization_barrier(jnp.sum(exponent, axis=-1, keepdims=True)))
        return jnp.einsum('hqk,khd->qhd', chances, values_wide, precision=HIGHEST)
    blocks = queries.reshape(row_count_total // width, width, QUERY_HEADS, HEAD_SIZE)
    mixed = lax.map(jax.checkpoint(one_block), (blocks, starts))
    return mixed.reshape(row_count_total, QUERY_HEADS * HEAD_SIZE)

def group_layer(tokens_g, layer_g, pick_g, trained, frozen):
    query_shrink, key_shrink, value_shrink, gate_shrink, up_shrink, out_shrink, down_shrink, query_expand, key_widen_maps, value_widen_maps, gate_expand, up_expand, out_expand, down_expand = trained
    norm_gains, head_norm_gains, query_weight, key_matrix, value_matrix, gate_weight, up_weight, out_weight, down_weight, laurel_left, laurel_right, layer_gate, layer_lift = frozen
    row_count_total = tokens_g.shape[0]
    positions = jnp.arange(row_count_total, dtype=jnp.int32)
    segments = segment_of(positions)
    seq_pos = jnp.where(positions < PROMPT, positions, PROMPT + (positions - PROMPT) % CONT)
    picked = jnp.where(segments == 0, -1, pick_g[jnp.maximum(segments - 1, 0)]).astype(jnp.int32)
    select = (jnp.arange(ADAPTER_COUNT * ADAPTER_RANK, dtype=jnp.int32)[None, :] // ADAPTER_RANK == picked[:, None]).astype(jnp.float32)
    frequency = THETA ** (-2.0 * jnp.arange(HEAD_SIZE // 2, dtype=jnp.float32) / HEAD_SIZE)
    rotary_angles = seq_pos.astype(jnp.float32)[:, None] * frequency[None, :]

    def adapter(inputs, shrink, expand):
        return precise(select * precise(inputs, shrink.T), expand)
    first_norm = normalized(tokens_g, norm_gains[0])
    first_low = rank_reduced(first_norm)
    query_proj = low_back(precise(first_low, query_weight) + adapter(first_low, query_shrink, query_expand))
    key_projected = low_back(precise(first_low, key_matrix) + adapter(first_low, key_shrink, key_widen_maps))
    value_projected = low_back(precise(first_low, value_matrix) + adapter(first_low, value_shrink, value_widen_maps))
    queries = rank_reduced(rotary_applied(normalized(query_proj.reshape(row_count_total, QUERY_HEADS, HEAD_SIZE), head_norm_gains[0]), rotary_angles) * HEAD_SIZE ** (-0.5))
    key_rows = rank_reduced(rotary_applied(normalized(key_projected.reshape(row_count_total, KEY_VALUE_HEADS, HEAD_SIZE), head_norm_gains[1]), rotary_angles))
    value_rows = rank_reduced(normalized(value_projected.reshape(row_count_total, KEY_VALUE_HEADS, HEAD_SIZE), 1.0))
    heads = rank_reduced(low_back(attention(queries, key_rows, value_rows)))
    attn_total = low_back(precise(heads, out_weight) + adapter(heads, out_shrink, out_expand))
    laurel_rank = rank_reduced(low_back(precise(first_low, laurel_left)))
    laurel_back = low_back(precise(laurel_rank, laurel_right))
    mid_stream = (tokens_g + normalized(attn_total, norm_gains[1]) + first_norm + normalized(laurel_back, norm_gains[2])) * ROOT_HALF
    second_low = rank_reduced(normalized(mid_stream, norm_gains[3]))
    gate_proj = low_back(precise(second_low, gate_weight) + adapter(second_low, gate_shrink, gate_expand))
    up_proj = low_back(precise(second_low, up_weight) + adapter(second_low, up_shrink, up_expand))
    hidden_low = rank_reduced(jax.nn.gelu(gate_proj, approximate=True) * up_proj)
    ffn_total = low_back(precise(hidden_low, down_weight) + adapter(hidden_low, down_shrink, down_expand))
    after_ffn = mid_stream + normalized(ffn_total, norm_gains[4])
    layer_pre = low_back(precise(rank_reduced(after_ffn), layer_gate))
    gated_low = rank_reduced(jax.nn.gelu(layer_pre, approximate=True) * layer_g)
    layer_back = low_back(precise(gated_low, layer_lift))
    return after_ffn + normalized(layer_back, norm_gains[5])

def reference(tokens, layer_input, out_grad, block_device, adapter_pick, norm_gains, head_norm_gains, query_weight, key_matrix, value_matrix, gate_weight, up_weight, out_weight, down_weight, laurel_left, laurel_right, layer_gate, layer_lift, query_shrink, key_shrink, value_shrink, gate_shrink, up_shrink, out_shrink, down_shrink, query_expand, key_widen_maps, value_widen_maps, gate_expand, up_expand, out_expand, down_expand):
    frozen = tuple((member.astype(jnp.float32) for member in (norm_gains, head_norm_gains, query_weight, key_matrix, value_matrix, gate_weight, up_weight, out_weight, down_weight, laurel_left, laurel_right, layer_gate, layer_lift)))
    trained = tuple((member.astype(jnp.float32) for member in (query_shrink, key_shrink, value_shrink, gate_shrink, up_shrink, out_shrink, down_shrink, query_expand, key_widen_maps, value_widen_maps, gate_expand, up_expand, out_expand, down_expand)))
    group_ids = jnp.arange(GROUPS, dtype=jnp.int32)
    natural_order = (block_device[:, :, None] * TOK_DEV + group_ids[:, None, None] * BLOCK + jnp.arange(BLOCK, dtype=jnp.int32)[None, None, :]).reshape(GROUPS, GTOK).astype(jnp.int32)

    def whole_batch(tokens_all, layer_all, trained_all):

        def one_group(carry, members):
            tokens_g, layer_g, pick_g = members
            return (carry, group_layer(tokens_g, layer_g, pick_g, trained_all, frozen))
        start_carry = jnp.zeros((), jnp.float32)
        ignored, outputs = lax.scan(jax.checkpoint(one_group), start_carry, (tokens_all[natural_order], layer_all[natural_order], adapter_pick))
        placed = jnp.zeros((TOKENS, MODEL_WIDTH), jnp.float32)
        return placed.at[natural_order.reshape(-1)].set(outputs.reshape(GROUPS * GTOK, MODEL_WIDTH))
    result, pull = jax.vjp(whole_batch, tokens.astype(jnp.float32), layer_input.astype(jnp.float32), trained)
    grad_tokens, grad_layer, grad_trained = pull(out_grad.astype(jnp.float32))
    return (result.astype(jnp.bfloat16), grad_tokens, grad_layer, grad_trained[0], grad_trained[1], grad_trained[2], grad_trained[3], grad_trained[4], grad_trained[5], grad_trained[6], grad_trained[7], grad_trained[8], grad_trained[9], grad_trained[10], grad_trained[11], grad_trained[12], grad_trained[13])
```

```python
import jax
import jax.numpy as jnp
from jax import lax
from jax.experimental import pallas as pl
from jax.experimental.pallas import tpu as pltpu
from jax.sharding import PartitionSpec as P

QUERY_HEADS = 8
KEY_VALUE_HEADS = 2
ADAPTER_COUNT = 8
ADAPTER_RANK = 16
PROMPT = 2048
CONT = 256

EPS = 1e-06
THETA = 1000000.0
ROOT_HALF = 0.5**0.5
F32 = jnp.float32
BF16 = jnp.bfloat16
SWAP = [(0, 1), (1, 0)]


def normalized(inputs, norm_gain):
    return inputs * lax.rsqrt(jnp.mean(inputs * inputs, axis=-1, keepdims=True) + EPS) * norm_gain


def norm_pull(inputs, norm_gain, upstream):
    return jax.vjp(lambda inner: normalized(inner, norm_gain), inputs)[1](upstream)[0]


def rotary_applied(inputs, cosine, sine_term):
    half_width = inputs.shape[-1] // 2
    first_half = inputs[..., :half_width]
    second_half = inputs[..., half_width:]
    return jnp.concatenate(
        [
            first_half * cosine - second_half * sine_term,
            second_half * cosine + first_half * sine_term,
        ],
        axis=-1,
    )


def glu_form(gate_in, up_in):
    return jax.nn.gelu(gate_in, approximate=True) * up_in


def product(left_side, right_side):
    return jnp.dot(left_side, right_side, preferred_element_type=F32)


def against(left_side, right_side):
    return lax.dot_general(
        left_side, right_side, (((1,), (1,)), ((), ())), preferred_element_type=F32
    )


def summed(left_side, right_side):
    return lax.dot_general(
        left_side, right_side, (((0,), (0,)), ((), ())), preferred_element_type=F32
    )


def low(value):
    return value.astype(BF16)


def attend_kernel(count_ref, kslot_ref, vslot_ref, q_ref, k_ref, v_ref, o_ref, lse_ref, acc, tot, *, heads, dim):
    group = pl.program_id(0)
    count = count_ref[group]
    rows = q_ref.shape[0]
    fold = tot.shape[-1]
    acc[...] = jnp.zeros_like(acc)
    tot[...] = jnp.zeros_like(tot)

    def step(index, masked):
        keys = k_ref[kslot_ref[group, index], 0]
        values = v_ref[vslot_ref[group, index], 0]
        for head in range(heads):
            lanes = slice(head * dim, (head + 1) * dim)
            scores = against(q_ref[:, lanes], keys)
            weights = jnp.exp(scores)
            if masked:
                row = lax.broadcasted_iota(jnp.int32, scores.shape, 0)
                col = lax.broadcasted_iota(jnp.int32, scores.shape, 1)
                weights = jnp.where(col <= row, weights, 0.0)
            part = weights[:, :fold]
            for start in range(fold, rows, fold):
                part = part + weights[:, start : start + fold]
            tot[head] += part
            acc[:, lanes] += product(low(weights), values)

    def body(index, carry):
        step(index, False)
        return carry

    lax.fori_loop(0, count - 1, body, 0)
    step(count - 1, True)
    lane = lax.broadcasted_iota(jnp.int32, lse_ref.shape, 1)
    lse = jnp.zeros(lse_ref.shape, F32)
    for head in range(heads):
        lanes = slice(head * dim, (head + 1) * dim)
        total = jnp.sum(tot[head], axis=-1, keepdims=True)
        o_ref[:, lanes] = low(acc[:, lanes] / total)
        lse = jnp.where(lane == head, jnp.log(total), lse)
    lse_ref[...] = lse


def attend_back_kernel(
    count_ref, kslot_ref, vslot_ref, dslot_ref, q_ref, k_ref, v_ref, o_ref, lse_ref, g_ref, dq_ref, dkv_ref, delta, *, heads, dim
):
    group = pl.program_id(0)
    count = count_ref[group]
    dq_ref[...] = jnp.zeros_like(dq_ref)
    dkv_ref[...] = jnp.zeros_like(dkv_ref)
    for head in range(heads):
        lanes = slice(head * dim, (head + 1) * dim)
        delta[head] = jnp.sum(
            o_ref[:, lanes].astype(F32) * g_ref[:, lanes].astype(F32), axis=-1, keepdims=True
        )

    def step(index, masked):
        keys = k_ref[kslot_ref[group, index], 0]
        values = v_ref[vslot_ref[group, index], 0]
        slot = dslot_ref[group, index]
        dk = jnp.zeros(keys.shape, F32)
        dv = jnp.zeros(values.shape, F32)
        for head in range(heads):
            lanes = slice(head * dim, (head + 1) * dim)
            queries = q_ref[:, lanes]
            upstream = g_ref[:, lanes]
            scores = against(queries, keys)
            weights = jnp.exp(scores - lse_ref[:, head : head + 1])
            if masked:
                row = lax.broadcasted_iota(jnp.int32, scores.shape, 0)
                col = lax.broadcasted_iota(jnp.int32, scores.shape, 1)
                weights = jnp.where(col <= row, weights, 0.0)
            grad_weights = against(upstream, values)
            grad_scores = low(weights * (grad_weights - delta[head]))
            dq_ref[:, lanes] += product(grad_scores, keys)
            dk += summed(grad_scores, queries)
            dv += summed(low(weights), upstream)
        dkv_ref[slot, 0, :, :dim] = low(dk)
        dkv_ref[slot, 0, :, dim:] = low(dv)

    def body(index, carry):
        step(index, False)
        return carry

    lax.fori_loop(0, count - 1, body, 0)
    step(count - 1, True)


def attend(tables, queries, key_all, value_all, groups, heads, dim):
    count, kslot, vslot = tables
    slots, _, block, _ = key_all.shape
    rows = queries.shape[0]
    fold = min(128, block)
    whole = pl.BlockSpec((slots, 1, block, dim), lambda g, *_: (0, g, 0, 0))
    mine = pl.BlockSpec((block, heads * dim), lambda g, *_: (g, 0))
    return pl.pallas_call(
        lambda *refs: attend_kernel(*refs, heads=heads, dim=dim),
        grid_spec=pltpu.PrefetchScalarGridSpec(
            num_scalar_prefetch=3,
            grid=(groups,),
            in_specs=[mine, whole, whole],
            out_specs=[mine, pl.BlockSpec((block, 128), lambda g, *_: (g, 0))],
            scratch_shapes=[
                pltpu.VMEM((block, heads * dim), F32),
                pltpu.VMEM((heads, block, fold), F32),
            ],
        ),
        out_shape=[
            jax.ShapeDtypeStruct((rows, heads * dim), BF16),
            jax.ShapeDtypeStruct((rows, 128), F32),
        ],
        compiler_params=pltpu.CompilerParams(vmem_limit_bytes=40 * 2**20),
        cost_estimate=pl.CostEstimate(
            flops=4 * rows * heads * dim * 2304, bytes_accessed=6 * 2**20, transcendentals=rows * heads * 2304
        ),
    )(count, kslot, vslot, queries, key_all, value_all)


def attend_back(tables, dslot, queries, key_all, value_all, heads_low, lse, grads, groups, heads, dim):
    count, kslot, vslot = tables
    slots, _, block, _ = key_all.shape
    rows = queries.shape[0]
    whole = pl.BlockSpec((slots, 1, block, dim), lambda g, *_: (0, g, 0, 0))
    mine = pl.BlockSpec((block, heads * dim), lambda g, *_: (g, 0))
    return pl.pallas_call(
        lambda *refs: attend_back_kernel(*refs, heads=heads, dim=dim),
        grid_spec=pltpu.PrefetchScalarGridSpec(
            num_scalar_prefetch=4,
            grid=(groups,),
            in_specs=[mine, whole, whole, mine, pl.BlockSpec((block, 128), lambda g, *_: (g, 0)), mine],
            out_specs=[mine, pl.BlockSpec((slots, 1, block, 2 * dim), lambda g, *_: (0, g, 0, 0))],
            scratch_shapes=[pltpu.VMEM((heads, block, 1), F32)],
        ),
        out_shape=[
            jax.ShapeDtypeStruct((rows, heads * dim), F32),
            jax.ShapeDtypeStruct((slots, groups, block, 2 * dim), BF16),
        ],
        compiler_params=pltpu.CompilerParams(vmem_limit_bytes=48 * 2**20),
        cost_estimate=pl.CostEstimate(
            flops=10 * rows * heads * dim * 2304, bytes_accessed=12 * 2**20, transcendentals=rows * heads * 2304
        ),
    )(count, kslot, vslot, dslot, queries, key_all, value_all, heads_low, lse, grads)


def local(
    tokens,
    layer_input,
    out_grad,
    block_device,
    adapter_pick,
    norm_gains,
    head_norm_gains,
    query_weight,
    key_matrix,
    value_matrix,
    gate_weight,
    up_weight,
    out_weight,
    down_weight,
    laurel_left,
    laurel_right,
    layer_gate,
    layer_lift,
    query_shrink,
    key_shrink,
    value_shrink,
    gate_shrink,
    up_shrink,
    out_shrink,
    down_shrink,
    query_expand,
    key_widen_maps,
    value_widen_maps,
    gate_expand,
    up_expand,
    out_expand,
    down_expand,
):
    count_ctx = lax.axis_size("ctx")
    bit_count = count_ctx.bit_length() - 1
    groups = block_device.shape[0]
    local_rows, width = tokens.shape
    block_len = local_rows // groups
    half_rows = local_rows // 2
    head_dim = head_norm_gains.shape[1]
    heads_local = query_weight.shape[1] // head_dim
    adapter_width = ADAPTER_COUNT * ADAPTER_RANK
    model_block = width // count_ctx
    hidden_slice = gate_weight.shape[1] // 4
    me = lax.axis_index("ctx")
    core = lax.axis_index("wt")

    team_groups = [
        [base + 2 * t for t in range(4)] for base in range(count_ctx) if (base >> 1) & 3 == 0
    ]
    plane_groups = [[base + t for t in range(4)] for base in range(0, count_ctx, 4)]
    column_groups = [[base + 4 * t for t in range(count_ctx // 4)] for base in range(4)]
    spread_bits = list(range(3, bit_count)) + [0]
    team_base = me - 2 * ((me >> 1) & 3)
    team_place = (me >> 1) & 3

    def flip(value, bit):
        return lax.ppermute(value, "ctx", [(i, i ^ (1 << bit)) for i in range(count_ctx)])

    def other_core(value):
        return lax.ppermute(value, "wt", SWAP)

    def own_half(value):
        return lax.dynamic_slice_in_dim(value, core * half_rows, half_rows, 0)

    def other_half(value):
        return lax.dynamic_slice_in_dim(value, (1 - core) * half_rows, half_rows, 0)

    def both_halves(own, other):
        return jnp.where(
            core == 0, jnp.concatenate([own, other], axis=0), jnp.concatenate([other, own], axis=0)
        )

    def column_blocks(value, places):
        return jnp.concatenate(
            [
                lax.dynamic_slice_in_dim(value, place * model_block, model_block, 1)
                for place in places
            ],
            axis=1,
        )

    def stage_mask(position, stages):
        return sum(((position >> i) & 1) << bit for i, bit in enumerate(stages))

    def stage_position(owner, stages):
        return sum((((owner ^ me) >> bit) & 1) << i for i, bit in enumerate(stages))

    def all_stages(first, last):
        return list(range(2, bit_count)) + [first, last]

    weight_stages = all_stages(0, 1)
    weight_order = [me ^ stage_mask(j, weight_stages) for j in range(count_ctx)]
    weight_back = [stage_position(b, weight_stages) for b in range(count_ctx)]
    piece_masks = [0]
    for bit in spread_bits:
        piece_masks = piece_masks + [mask | (1 << bit) for mask in piece_masks]
    team_order = [(team_base ^ mask) + 2 * t for mask in piece_masks for t in range(4)]
    team_back = [
        4 * sum((((b ^ me) >> bit) & 1) << i for i, bit in enumerate(spread_bits)) + ((b >> 1) & 3)
        for b in range(count_ctx)
    ]

    def gather_slabs(shard, stages):
        slab = shard
        for bit in stages[:-1]:
            slab = jnp.concatenate([slab, flip(slab, bit)], axis=0)
        return slab, flip(slab, stages[-1])

    def team_pieces(shard):
        split = shard.reshape(model_block, 4, hidden_slice).transpose(1, 0, 2)
        piece = lax.all_to_all(split, "ctx", 0, 0, axis_index_groups=team_groups, tiled=True)
        pieces = [piece.reshape(4 * model_block, hidden_slice)]
        for bit in spread_bits:
            pieces = pieces + [flip(piece, bit) for piece in pieces]
        return pieces

    prompt_blocks = PROMPT // block_len
    cont_blocks = CONT // block_len
    device_ids = jnp.arange(count_ctx, dtype=jnp.int32)
    block_of = jnp.sum(
        jnp.where(block_device[None] == device_ids[:, None, None], device_ids[None, None, :], 0),
        axis=2,
    )
    cont_of = (block_of - prompt_blocks) // cont_blocks
    pick_of = jnp.sum(
        jnp.where(
            cont_of[:, :, None] == jnp.arange(adapter_pick.shape[1], dtype=jnp.int32),
            adapter_pick[None],
            0,
        ),
        axis=2,
    )
    pick_of = jnp.where(block_of < prompt_blocks, -1, pick_of)

    def picks_at(device):
        return jnp.sum(jnp.where(device_ids[:, None] == device, pick_of, 0), axis=0)

    def select_rows(picks):
        rows = jnp.repeat(picks, block_len)
        return (
            jnp.arange(adapter_width, dtype=jnp.int32)[None, :] // ADAPTER_RANK == rows[:, None]
        ).astype(F32)

    select = select_rows(picks_at(me))
    select_own = own_half(select)
    team_select = [select_rows(picks_at(team_base + 2 * t)) for t in range(4)]
    select_near = jnp.concatenate([own_half(part) for part in team_select], axis=0)
    select_far = jnp.concatenate([other_half(part) for part in team_select], axis=0)

    my_block = jnp.sum(jnp.where(device_ids[:, None] == me, block_of, 0), axis=0)
    positions = (
        my_block[:, None] * block_len + jnp.arange(block_len, dtype=jnp.int32)[None, :]
    ).reshape(-1)
    seq_pos = jnp.where(positions < PROMPT, positions, PROMPT + (positions - PROMPT) % CONT)
    frequency = THETA ** (-2.0 * jnp.arange(head_dim // 2, dtype=F32) / head_dim)
    rotary_angles = seq_pos.astype(F32)[:, None] * frequency[None, :]
    cosine = jnp.cos(rotary_angles)[:, None, :]
    sine_term = jnp.sin(rotary_angles)[:, None, :]
    cont_start = prompt_blocks + (my_block - prompt_blocks) // cont_blocks * cont_blocks
    is_prompt = my_block < prompt_blocks
    visible_count = jnp.where(
        is_prompt, my_block + 1, prompt_blocks + my_block - cont_start + 1
    ).astype(jnp.int32)
    entries = jnp.arange(prompt_blocks + cont_blocks, dtype=jnp.int32)
    visible_block = jnp.where(
        is_prompt[:, None] | (entries < prompt_blocks)[None, :],
        entries[None, :],
        cont_start[:, None] + entries[None, :] - prompt_blocks,
    )
    visible_device = jnp.sum(
        jnp.where(
            visible_block[:, :, None] == device_ids[None, None, :], block_device[:, None, :], 0
        ),
        axis=2,
    )
    key_stages, value_stages = all_stages(0, 1), all_stages(1, 0)
    key_slot = stage_position(visible_device, key_stages).astype(jnp.int32)
    value_slot = stage_position(visible_device, value_stages).astype(jnp.int32)
    grad_slot = (
        (visible_device % 4) * (count_ctx // 4) + visible_device // 4
    ).astype(jnp.int32)
    tables = (visible_count, key_slot, value_slot)

    gains = norm_gains.astype(F32)
    query_gain = head_norm_gains[0].astype(F32)
    key_gain = head_norm_gains[1].astype(F32)

    def query_piece(projected):
        return (
            rotary_applied(
                normalized(projected.reshape(local_rows, -1, head_dim), query_gain),
                cosine,
                sine_term,
            )
            * head_dim ** (-0.5)
        ).reshape(local_rows, -1)

    def key_piece(projected):
        return rotary_applied(
            normalized(projected.reshape(local_rows, -1, head_dim), key_gain), cosine, sine_term
        ).reshape(local_rows, -1)

    def value_piece(projected):
        return normalized(projected.reshape(local_rows, -1, head_dim), 1.0).reshape(local_rows, -1)

    kv_slabs = gather_slabs(jnp.concatenate([key_matrix, value_matrix], axis=1), weight_stages)
    query_slabs = gather_slabs(query_weight, weight_stages)
    out_slabs = gather_slabs(out_weight.T, weight_stages)
    gate_pieces = team_pieces(gate_weight)
    up_pieces = team_pieces(up_weight)
    down_pieces = team_pieces(down_weight.T)

    def slab_product(value, slabs):
        middle = value.shape[1] // 2
        return product(value[:, :middle], slabs[0]) + product(value[:, middle:], slabs[1])

    def slab_against(value, slabs):
        return jnp.concatenate([against(value, slabs[0]), against(value, slabs[1])], axis=1)

    def piece_product(value, pieces):
        rows = pieces[0].shape[0]
        total = product(value[:, :rows], pieces[0])
        for i in range(1, len(pieces)):
            total = total + product(value[:, i * rows : (i + 1) * rows], pieces[i])
        return total

    first_norm = normalized(tokens.astype(F32), gains[0])
    first_low = low(first_norm)
    first_moved = column_blocks(first_low, weight_order)
    rank_query = low(select * against(first_low, query_shrink))
    rank_key = low(select * against(first_low, key_shrink))
    rank_value = low(select * against(first_low, value_shrink))
    kv_projected = slab_product(first_moved, kv_slabs)
    kv_width = key_matrix.shape[1]
    key_projected = kv_projected[:, :kv_width] + product(rank_key, key_widen_maps)
    value_projected = kv_projected[:, kv_width:] + product(rank_value, value_widen_maps)
    key_low = low(key_piece(key_projected))
    value_low = low(value_piece(value_projected))

    def gather_blocks(value, stages):
        slabs = gather_slabs(value.reshape(1, groups, block_len, head_dim), stages)
        return jnp.concatenate(slabs, axis=0)

    key_all = gather_blocks(key_low, key_stages)
    value_all = gather_blocks(value_low, value_stages)
    query_proj = slab_product(first_moved, query_slabs) + product(rank_query, query_expand)
    query_low = low(query_piece(query_proj))
    heads_low, lse = attend(tables, query_low, key_all, value_all, groups, heads_local, head_dim)

    def core_sum(value):
        return own_half(value) + other_core(other_half(value))

    attn_part = jnp.concatenate(
        [slab_against(heads_low, out_slabs), select * against(heads_low, out_shrink)], axis=1
    )
    attn_sum = core_sum(attn_part)
    rank_out = low(attn_sum[:, width:])
    attn_total = column_blocks(attn_sum[:, :width], weight_back) + product(rank_out, out_expand)

    tokens_own = own_half(tokens).astype(F32)
    first_own = normalized(tokens_own, gains[0])
    first_own_low = low(first_own)
    laurel_rank = low(product(first_own_low, laurel_left))
    laurel_back = product(laurel_rank, laurel_right)
    mid_stream = (
        tokens_own + normalized(attn_total, gains[1]) + first_own + normalized(laurel_back, gains[2])
    ) * ROOT_HALF
    second_low = low(normalized(mid_stream, gains[3]))

    def team_gather(value):
        sent = jnp.broadcast_to(value[None], (4,) + value.shape)
        near = lax.all_to_all(sent, "ctx", 0, 0, axis_index_groups=team_groups, tiled=True)
        near = near.reshape(4 * value.shape[0], value.shape[1])
        return near, other_core(near)

    def team_sum(near, far):
        total = low(near + other_core(low(far)).astype(F32))
        total = total.reshape(4, half_rows, total.shape[1])
        parts = lax.all_to_all(total, "ctx", 0, 0, axis_index_groups=team_groups, tiled=True)
        return jnp.sum(parts.astype(F32), axis=0)

    def hidden_columns(value):
        return lax.dynamic_slice_in_dim(value, team_place * hidden_slice, hidden_slice, 1)

    shrink_moved = column_blocks(jnp.concatenate([gate_shrink, up_shrink], axis=0), team_order)
    down_expand_moved = column_blocks(down_expand, team_order)
    gate_expand_slice = hidden_columns(gate_expand)
    up_expand_slice = hidden_columns(up_expand)
    down_shrink_slice = hidden_columns(down_shrink)

    def feed(second_part, select_part):
        ranks = against(second_part, shrink_moved)
        rank_gate = low(select_part * ranks[:, :adapter_width])
        rank_up = low(select_part * ranks[:, adapter_width:])
        gate_proj = piece_product(second_part, gate_pieces) + product(rank_gate, gate_expand_slice)
        up_proj = piece_product(second_part, up_pieces) + product(rank_up, up_expand_slice)
        hidden = low(glu_form(gate_proj, up_proj))
        part = jnp.concatenate(
            [against(hidden, piece) for piece in down_pieces]
            + [select_part * against(hidden, down_shrink_slice)],
            axis=1,
        )
        return rank_gate, rank_up, gate_proj, up_proj, hidden, part

    second_near, second_far = team_gather(column_blocks(second_low, team_order))
    kept_far = feed(second_far, select_far)
    kept_near = feed(second_near, select_near)
    ffn_sum = team_sum(kept_near[-1], kept_far[-1])
    rank_down = low(ffn_sum[:, width:])
    ffn_total = column_blocks(ffn_sum[:, :width], team_back) + product(rank_down, down_expand)
    after_ffn = mid_stream + normalized(ffn_total, gains[4])

    layer_pre = product(low(after_ffn), layer_gate)
    layer_wide = own_half(layer_input).astype(F32)
    gated_low = low(glu_form(layer_pre, layer_wide))
    layer_back = product(gated_low, layer_lift)
    result_own = low(after_ffn + normalized(layer_back, gains[5]))
    upstream = own_half(out_grad).astype(F32)
    grad_layer_back = low(norm_pull(layer_back, gains[5], upstream))
    grad_gated = against(grad_layer_back, layer_lift)
    grad_pre, layer_input_own = jax.vjp(glu_form, layer_pre, layer_wide)[1](grad_gated)
    grad_after = upstream + against(low(grad_pre), layer_gate)
    grad_ffn = low(norm_pull(ffn_total, gains[4], grad_after))
    down_expand_grad = summed(rank_down, grad_ffn)

    def feed_back(grad_part, select_part, kept):
        rank_gate, rank_up, gate_proj, up_proj, hidden, _ = kept
        grad_rank_down = low(select_part * against(grad_part, down_expand_moved))
        grad_hidden = piece_product(grad_part, down_pieces) + product(
            grad_rank_down, down_shrink_slice
        )
        grad_gate, grad_up = jax.vjp(glu_form, gate_proj, up_proj)[1](grad_hidden)
        grad_gate, grad_up = low(grad_gate), low(grad_up)
        part = jnp.concatenate(
            [
                against(grad_gate, gate_piece) + against(grad_up, up_piece)
                for gate_piece, up_piece in zip(gate_pieces, up_pieces)
            ]
            + [
                select_part * against(grad_gate, gate_expand_slice),
                select_part * against(grad_up, up_expand_slice),
            ],
            axis=1,
        )
        return (
            part,
            summed(rank_gate, grad_gate),
            summed(rank_up, grad_up),
            summed(grad_rank_down, hidden),
        )

    grad_near, grad_far = team_gather(column_blocks(grad_ffn, team_order))
    back_far = feed_back(grad_far, select_far, kept_far)
    back_near = feed_back(grad_near, select_near, kept_near)
    gate_expand_grad, up_expand_grad, down_shrink_grad = (
        near + far for near, far in zip(back_near[1:], back_far[1:])
    )
    second_sum = team_sum(back_near[0], back_far[0])
    grad_rank_gate = low(second_sum[:, width : width + adapter_width])
    grad_rank_up = low(second_sum[:, width + adapter_width :])
    grad_second = (
        column_blocks(second_sum[:, :width], team_back)
        + product(grad_rank_gate, gate_shrink)
        + product(grad_rank_up, up_shrink)
    )
    gate_shrink_grad = summed(grad_rank_gate, second_low)
    up_shrink_grad = summed(grad_rank_up, second_low)

    grad_mid = grad_after + norm_pull(mid_stream, gains[3], grad_second)
    grad_scaled = grad_mid * ROOT_HALF
    grad_attn_own = low(norm_pull(attn_total, gains[1], grad_scaled))
    grad_laurel_back = low(norm_pull(laurel_back, gains[2], grad_scaled))
    grad_laurel_rank = low(against(grad_laurel_back, laurel_right))
    grad_first = grad_scaled + against(grad_laurel_rank, laurel_left)
    out_expand_grad = summed(rank_out, grad_attn_own)
    grad_rank_out_own = low(select_own * against(grad_attn_own, out_expand))
    grad_sent = jnp.concatenate(
        [column_blocks(grad_attn_own, weight_order), grad_rank_out_own], axis=1
    )
    grad_joined = both_halves(grad_sent, other_core(grad_sent))
    grad_attn = grad_joined[:, :width]
    grad_rank_out = grad_joined[:, width:]
    out_shrink_grad = summed(grad_rank_out, heads_low)
    grad_heads = low(slab_product(grad_attn, out_slabs) + product(grad_rank_out, out_shrink))

    grad_queries, grad_kv = attend_back(
        tables,
        grad_slot,
        query_low,
        key_all,
        value_all,
        heads_low,
        lse,
        grad_heads,
        groups,
        heads_local,
        head_dim,
    )
    grad_kv = grad_kv.reshape(4, -1, head_dim * 2)
    parts = lax.all_to_all(grad_kv, "ctx", 0, 0, axis_index_groups=plane_groups, tiled=True)
    parts = low(jnp.sum(parts.astype(F32), axis=0)).reshape(count_ctx // 4, local_rows, 2 * head_dim)
    parts = lax.all_to_all(parts, "ctx", 0, 0, axis_index_groups=column_groups, tiled=True)
    grad_kv_own = jnp.sum(parts.astype(F32), axis=0)

    grad_query_proj = low(jax.vjp(query_piece, query_proj)[1](grad_queries)[0])
    grad_key_proj = low(jax.vjp(key_piece, key_projected)[1](grad_kv_own[:, :head_dim])[0])
    grad_value_proj = low(jax.vjp(value_piece, value_projected)[1](grad_kv_own[:, head_dim:])[0])
    query_expand_grad = summed(rank_query, grad_query_proj)
    key_expand_grad = summed(rank_key, grad_key_proj)
    value_expand_grad = summed(rank_value, grad_value_proj)
    grad_kv_proj = jnp.concatenate([grad_key_proj, grad_value_proj], axis=1)
    first_part = jnp.concatenate(
        [
            slab_against(grad_query_proj, query_slabs) + slab_against(grad_kv_proj, kv_slabs),
            select * against(grad_query_proj, query_expand),
            select * against(grad_key_proj, key_widen_maps),
            select * against(grad_value_proj, value_widen_maps),
        ],
        axis=1,
    )
    first_sum = own_half(first_part) + other_core(low(other_half(first_part))).astype(F32)
    grad_rank_query, grad_rank_key, grad_rank_value = (
        low(first_sum[:, width + i * adapter_width : width + (i + 1) * adapter_width])
        for i in range(3)
    )
    grad_first = (
        grad_first
        + column_blocks(first_sum[:, :width], weight_back)
        + product(grad_rank_query, query_shrink)
        + product(grad_rank_key, key_shrink)
        + product(grad_rank_value, value_shrink)
    )
    query_shrink_grad = summed(grad_rank_query, first_own_low)
    key_shrink_grad = summed(grad_rank_key, first_own_low)
    value_shrink_grad = summed(grad_rank_value, first_own_low)
    input_own = grad_scaled + norm_pull(tokens_own, gains[0], grad_first)

    def scatter_split(grads):
        rows = adapter_width // count_ctx
        joined = low(jnp.concatenate(grads, axis=1))
        parts = joined.reshape(count_ctx, rows, joined.shape[1])
        parts = lax.all_to_all(parts, "ctx", 0, 0, tiled=True)
        total = jnp.sum(parts.astype(F32), axis=0)
        cuts, start = [], 0
        for grad in grads:
            cuts.append(total[:, start : start + grad.shape[1]])
            start += grad.shape[1]
        return cuts

    def scatter_team(grads):
        rows = adapter_width // count_ctx
        joined = low(jnp.stack(grads, axis=0)).reshape(len(grads), count_ctx, rows, hidden_slice)
        parts = joined.transpose(1, 0, 2, 3).reshape(count_ctx, len(grads) * rows, hidden_slice)
        parts = lax.all_to_all(parts, "ctx", 0, 0, tiled=True)
        teams = [
            sum(parts[i].astype(F32) for i in range(count_ctx) if (i >> 1) & 3 == t)
            for t in range(4)
        ]
        total = jnp.concatenate(teams, axis=1)
        return [total[i * rows : (i + 1) * rows] for i in range(len(grads))]

    def scatter_shared(grads):
        rows = adapter_width // (2 * count_ctx)
        shaped = jnp.stack(grads, axis=0).reshape(len(grads), count_ctx, 2, rows, width)
        keep = lax.dynamic_index_in_dim(shaped, core, 2, keepdims=False)
        send = lax.dynamic_index_in_dim(shaped, 1 - core, 2, keepdims=False)
        joined = low(keep + other_core(low(send)).astype(F32))
        parts = joined.transpose(1, 0, 2, 3).reshape(count_ctx, len(grads) * rows, width)
        parts = lax.all_to_all(parts, "ctx", 0, 0, tiled=True)
        total = jnp.sum(parts.astype(F32), axis=0)
        return [total[i * rows : (i + 1) * rows] for i in range(len(grads))]

    gate_expand_out, up_expand_out, down_shrink_out = scatter_team(
        [gate_expand_grad, up_expand_grad, down_shrink_grad]
    )
    (out_shrink_out,) = scatter_split([out_shrink_grad])
    gate_shrink_out, up_shrink_out, down_expand_out, out_expand_out = scatter_shared(
        [gate_shrink_grad, up_shrink_grad, down_expand_grad, out_expand_grad]
    )
    query_expand_out, key_expand_out, value_expand_out = scatter_split(
        [query_expand_grad, key_expand_grad, value_expand_grad]
    )
    query_shrink_out, key_shrink_out, value_shrink_out = scatter_shared(
        [query_shrink_grad, key_shrink_grad, value_shrink_grad]
    )

    return (
        both_halves(result_own, other_core(result_own)),
        both_halves(input_own, other_core(input_own)),
        both_halves(layer_input_own, other_core(layer_input_own)),
        query_shrink_out,
        key_shrink_out,
        value_shrink_out,
        gate_shrink_out,
        up_shrink_out,
        out_shrink_out,
        down_shrink_out,
        query_expand_out,
        key_expand_out,
        value_expand_out,
        gate_expand_out,
        up_expand_out,
        out_expand_out,
        down_expand_out,
    )


def solution(mesh):
    in_specs = (
        P("ctx", None),
        P("ctx", None),
        P("ctx", None),
        P(),
        P(),
        P(),
        P(),
        P("ctx", "wt"),
        P("ctx", "wt"),
        P("ctx", "wt"),
        P("ctx", "wt"),
        P("ctx", "wt"),
        P("wt", "ctx"),
        P("wt", "ctx"),
        P(),
        P(),
        P(),
        P(),
        P(),
        P(),
        P(),
        P(),
        P(),
        P(None, "wt"),
        P(None, "wt"),
        P(None, "wt"),
        P(None, "wt"),
        P(None, "wt"),
        P(None, "wt"),
        P(None, "wt"),
        P(),
        P(),
    )
    out_specs = (
        P("ctx", None),
        P("ctx", None),
        P("ctx", None),
        P(("ctx", "wt"), None),
        P(("ctx", "wt"), None),
        P(("ctx", "wt"), None),
        P(("ctx", "wt"), None),
        P(("ctx", "wt"), None),
        P("ctx", "wt"),
        P("ctx", "wt"),
        P("ctx", "wt"),
        P("ctx", "wt"),
        P("ctx", "wt"),
        P("ctx", "wt"),
        P("ctx", "wt"),
        P(("ctx", "wt"), None),
        P(("ctx", "wt"), None),
    )
    return jax.shard_map(local, mesh=mesh, in_specs=in_specs, out_specs=out_specs, check_vma=False)
```

```python
import jax
import jax.numpy as jnp
from jax import lax
from jax.experimental import pallas as pl
from jax.experimental.pallas import tpu as pltpu
from jax.sharding import PartitionSpec as P

QUERY_HEADS = 8
KEY_VALUE_HEADS = 2
ADAPTER_COUNT = 8
ADAPTER_RANK = 16
PROMPT = 2048
CONT = 256

EPS = 1e-06
THETA = 1000000.0
ROOT_HALF = 0.5**0.5
F32 = jnp.float32
BF16 = jnp.bfloat16
SWAP = [(0, 1), (1, 0)]


def normalized(inputs, norm_gain):
    return inputs * lax.rsqrt(jnp.mean(inputs * inputs, axis=-1, keepdims=True) + EPS) * norm_gain


def rotary_applied(inputs, cosine, sine_term):
    half_width = inputs.shape[-1] // 2
    first_half = inputs[..., :half_width]
    second_half = inputs[..., half_width:]
    return jnp.concatenate(
        [
            first_half * cosine - second_half * sine_term,
            second_half * cosine + first_half * sine_term,
        ],
        axis=-1,
    )


def product(left_side, right_side):
    return jnp.dot(left_side, right_side, preferred_element_type=F32)


def against(left_side, right_side):
    return lax.dot_general(
        left_side, right_side, (((1,), (1,)), ((), ())), preferred_element_type=F32
    )


def summed(left_side, right_side):
    return lax.dot_general(
        left_side, right_side, (((0,), (0,)), ((), ())), preferred_element_type=F32
    )


def low(value):
    return value.astype(BF16)


def attend_kernel(count_ref, kslot_ref, vslot_ref, q_ref, k_ref, v_ref, o_ref, lse_ref, acc, tot, *, heads, dim):
    group = pl.program_id(0)
    count = count_ref[group]
    rows = q_ref.shape[0]
    fold = tot.shape[-1]
    acc[...] = jnp.zeros_like(acc)
    tot[...] = jnp.zeros_like(tot)

    def step(index, masked):
        keys = k_ref[kslot_ref[group, index], 0]
        values = v_ref[vslot_ref[group, index], 0]
        for head in range(heads):
            lanes = slice(head * dim, (head + 1) * dim)
            scores = against(q_ref[:, lanes], keys)
            weights = jnp.exp(scores)
            if masked:
                row = lax.broadcasted_iota(jnp.int32, scores.shape, 0)
                col = lax.broadcasted_iota(jnp.int32, scores.shape, 1)
                weights = jnp.where(col <= row, weights, 0.0)
            part = weights[:, :fold]
            for start in range(fold, rows, fold):
                part = part + weights[:, start : start + fold]
            tot[head] += part
            acc[:, lanes] += product(low(weights), values)

    def body(index, carry):
        step(index, False)
        return carry

    lax.fori_loop(0, count - 1, body, 0)
    step(count - 1, True)
    lane = lax.broadcasted_iota(jnp.int32, lse_ref.shape, 1)
    lse = jnp.zeros(lse_ref.shape, F32)
    for head in range(heads):
        lanes = slice(head * dim, (head + 1) * dim)
        total = jnp.sum(tot[head], axis=-1, keepdims=True)
        o_ref[:, lanes] = low(acc[:, lanes] / total)
        lse = jnp.where(lane == head, jnp.log(total), lse)
    lse_ref[...] = lse


def attend_back_kernel(
    count_ref, kslot_ref, vslot_ref, q_ref, k_ref, v_ref, o_ref, lse_ref, g_ref, dq_ref, dk_near, dk_far, dv_near, dv_far, delta, *, heads, dim
):
    group = pl.program_id(0)
    count = count_ref[group]
    dq_ref[...] = jnp.zeros_like(dq_ref)
    for out_ref in (dk_near, dk_far, dv_near, dv_far):
        out_ref[...] = jnp.zeros_like(out_ref)
    half = dk_near.shape[0]

    def put(near_ref, far_ref, slot, value):
        @pl.when(slot < half)
        def _():
            near_ref[slot, 0] = low(value)

        @pl.when(slot >= half)
        def _():
            far_ref[slot - half, 0] = low(value)

    for head in range(heads):
        lanes = slice(head * dim, (head + 1) * dim)
        delta[head] = jnp.sum(
            o_ref[:, lanes].astype(F32) * g_ref[:, lanes].astype(F32), axis=-1, keepdims=True
        )

    def step(index, masked):
        keys = k_ref[kslot_ref[group, index], 0]
        values = v_ref[vslot_ref[group, index], 0]
        dk = jnp.zeros(keys.shape, F32)
        dv = jnp.zeros(values.shape, F32)
        for head in range(heads):
            lanes = slice(head * dim, (head + 1) * dim)
            queries = q_ref[:, lanes]
            upstream = g_ref[:, lanes]
            scores = against(queries, keys)
            weights = jnp.exp(scores - lse_ref[:, head : head + 1])
            if masked:
                row = lax.broadcasted_iota(jnp.int32, scores.shape, 0)
                col = lax.broadcasted_iota(jnp.int32, scores.shape, 1)
                weights = jnp.where(col <= row, weights, 0.0)
            grad_weights = against(upstream, values)
            grad_scores = low(weights * (grad_weights - delta[head]))
            dq_ref[:, lanes] += product(grad_scores, keys)
            dk += summed(grad_scores, queries)
            dv += summed(low(weights), upstream)
        put(dk_near, dk_far, kslot_ref[group, index], dk)
        put(dv_near, dv_far, vslot_ref[group, index], dv)

    def body(index, carry):
        step(index, False)
        return carry

    lax.fori_loop(0, count - 1, body, 0)
    step(count - 1, True)


def attend(tables, queries, key_all, value_all, groups, heads, dim):
    count, kslot, vslot = tables
    slots, _, block, _ = key_all.shape
    rows = queries.shape[0]
    fold = min(128, block)
    whole = pl.BlockSpec((slots, 1, block, dim), lambda g, *_: (0, g, 0, 0))
    mine = pl.BlockSpec((block, heads * dim), lambda g, *_: (g, 0))
    return pl.pallas_call(
        lambda *refs: attend_kernel(*refs, heads=heads, dim=dim),
        grid_spec=pltpu.PrefetchScalarGridSpec(
            num_scalar_prefetch=3,
            grid=(groups,),
            in_specs=[mine, whole, whole],
            out_specs=[mine, pl.BlockSpec((block, 128), lambda g, *_: (g, 0))],
            scratch_shapes=[
                pltpu.VMEM((block, heads * dim), F32),
                pltpu.VMEM((heads, block, fold), F32),
            ],
        ),
        out_shape=[
            jax.ShapeDtypeStruct((rows, heads * dim), BF16),
            jax.ShapeDtypeStruct((rows, 128), F32),
        ],
        compiler_params=pltpu.CompilerParams(vmem_limit_bytes=40 * 2**20),
        cost_estimate=pl.CostEstimate(
            flops=4 * rows * heads * dim * 2304, bytes_accessed=6 * 2**20, transcendentals=rows * heads * 2304
        ),
    )(count, kslot, vslot, queries, key_all, value_all)


def attend_back(tables, queries, key_all, value_all, heads_low, lse, grads, groups, heads, dim):
    count, kslot, vslot = tables
    slots, _, block, _ = key_all.shape
    rows = queries.shape[0]
    whole = pl.BlockSpec((slots, 1, block, dim), lambda g, *_: (0, g, 0, 0))
    part = pl.BlockSpec((slots // 2, 1, block, dim), lambda g, *_: (0, g, 0, 0))
    mine = pl.BlockSpec((block, heads * dim), lambda g, *_: (g, 0))
    return pl.pallas_call(
        lambda *refs: attend_back_kernel(*refs, heads=heads, dim=dim),
        grid_spec=pltpu.PrefetchScalarGridSpec(
            num_scalar_prefetch=3,
            grid=(groups,),
            in_specs=[mine, whole, whole, mine, pl.BlockSpec((block, 128), lambda g, *_: (g, 0)), mine],
            out_specs=[mine] + [part] * 4,
            scratch_shapes=[pltpu.VMEM((heads, block, 1), F32)],
        ),
        out_shape=[
            jax.ShapeDtypeStruct((rows, heads * dim), F32),
        ]
        + [jax.ShapeDtypeStruct((slots // 2, groups, block, dim), BF16)] * 4,
        compiler_params=pltpu.CompilerParams(vmem_limit_bytes=48 * 2**20),
        cost_estimate=pl.CostEstimate(
            flops=10 * rows * heads * dim * 2304, bytes_accessed=12 * 2**20, transcendentals=rows * heads * 2304
        ),
    )(count, kslot, vslot, queries, key_all, value_all, heads_low, lse, grads)


def gelu_parts(gate):
    slope = 0.7978845608028654
    square = gate * gate
    bend = jnp.tanh(slope * gate * (1.0 + 0.044715 * square))
    half = 0.5 * (1.0 + bend)
    grad = half + 0.5 * gate * (1.0 - bend * bend) * slope * (1.0 + 0.134145 * square)
    return gate * half, grad


def rms_scale(value):
    return lax.rsqrt(jnp.mean(value * value, axis=-1, keepdims=True) + EPS)


def rms_pull(value, scale, weighted):
    return scale * weighted - value * (
        scale * scale * scale * jnp.mean(value * weighted, axis=-1, keepdims=True)
    )


def move_columns(out_ref, in_ref, table_ref, count, block):
    for j in range(count):
        start = pl.multiple_of(table_ref[j] * block, block)
        out_ref[:, j * block : (j + 1) * block] = in_ref[:, pl.ds(start, block)].astype(
            out_ref.dtype
        )


def whole_call(kernel, inputs, outputs, scratch=(), tables=(), specs=None, flops=10**9):
    specs = specs or {}

    def full(array):
        return pl.BlockSpec(array.shape, lambda *_: (0,) * len(array.shape))

    in_specs = [specs.get(i, full(array)) for i, array in enumerate(inputs)]
    size = sum(a.size * a.dtype.itemsize for a in inputs)
    return pl.pallas_call(
        kernel,
        grid_spec=pltpu.PrefetchScalarGridSpec(
            num_scalar_prefetch=len(tables),
            grid=(1,),
            in_specs=in_specs,
            out_specs=[full(array) for array in outputs],
            scratch_shapes=list(scratch),
        ),
        out_shape=list(outputs),
        compiler_params=pltpu.CompilerParams(vmem_limit_bytes=56 * 2**20),
        cost_estimate=pl.CostEstimate(flops=flops, bytes_accessed=size, transcendentals=0),
    )(*tables, *inputs)


def first_kernel(order_ref, tokens_ref, gains_ref, select_ref, shrink_ref, moved_ref, low_ref, rank_ref, *, count, block, aligned):
    tokens = tokens_ref[...].astype(F32)
    first = low(tokens * rms_scale(tokens) * gains_ref[0:1, :])
    low_ref[...] = first
    ranks = against(first, shrink_ref[...])
    select = select_ref[...]
    width = select.shape[1]
    for i in range(3):
        rank_ref[:, i * width : (i + 1) * width] = low(select * ranks[:, i * width : (i + 1) * width])
    if aligned:
        move_columns(moved_ref, low_ref, order_ref, count, block)
    else:
        moved_ref[...] = first


def middle_kernel(
    half_ref, back_ref, own_ref, other_ref, tokens_ref, gains_ref, expand_ref, left_ref, right_ref,
    total_ref, laurel_ref, mid_ref, second_ref, rank_ref, work, *, count, block, aligned
):
    width = total_ref.shape[1]
    summed_all = own_ref[...] + other_ref[...].astype(F32)
    rank = low(summed_all[:, width:])
    rank_ref[...] = rank
    if aligned:
        work[...] = summed_all[:, :width]
        move_columns(total_ref, work, back_ref, count, block)
        attn = total_ref[...] + product(rank, expand_ref[...])
    else:
        attn = summed_all[:, :width] + product(rank, expand_ref[...])
    total_ref[...] = attn
    tokens = tokens_ref[...].astype(F32)
    first = tokens * rms_scale(tokens) * gains_ref[0:1, :]
    laurel = product(low(product(low(first), left_ref[...])), right_ref[...])
    laurel_ref[...] = laurel
    mid = (
        tokens
        + attn * rms_scale(attn) * gains_ref[1:2, :]
        + first
        + laurel * rms_scale(laurel) * gains_ref[2:3, :]
    ) * ROOT_HALF
    mid_ref[...] = mid
    second_ref[...] = low(mid * rms_scale(mid) * gains_ref[3:4, :])


def keep_rows(out_ref, work_ref, value, pick_ref):
    if out_ref.shape[0] == value.shape[0]:
        out_ref[...] = value.astype(out_ref.dtype)
    else:
        work_ref[...] = value
        rows = out_ref.shape[0]
        start = pl.multiple_of(pick_ref[0] * rows, rows)
        out_ref[...] = work_ref[pl.ds(start, rows), :].astype(out_ref.dtype)


def layer_kernel(
    half_ref, pick_ref, near_ref, y_ref, z_ref, yz_ref, mid_ref, gains_ref, expand_ref, gate_ref, lift_ref, layer_ref, up_ref,
    result_ref, layer_grad_ref, after_ref, grad_ref, expand_grad_ref, kept
):
    width = mid_ref.shape[1]
    joined = near_ref[...].astype(F32) + y_ref[...] + z_ref[...] + yz_ref[...]
    rank = low(joined[:, width:])
    total = joined[:, :width] + product(rank, expand_ref[...])
    scale = rms_scale(total)
    gain = gains_ref[4:5, :]
    after = mid_ref[...] + total * scale * gain
    layer_pre = product(low(after), gate_ref[...])
    layer_in = layer_ref[...].astype(F32)
    act, slope = gelu_parts(layer_pre)
    back = product(low(act * layer_in), lift_ref[...])
    back_scale = rms_scale(back)
    last_gain = gains_ref[5:6, :]
    result_ref[...] = low(after + back * back_scale * last_gain)
    upstream = up_ref[...].astype(F32)
    grad_back = low(rms_pull(back, back_scale, upstream * last_gain))
    grad_gated = against(grad_back, lift_ref[...])
    layer_grad_ref[...] = grad_gated * act
    grad_pre = low(grad_gated * layer_in * slope)
    grad_after = upstream + against(grad_pre, gate_ref[...])
    after_ref[...] = grad_after
    grad_ffn = low(rms_pull(total, scale, grad_after * gain))
    grad_ref[...] = grad_ffn
    keep_rows(expand_grad_ref, kept, summed(rank, grad_ffn), pick_ref)


def turn_kernel(
    order_ref, pick_ref, near_ref, y_ref, z_ref, yz_ref, mid_ref, after_ref, total_ref, laurel_ref, second_ref, gains_ref, gate_ref, up_ref,
    right_ref, left_ref, expand_ref, rank_ref, select_ref,
    sent_ref, scaled_ref, first_ref, grads_ref, work, kept, *, count, block, aligned
):
    width = mid_ref.shape[1]
    ranks = select_ref.shape[1]
    joined = near_ref[...].astype(F32) + y_ref[...] + z_ref[...] + yz_ref[...]
    rank_gate = low(joined[:, width : width + ranks])
    rank_up = low(joined[:, width + ranks :])
    grad_second = joined[:, :width]
    grad_second = grad_second + product(rank_gate, gate_ref[...]) + product(rank_up, up_ref[...])
    keep_rows(grads_ref.at[0], kept, summed(rank_gate, second_ref[...]), pick_ref)
    keep_rows(grads_ref.at[1], kept, summed(rank_up, second_ref[...]), pick_ref)
    mid = mid_ref[...]
    grad_mid = after_ref[...] + rms_pull(mid, rms_scale(mid), grad_second * gains_ref[3:4, :])
    scaled = grad_mid * ROOT_HALF
    scaled_ref[...] = scaled
    attn = total_ref[...]
    grad_attn = rms_pull(attn, rms_scale(attn), scaled * gains_ref[1:2, :])
    laurel = laurel_ref[...]
    grad_laurel = low(rms_pull(laurel, rms_scale(laurel), scaled * gains_ref[2:3, :]))
    grad_rank = low(against(grad_laurel, right_ref[...]))
    first_ref[...] = scaled + against(grad_rank, left_ref[...])
    attn_low = low(grad_attn)
    keep_rows(grads_ref.at[2], kept, summed(rank_ref[...], attn_low), pick_ref)
    sent_ref[:, width:] = low(select_ref[...] * against(attn_low, expand_ref[...]))
    if aligned:
        work[...] = grad_attn
        for j in range(count):
            start = pl.multiple_of(order_ref[j] * block, block)
            sent_ref[:, j * block : (j + 1) * block] = low(work[:, pl.ds(start, block)])
    else:
        sent_ref[:, :width] = attn_low


def last_kernel(
    half_ref, back_ref, pick_ref, own_ref, other_ref, tokens_ref, gains_ref, scaled_ref, first_ref, shrink_ref,
    input_ref, grads_ref, work, place, kept, *, count, block, aligned
):
    width = scaled_ref.shape[1]
    joined = own_ref[...] + other_ref[...].astype(F32)
    ranks = low(joined[:, width:])
    each = ranks.shape[1] // 3
    work[...] = joined[:, :width]
    if aligned:
        move_columns(place, work, back_ref, count, block)
        grad_first = place[...]
    else:
        grad_first = work[...]
    grad_first = grad_first + first_ref[...] + product(ranks, shrink_ref[...])
    tokens = tokens_ref[...].astype(F32)
    scale = rms_scale(tokens)
    gain = gains_ref[0:1, :]
    input_ref[...] = scaled_ref[...] + rms_pull(tokens, scale, grad_first * gain)
    first = low(tokens * scale * gain)
    for i in range(3):
        keep_rows(
            grads_ref.at[i], kept, summed(ranks[:, i * each : (i + 1) * each], first), pick_ref
        )


def gather_parts(out_ref, parts, table_ref, count, width):
    height = parts[0].shape[0]
    block = width // count
    for i, part in enumerate(parts):
        rows = slice(i * height, (i + 1) * height)
        if block % 128 == 0:
            for j in range(count):
                start = pl.multiple_of(table_ref[j] * block, block)
                out_ref[rows, j * block : (j + 1) * block] = part[:, pl.ds(start, block)]
        else:
            out_ref[rows, :] = part[...]


def ranks_of(out_ref, parts, select_ref, maps_ref):
    height = parts[0].shape[0]
    ranks = select_ref.shape[1]
    for i, part in enumerate(parts):
        rows = slice(i * height, (i + 1) * height)
        found = against(part[...], maps_ref[...])
        for start in range(0, out_ref.shape[1], ranks):
            out_ref[rows, start : start + ranks] = low(
                select_ref[rows, :] * found[:, start : start + ranks]
            )


def bring(pieces, space, sems):
    rows = pieces[0].shape[0]
    copies = [
        pltpu.make_async_copy(piece, space.at[pl.ds(i * rows, rows), :], sems.at[i])
        for i, piece in enumerate(pieces)
    ]
    for copy in copies:
        copy.start()
    return copies


def put_columns(out_ref, value, start, table_ref, block):
    size = value.shape[1]
    if block % 128:
        out_ref[:, pl.ds(start, size)] = value.astype(out_ref.dtype)
        return
    for i in range(size // block):
        place = pl.multiple_of(table_ref[start // block + i] * block, block)
        out_ref[:, pl.ds(place, block)] = value[:, i * block : (i + 1) * block].astype(out_ref.dtype)


def feed_kernel(order_ref, *refs, pieces, width, count):
    parts, (select_ref, shrink_ref, gexp_ref, uexp_ref, dshr_ref), refs = refs[:4], refs[4:9], refs[9:]
    gates, ups, downs = refs[:pieces], refs[pieces : 2 * pieces], refs[2 * pieces : 3 * pieces]
    rank_ref, act_ref, slope_ref, hid_ref, part_ref, x_ref, gate_w, up_w, down_w, sems = refs[3 * pieces :]
    arriving = bring(gates, gate_w, sems.at[0]) + bring(ups, up_w, sems.at[1])
    arriving_down = bring(downs, down_w, sems.at[2])
    ranks = select_ref.shape[1]
    hidden_width = gate_w.shape[1]
    chunk = min(256, hidden_width)
    gather_parts(x_ref, parts, order_ref, count, width)
    ranks_of(rank_ref, parts, select_ref, shrink_ref)
    for copy in arriving:
        copy.wait()

    @pl.loop(0, hidden_width // chunk)
    def _(i):
        lanes = pl.ds(pl.multiple_of(i * chunk, chunk), chunk)
        gate = product(x_ref[...], gate_w[:, lanes]) + product(rank_ref[:, :ranks], gexp_ref[:, lanes])
        up = product(x_ref[...], up_w[:, lanes]) + product(rank_ref[:, ranks:], uexp_ref[:, lanes])
        act, slope = gelu_parts(gate)
        act_ref[:, lanes] = low(act)
        slope_ref[:, lanes] = low(slope * up)
        hid_ref[:, lanes] = low(act * up)

    for copy in arriving_down:
        copy.wait()
    step = 256

    @pl.loop(0, width // step)
    def _(i):
        start = pl.multiple_of(i * step, step)
        put_columns(
            part_ref, against(hid_ref[...], down_w[pl.ds(start, step), :]), start, order_ref, width // count
        )

    part_ref[:, width:] = (select_ref[...] * against(hid_ref[...], dshr_ref[...])).astype(part_ref.dtype)


def feed_call(kernel, order, parts, inputs, weights, outputs, scratch, flops):
    def full(array):
        return pl.BlockSpec(array.shape, lambda *_: (0,) * len(array.shape))

    pieces = [piece for matrix in weights for piece in matrix]
    matrix = pltpu.VMEM((len(weights[0]) * weights[0][0].shape[0], weights[0][0].shape[1]), BF16)
    width = parts[0].shape[1]
    return pl.pallas_call(
        lambda *refs: kernel(*refs, pieces=len(weights[0]), width=width, count=order.shape[0]),
        grid_spec=pltpu.PrefetchScalarGridSpec(
            num_scalar_prefetch=1,
            grid=(1,),
            in_specs=[full(array) for array in (*parts, *inputs)]
            + [pl.BlockSpec(memory_space=pl.ANY)] * len(pieces),
            out_specs=[full(array) for array in outputs],
            scratch_shapes=list(scratch)
            + [matrix, matrix, matrix, pltpu.SemaphoreType.DMA((3, len(weights[0])))],
        ),
        out_shape=list(outputs),
        compiler_params=pltpu.CompilerParams(vmem_limit_bytes=58 * 2**20),
        cost_estimate=pl.CostEstimate(flops=flops, bytes_accessed=20 * 2**20, transcendentals=0),
    )(order, *parts, *inputs, *pieces)


def feed(order, parts, select, shrink, gexp, uexp, dshr, gates, ups, downs, out_dtype):
    rows, width = 4 * parts[0].shape[0], parts[0].shape[1]
    hidden, ranks = gexp.shape[1], select.shape[1]
    low_hidden = jax.ShapeDtypeStruct((rows, hidden), BF16)
    return feed_call(
        feed_kernel,
        order,
        parts,
        (select, shrink, gexp, uexp, dshr),
        (gates, ups, downs),
        (
            jax.ShapeDtypeStruct((rows, 2 * ranks), BF16),
            low_hidden,
            low_hidden,
            low_hidden,
            jax.ShapeDtypeStruct((rows, width + ranks), out_dtype),
        ),
        (pltpu.VMEM((rows, width), BF16),),
        6 * rows * width * hidden,
    )


def feed_back_kernel(order_ref, *refs, pieces, width, count):
    parts, refs = refs[:4], refs[4:]
    (
        select_ref,
        dexp_ref,
        rank_ref,
        start_ref,
        act_ref,
        slope_ref,
        hid_ref,
        gexp_ref,
        uexp_ref,
        dshr_ref,
    ), refs = refs[:10], refs[10:]
    gates, ups, downs = refs[:pieces], refs[pieces : 2 * pieces], refs[2 * pieces : 3 * pieces]
    part_ref, grads_ref, g_ref, down_rank, gate_grad, up_grad, gate_w, up_w, down_w, sems = refs[3 * pieces :]
    arriving = bring(downs, down_w, sems.at[2])
    arriving_next = bring(gates, gate_w, sems.at[0]) + bring(ups, up_w, sems.at[1])
    ranks = select_ref.shape[1]
    hidden_width = gate_w.shape[1]
    chunk = min(256, hidden_width)
    gather_parts(g_ref, parts, order_ref, count, width)
    ranks_of(down_rank, parts, select_ref, dexp_ref)
    for copy in arriving:
        copy.wait()

    @pl.loop(0, hidden_width // chunk)
    def _(i):
        lanes = pl.ds(pl.multiple_of(i * chunk, chunk), chunk)
        grad_hidden = product(g_ref[...], down_w[:, lanes]) + product(down_rank[...], dshr_ref[:, lanes])
        grad_gate = low(grad_hidden * slope_ref[:, lanes].astype(F32))
        grad_up = low(grad_hidden * act_ref[:, lanes].astype(F32))
        gate_grad[:, lanes] = grad_gate
        up_grad[:, lanes] = grad_up
        grads_ref[0, :, lanes] = start_ref[0, :, lanes] + summed(rank_ref[:, :ranks], grad_gate)
        grads_ref[1, :, lanes] = start_ref[1, :, lanes] + summed(rank_ref[:, ranks:], grad_up)
        grads_ref[2, :, lanes] = start_ref[2, :, lanes] + summed(down_rank[...], hid_ref[:, lanes])

    for copy in arriving_next:
        copy.wait()
    step = 256

    @pl.loop(0, width // step)
    def _(i):
        start = pl.multiple_of(i * step, step)
        found = against(gate_grad[...], gate_w[pl.ds(start, step), :]) + against(
            up_grad[...], up_w[pl.ds(start, step), :]
        )
        put_columns(part_ref, found, start, order_ref, width // count)

    select = select_ref[...]
    part_ref[:, width : width + ranks] = (select * against(gate_grad[...], gexp_ref[...])).astype(part_ref.dtype)
    part_ref[:, width + ranks :] = (select * against(up_grad[...], uexp_ref[...])).astype(part_ref.dtype)


def feed_back(order, parts, select, dexp, start, kept, gexp, uexp, dshr, gates, ups, downs, out_dtype):
    rows, width = 4 * parts[0].shape[0], parts[0].shape[1]
    hidden, ranks = gexp.shape[1], select.shape[1]
    low_hidden = pltpu.VMEM((rows, hidden), BF16)
    return feed_call(
        feed_back_kernel,
        order,
        parts,
        (select, dexp, kept[0], start, *kept[1:], gexp, uexp, dshr),
        (gates, ups, downs),
        (
            jax.ShapeDtypeStruct((rows, width + 2 * ranks), out_dtype),
            jax.ShapeDtypeStruct((3, ranks, hidden), F32),
        ),
        (pltpu.VMEM((rows, width), BF16), pltpu.VMEM((rows, ranks), BF16), low_hidden, low_hidden),
        6 * rows * width * hidden,
    )


def local(
    tokens,
    layer_input,
    out_grad,
    block_device,
    adapter_pick,
    norm_gains,
    head_norm_gains,
    query_weight,
    key_matrix,
    value_matrix,
    gate_weight,
    up_weight,
    out_weight,
    down_weight,
    laurel_left,
    laurel_right,
    layer_gate,
    layer_lift,
    query_shrink,
    key_shrink,
    value_shrink,
    gate_shrink,
    up_shrink,
    out_shrink,
    down_shrink,
    query_expand,
    key_widen_maps,
    value_widen_maps,
    gate_expand,
    up_expand,
    out_expand,
    down_expand,
):
    count_ctx = lax.axis_size("ctx")
    bit_count = count_ctx.bit_length() - 1
    groups = block_device.shape[0]
    local_rows, width = tokens.shape
    block_len = local_rows // groups
    half_rows = local_rows // 2
    head_dim = head_norm_gains.shape[1]
    heads_local = query_weight.shape[1] // head_dim
    adapter_width = ADAPTER_COUNT * ADAPTER_RANK
    model_block = width // count_ctx
    hidden_slice = gate_weight.shape[1] // 4
    me = lax.axis_index("ctx")
    core = lax.axis_index("wt")

    spread_bits = list(range(3, bit_count)) + [0]
    team_place = (me >> 1) & 3

    def flip(value, bit):
        return lax.ppermute(value, "ctx", [(i, i ^ (1 << bit)) for i in range(count_ctx)])

    def other_core(value):
        return lax.ppermute(value, "wt", SWAP)

    def own_half(value):
        return lax.dynamic_slice_in_dim(value, core * half_rows, half_rows, 0)

    def other_half(value):
        return lax.dynamic_slice_in_dim(value, (1 - core) * half_rows, half_rows, 0)

    def both_halves(own, other):
        return jnp.where(
            core == 0, jnp.concatenate([own, other], axis=0), jnp.concatenate([other, own], axis=0)
        )

    def column_blocks(value, places):
        return jnp.concatenate(
            [
                lax.dynamic_slice_in_dim(value, place * model_block, model_block, 1)
                for place in places
            ],
            axis=1,
        )

    rest = count_ctx // 4
    rest_bits = list(range(2, bit_count))

    def rest_place(apart):
        return sum(((apart >> bit) & 1) << i for i, bit in enumerate(rest_bits))

    weight_order = [
        me
        ^ (
            (j // (2 * rest)) * 2
            + (j // rest) % 2
            + sum(((j >> i) & 1) << bit for i, bit in enumerate(rest_bits))
        )
        for j in range(count_ctx)
    ]
    weight_back = [
        (((d ^ me) >> 1) & 1) * 2 * rest + ((d ^ me) & 1) * rest + rest_place(d ^ me)
        for d in range(count_ctx)
    ]
    piece_masks = [0]
    for bit in spread_bits:
        piece_masks = piece_masks + [mask | (1 << bit) for mask in piece_masks]
    team_order = [me ^ mask ^ (2 * t) for mask in piece_masks for t in range(4)]
    team_back = [
        4 * sum((((b ^ me) >> bit) & 1) << i for i, bit in enumerate(spread_bits))
        + (((b ^ me) >> 1) & 3)
        for b in range(count_ctx)
    ]

    def to_member(value, member):
        if member == 0:
            return value
        return lax.ppermute(value, "ctx", [(d, d ^ (2 * member)) for d in range(count_ctx)])

    def team_split(shard):
        parts = [
            to_member(
                lax.dynamic_slice_in_dim(
                    shard, (team_place ^ member) * hidden_slice, hidden_slice, 1
                ),
                member,
            )
            for member in range(4)
        ]
        return joined(parts[0], parts[1]), joined(parts[2], parts[3])

    def joined(own, arrived):
        return jnp.concatenate([own, arrived], axis=0)

    prompt_blocks = PROMPT // block_len
    cont_blocks = CONT // block_len
    device_ids = jnp.arange(count_ctx, dtype=jnp.int32)
    block_of = jnp.sum(
        jnp.where(block_device[None] == device_ids[:, None, None], device_ids[None, None, :], 0),
        axis=2,
    )
    cont_of = (block_of - prompt_blocks) // cont_blocks
    pick_of = jnp.sum(
        jnp.where(
            cont_of[:, :, None] == jnp.arange(adapter_pick.shape[1], dtype=jnp.int32),
            adapter_pick[None],
            0,
        ),
        axis=2,
    )
    pick_of = jnp.where(block_of < prompt_blocks, -1, pick_of)
    compact = groups == 1 and count_ctx * 8 == adapter_width
    own_pick = jnp.maximum(jnp.sum(jnp.where(device_ids[:, None] == me, pick_of, 0), axis=0), 0)
    own_pick = own_pick[:1].astype(jnp.int32)
    grad_rows = ADAPTER_RANK if compact else adapter_width
    grad_type = BF16 if compact else F32

    def picks_at(device):
        return jnp.sum(jnp.where(device_ids[:, None] == device, pick_of, 0), axis=0)

    def select_rows(picks):
        rows = jnp.repeat(picks, block_len)
        return (
            jnp.arange(adapter_width, dtype=jnp.int32)[None, :] // ADAPTER_RANK == rows[:, None]
        ).astype(F32)

    select = select_rows(picks_at(me))
    select_own = own_half(select)
    team_select = [select_rows(picks_at(me ^ (2 * t))) for t in range(4)]
    select_near = jnp.concatenate([own_half(part) for part in team_select], axis=0)
    select_far = jnp.concatenate([other_half(part) for part in team_select], axis=0)

    my_block = jnp.sum(jnp.where(device_ids[:, None] == me, block_of, 0), axis=0)
    positions = (
        my_block[:, None] * block_len + jnp.arange(block_len, dtype=jnp.int32)[None, :]
    ).reshape(-1)
    seq_pos = jnp.where(positions < PROMPT, positions, PROMPT + (positions - PROMPT) % CONT)
    frequency = THETA ** (-2.0 * jnp.arange(head_dim // 2, dtype=F32) / head_dim)
    rotary_angles = seq_pos.astype(F32)[:, None] * frequency[None, :]
    cosine = jnp.cos(rotary_angles)[:, None, :]
    sine_term = jnp.sin(rotary_angles)[:, None, :]
    cont_start = prompt_blocks + (my_block - prompt_blocks) // cont_blocks * cont_blocks
    is_prompt = my_block < prompt_blocks
    visible_count = jnp.where(
        is_prompt, my_block + 1, prompt_blocks + my_block - cont_start + 1
    ).astype(jnp.int32)
    entries = jnp.arange(prompt_blocks + cont_blocks, dtype=jnp.int32)
    visible_block = jnp.where(
        is_prompt[:, None] | (entries < prompt_blocks)[None, :],
        entries[None, :],
        cont_start[:, None] + entries[None, :] - prompt_blocks,
    )
    visible_device = jnp.sum(
        jnp.where(
            visible_block[:, :, None] == device_ids[None, None, :], block_device[:, None, :], 0
        ),
        axis=2,
    )
    apart = visible_device ^ me
    key_slot = (((apart >> 1) & 1) * 2 + (apart & 1)) * rest + rest_place(apart)
    value_slot = ((apart & 1) * 2 + ((apart >> 1) & 1)) * rest + rest_place(apart)
    tables = (visible_count, key_slot.astype(jnp.int32), value_slot.astype(jnp.int32))

    gains = norm_gains.astype(F32)
    query_gain = head_norm_gains[0].astype(F32)
    key_gain = head_norm_gains[1].astype(F32)

    def query_piece(projected):
        return (
            rotary_applied(
                normalized(projected.reshape(local_rows, -1, head_dim), query_gain),
                cosine,
                sine_term,
            )
            * head_dim ** (-0.5)
        ).reshape(local_rows, -1)

    def key_piece(projected):
        return rotary_applied(
            normalized(projected.reshape(local_rows, -1, head_dim), key_gain), cosine, sine_term
        ).reshape(local_rows, -1)

    def value_piece(projected):
        return normalized(projected.reshape(local_rows, -1, head_dim), 1.0).reshape(local_rows, -1)

    def slab_product(value, slabs):
        middle = value.shape[1] // 2
        return product(value[:, :middle], slabs[0]) + product(value[:, middle:], slabs[1])

    def slab_against(value, slabs):
        return jnp.concatenate([against(value, slabs[0]), against(value, slabs[1])], axis=1)

    half = jnp.reshape(core, (1,)).astype(jnp.int32)
    aligned = model_block % 128 == 0
    style = dict(count=count_ctx, block=model_block, aligned=aligned)
    weight_order_table = jnp.stack(weight_order).astype(jnp.int32)
    weight_back_table = jnp.stack(weight_back).astype(jnp.int32)
    team_order_table = jnp.stack(team_order).astype(jnp.int32)
    half_spec = pl.BlockSpec((half_rows, width), lambda i, half, *_: (half[0], 0))
    wide_f32 = jax.ShapeDtypeStruct((half_rows, width), F32)
    wide_low = jax.ShapeDtypeStruct((half_rows, width), BF16)
    work_space = pltpu.VMEM((half_rows, width), F32)
    kept_space = pltpu.VMEM((adapter_width, width), F32)

    def moved(value, places):
        return value if aligned else column_blocks(value, places)

    def moved_back(value, places):
        if aligned:
            return value
        flat = value.reshape(-1, value.shape[-1])
        flat = jnp.concatenate([column_blocks(flat[:, :width], places), flat[:, width:]], axis=1)
        return flat.reshape(value.shape)

    first_shrink = jnp.concatenate([query_shrink, key_shrink, value_shrink], axis=0)
    first_moved, first_low, rank_first = whole_call(
        lambda *refs: first_kernel(*refs, **style),
        (tokens, gains, select, first_shrink),
        (
            jax.ShapeDtypeStruct(tokens.shape, BF16),
            jax.ShapeDtypeStruct(tokens.shape, BF16),
            jax.ShapeDtypeStruct((local_rows, 3 * adapter_width), BF16),
        ),
        tables=(weight_order_table,),
    )
    first_moved = moved(first_moved, weight_order)
    rank_query = rank_first[:, :adapter_width]
    rank_key = rank_first[:, adapter_width : 2 * adapter_width]
    rank_value = rank_first[:, 2 * adapter_width :]

    far_bits, near_bit = spread_bits[:-1], spread_bits[-1]
    x_bit, y_bit = 0, 1
    first_bit = rest_bits[0]
    sent_before = {}

    def queued(line, value, move, depth=2):
        earlier = sent_before.setdefault(line, [])
        if len(earlier) >= depth:
            value = lax.optimization_barrier((value, earlier[-depth]))[0]
        result = move(value)
        earlier.append(result)
        return result

    def over_x(value):
        return queued("x", value, lambda v: flip(v, x_bit))

    def over_y(value):
        return queued("y", value, lambda v: flip(v, y_bit))

    def over_rest(value, bits):
        for bit in bits:
            value = joined(value, queued("z", value, lambda v, bit=bit: flip(v, bit)))
        return value

    def spread_far(piece):
        pieces = [piece]
        for bit in far_bits:
            pieces = pieces + [queued("z", other, lambda v, bit=bit: flip(v, bit)) for other in pieces]
        return pieces[1:]

    def near(pieces):
        return [over_x(piece) for piece in pieces]

    step = lax.optimization_barrier
    kv_weight = jnp.concatenate([key_matrix, value_matrix], axis=1)
    out_rows, down_rows = out_weight.T, down_weight.T
    kv_part = joined(kv_weight, flip(kv_weight, first_bit))
    query_part = joined(query_weight, flip(query_weight, first_bit))
    out_part = joined(out_rows, flip(out_rows, first_bit))
    kv_part = over_rest(kv_part, rest_bits[1:])
    gate_a, gate_b = team_split(gate_weight)
    query_part = over_rest(query_part, rest_bits[1:])
    kv_slab = joined(kv_part, over_x(kv_part))
    kv_slab, gate_a, gate_b, up_weight, down_rows, out_part = step(
        (kv_slab, gate_a, gate_b, up_weight, down_rows, out_part)
    )
    kv_slabs = kv_slab, over_y(kv_slab)
    up_a, up_b = team_split(up_weight)
    query_slab = joined(query_part, over_x(query_part))
    gate_far_a = spread_far(gate_a)
    gate_near_a = near([gate_a])
    query_y_a = over_y(query_slab[: width // 4])
    kv_slabs, query_slab, gate_far_a, up_a, up_b = step((kv_slabs, query_slab, gate_far_a, up_a, up_b))

    kv_projected = slab_product(first_moved, kv_slabs)
    kv_width = key_matrix.shape[1]
    key_projected = kv_projected[:, :kv_width] + product(rank_key, key_widen_maps)
    value_projected = kv_projected[:, kv_width:] + product(rank_value, value_widen_maps)
    key_low = low(key_piece(key_projected)).reshape(1, groups, block_len, head_dim)
    value_low = low(value_piece(value_projected)).reshape(1, groups, block_len, head_dim)
    kv_part = jnp.stack([key_low, value_low], axis=1)
    gate_far_b = spread_far(gate_b)
    down_a, down_b = team_split(down_rows)
    kv_part, gate_far_b, gate_near_a, query_y_a, down_a, down_b, out_part = step(
        (kv_part, gate_far_b, gate_near_a, query_y_a, down_a, down_b, out_part)
    )
    for bit in rest_bits:
        kv_part = joined(kv_part, flip(kv_part, bit))
    out_part = over_rest(out_part, rest_bits[1:])
    query_y_b = over_y(query_slab[width // 4 :])
    gate_near_b = near([gate_b])
    gate_far_near_a = near(gate_far_a)
    kv_part, out_part, gate_near_b, gate_far_near_a, query_y_b = step(
        (kv_part, out_part, gate_near_b, gate_far_near_a, query_y_b)
    )
    key_part, value_part = kv_part[:, 0], kv_part[:, 1]
    key_x, value_y = flip(key_part, x_bit), flip(value_part, y_bit)
    up_far_a = spread_far(up_a)
    key_x, value_y, up_far_a = step((key_x, value_y, up_far_a))
    key_part = joined(key_part, key_x)
    value_part = joined(value_part, value_y)
    key_all = joined(key_part, flip(key_part, y_bit))
    value_all = joined(value_part, flip(value_part, x_bit))
    query_slabs = query_slab, joined(query_y_a, query_y_b)
    query_proj = slab_product(first_moved, query_slabs) + product(rank_query, query_expand)
    query_low = low(query_piece(query_proj))
    up_far_b = spread_far(up_b)
    out_slab = joined(out_part, over_x(out_part))
    key_all, value_all, query_low, up_far_b, out_slab = step(
        (key_all, value_all, query_low, up_far_b, out_slab)
    )
    out_slabs = out_slab, over_y(out_slab)
    down_far_a = spread_far(down_a)
    gate_far_near_b = near(gate_far_b)
    up_near_a = near([up_a])
    up_near_b = near([up_b])
    heads_low, lse = attend(tables, query_low, key_all, value_all, groups, heads_local, head_dim)

    heads_low, out_slabs, down_far_a, gate_far_near_b, up_near_a, up_near_b = step(
        (heads_low, out_slabs, down_far_a, gate_far_near_b, up_near_a, up_near_b)
    )
    down_far_b = spread_far(down_b)
    up_far_near_a = near(up_far_a)
    down_near_a, down_near_b = near([down_a]), near([down_b])
    attn_part = jnp.concatenate(
        [slab_against(heads_low, out_slabs), select * against(heads_low, out_shrink)], axis=1
    )
    attn_total, laurel_back, mid_stream, second_low, rank_out = whole_call(
        lambda *refs: middle_kernel(*refs, **style),
        (
            moved_back(own_half(attn_part), weight_back),
            moved_back(other_core(other_half(attn_part)), weight_back),
            tokens,
            gains,
            out_expand,
            laurel_left,
            laurel_right,
        ),
        (
            wide_f32,
            wide_f32,
            wide_f32,
            wide_low,
            jax.ShapeDtypeStruct((half_rows, adapter_width), BF16),
        ),
        scratch=(work_space,),
        tables=(half, weight_back_table),
        specs={2: half_spec},
    )

    second_low, down_far_b, up_far_near_a, down_near_a, down_near_b = step(
        (second_low, down_far_b, up_far_near_a, down_near_a, down_near_b)
    )
    up_far_near_b = near(up_far_b)
    down_far_near_a, down_far_near_b = near(down_far_a), near(down_far_b)

    def in_order(own, far, near_own, near_far):
        first, second = ([o] + f + n + nf for o, f, n, nf in zip(own, far, near_own, near_far))
        return [piece for pair in zip(first, second) for piece in pair]

    gate_pieces = in_order(
        (gate_a, gate_b),
        (gate_far_a, gate_far_b),
        (gate_near_a, gate_near_b),
        (gate_far_near_a, gate_far_near_b),
    )
    up_pieces = in_order(
        (up_a, up_b), (up_far_a, up_far_b), (up_near_a, up_near_b), (up_far_near_a, up_far_near_b)
    )
    down_pieces = in_order(
        (down_a, down_b),
        (down_far_a, down_far_b),
        (down_near_a, down_near_b),
        (down_far_near_a, down_far_near_b),
    )

    def team_gather(value):
        near_parts = [to_member(value, member) for member in range(4)]
        return near_parts, [other_core(part) for part in near_parts]

    def team_sum(near_part, far_part):
        arrived = other_core(far_part).astype(F32)
        parts = []
        for member in (3, 1, 2, 0):
            rows = slice(member * half_rows, (member + 1) * half_rows)
            parts.append(to_member(low(near_part[rows] + arrived[rows]), member))
        return parts

    def hidden_columns(value):
        return lax.dynamic_slice_in_dim(value, team_place * hidden_slice, hidden_slice, 1)

    feed_maps = moved(jnp.concatenate([gate_shrink, up_shrink], axis=0), team_order)
    down_map = moved(down_expand, team_order)
    slices = tuple(hidden_columns(value) for value in (gate_expand, up_expand, down_shrink))
    pieces = (gate_pieces, up_pieces, down_pieces)

    second_near, second_far = team_gather(moved(second_low, team_order))
    *kept_far, part_far = feed(
        team_order_table, second_far, select_far, feed_maps, *slices, *pieces, BF16
    )
    *kept_near, part_near = feed(
        team_order_table, second_near, select_near, feed_maps, *slices, *pieces, F32
    )
    ffn_parts = team_sum(part_near, part_far)

    result_own, layer_input_own, grad_after, grad_ffn, down_expand_grad = whole_call(
        layer_kernel,
        (
            *(moved_back(part, team_back) for part in ffn_parts),
            mid_stream,
            gains,
            down_expand,
            layer_gate,
            layer_lift,
            layer_input,
            out_grad,
        ),
        (
            wide_low,
            jax.ShapeDtypeStruct((half_rows, layer_input.shape[1]), F32),
            wide_f32,
            wide_low,
            jax.ShapeDtypeStruct((grad_rows, width), grad_type),
        ),
        scratch=(kept_space,),
        tables=(half, own_pick),
        specs={
            9: pl.BlockSpec((half_rows, layer_input.shape[1]), lambda i, half, *_: (half[0], 0)),
            10: half_spec,
        },
    )

    grad_near, grad_far = team_gather(moved(grad_ffn, team_order))
    nothing = jnp.zeros((3, adapter_width, hidden_slice), F32)
    back_far, team_grads = feed_back(
        team_order_table, grad_far, select_far, down_map, nothing, kept_far, *slices, *pieces, BF16
    )
    back_near, team_grads = feed_back(
        team_order_table, grad_near, select_near, down_map, team_grads, kept_near, *slices, *pieces, F32
    )
    second_parts = team_sum(back_near, back_far)
    grad_sent, grad_scaled, grad_first, own_grads = whole_call(
        lambda *refs: turn_kernel(*refs, **style),
        (
            *(moved_back(part, team_back) for part in second_parts),
            mid_stream,
            grad_after,
            attn_total,
            laurel_back,
            second_low,
            gains,
            gate_shrink,
            up_shrink,
            laurel_right,
            laurel_left,
            out_expand,
            rank_out,
            select_own,
        ),
        (
            jax.ShapeDtypeStruct((half_rows, width + adapter_width), BF16),
            wide_f32,
            wide_f32,
            jax.ShapeDtypeStruct((3, grad_rows, width), grad_type),
        ),
        scratch=(work_space, kept_space),
        tables=(weight_order_table, own_pick),
    )
    if not aligned:
        grad_sent = jnp.concatenate(
            [column_blocks(grad_sent[:, :width], weight_order), grad_sent[:, width:]], axis=1
        )
    grad_joined = both_halves(grad_sent, other_core(grad_sent))
    grad_attn = grad_joined[:, :width]
    grad_rank_out = grad_joined[:, width:]
    out_shrink_grad = summed(grad_rank_out, heads_low)
    grad_heads = low(slab_product(grad_attn, out_slabs) + product(grad_rank_out, out_shrink))

    grad_queries, keys_near, keys_far, values_near, values_far = attend_back(
        tables, query_low, key_all, value_all, heads_low, lse, grad_heads, groups, heads_local, head_dim
    )

    keys_come, values_come = flip(keys_far, y_bit), flip(values_far, x_bit)
    keep = keys_near.shape[0] // 2

    def sum_of(own, arrived, rows):
        return low(own[rows].astype(F32) + arrived[rows])

    keys_far = flip(sum_of(keys_near, keys_come, slice(keep, None)), x_bit)
    values_far = flip(sum_of(values_near, values_come, slice(keep, None)), y_bit)
    near_rows = slice(None, keep)
    grad_keys = low(keys_near[near_rows].astype(F32) + keys_come[near_rows] + keys_far)
    grad_values = low(values_near[near_rows].astype(F32) + values_come[near_rows] + values_far)

    def collect(value):
        total = value[0].astype(F32)
        for i in range(1, rest):
            mask = sum(((i >> j) & 1) << bit for j, bit in enumerate(rest_bits))
            total = total + lax.ppermute(
                value[i], "ctx", [(d, d ^ mask) for d in range(count_ctx)]
            )
        return total.reshape(local_rows, -1)

    grad_kv_own = jnp.concatenate([collect(grad_keys), collect(grad_values)], axis=1)

    grad_query_proj = low(jax.vjp(query_piece, query_proj)[1](grad_queries)[0])
    grad_key_proj = low(jax.vjp(key_piece, key_projected)[1](grad_kv_own[:, :head_dim])[0])
    grad_value_proj = low(jax.vjp(value_piece, value_projected)[1](grad_kv_own[:, head_dim:])[0])
    query_expand_grad = summed(rank_query, grad_query_proj)
    key_expand_grad = summed(rank_key, grad_key_proj)
    value_expand_grad = summed(rank_value, grad_value_proj)
    grad_kv_proj = jnp.concatenate([grad_key_proj, grad_value_proj], axis=1)
    first_part = jnp.concatenate(
        [
            slab_against(grad_query_proj, query_slabs) + slab_against(grad_kv_proj, kv_slabs),
            select * against(grad_query_proj, query_expand),
            select * against(grad_key_proj, key_widen_maps),
            select * against(grad_value_proj, value_widen_maps),
        ],
        axis=1,
    )
    input_own, first_grads = whole_call(
        lambda *refs: last_kernel(*refs, **style),
        (
            moved_back(own_half(first_part), weight_back),
            moved_back(other_core(low(other_half(first_part))), weight_back),
            tokens,
            gains,
            grad_scaled,
            grad_first,
            first_shrink,
        ),
        (wide_f32, jax.ShapeDtypeStruct((3, grad_rows, width), grad_type)),
        scratch=(work_space, work_space, kept_space),
        tables=(half, weight_back_table, own_pick),
        specs={2: half_spec},
    )

    def scatter_split(grads):
        rows = adapter_width // count_ctx
        joined = low(jnp.concatenate(grads, axis=1))
        parts = joined.reshape(count_ctx, rows, joined.shape[1])
        parts = lax.all_to_all(parts, "ctx", 0, 0, tiled=True)
        total = jnp.sum(parts.astype(F32), axis=0)
        cuts, start = [], 0
        for grad in grads:
            cuts.append(total[:, start : start + grad.shape[1]])
            start += grad.shape[1]
        return cuts

    def scatter_team(grads):
        rows = adapter_width // count_ctx
        joined = low(grads).reshape(3, count_ctx, rows, hidden_slice)
        parts = joined.transpose(1, 0, 2, 3).reshape(count_ctx, 3 * rows, hidden_slice)
        parts = lax.all_to_all(parts, "ctx", 0, 0, tiled=True)
        teams = [
            sum(parts[i].astype(F32) for i in range(count_ctx) if (i >> 1) & 3 == t)
            for t in range(4)
        ]
        total = jnp.concatenate(teams, axis=1)
        return [total[i * rows : (i + 1) * rows] for i in range(3)]

    def scatter_shared(grads):
        rows = adapter_width // (2 * count_ctx)
        shaped = grads.reshape(grads.shape[0], count_ctx, 2, rows, width)
        keep = lax.dynamic_index_in_dim(shaped, core, 2, keepdims=False)
        send = lax.dynamic_index_in_dim(shaped, 1 - core, 2, keepdims=False)
        joined = low(keep + other_core(low(send)).astype(F32))
        parts = joined.transpose(1, 0, 2, 3).reshape(count_ctx, grads.shape[0] * rows, width)
        parts = lax.all_to_all(parts, "ctx", 0, 0, tiled=True)
        total = jnp.sum(parts.astype(F32), axis=0)
        return [total[i * rows : (i + 1) * rows] for i in range(grads.shape[0])]

    def one_adapter(grad):
        return low(lax.dynamic_slice_in_dim(grad, own_pick[0] * ADAPTER_RANK, ADAPTER_RANK, 0))

    def core_rows(grads):
        shaped = grads.reshape(grads.shape[0], 2, 2, 4, width)
        keep = lax.dynamic_index_in_dim(shaped, core, 2, keepdims=False).astype(F32)
        send = lax.dynamic_index_in_dim(shaped, 1 - core, 2, keepdims=False)
        return low(keep + other_core(send)).transpose(1, 0, 2, 3).reshape(2, -1, width)

    def deliver(load):
        loads = [load] + [
            lax.ppermute(load, "ctx", [(d, d ^ (4 * r)) for d in range(count_ctx)])
            for r in range(1, count_ctx // 4)
        ]
        picks = [
            jnp.sum(jnp.where(device_ids == (me ^ (4 * r)), pick_of[:, 0], 0))
            for r in range(count_ctx // 4)
        ]
        total = 0.0
        for m in (3, 1, 2, 0):
            place = (me & 3) ^ m
            wanted = (me >> 2) * 2 + (place >> 1)
            sent = sum(
                jnp.where(
                    pick == wanted,
                    lax.dynamic_index_in_dim(each, place & 1, 0, keepdims=False).astype(F32),
                    0.0,
                )
                for pick, each in zip(picks, loads)
            )
            if m:
                sent = lax.ppermute(low(sent), "ctx", [(d, d ^ m) for d in range(count_ctx)])
            total = total + sent.astype(F32)
        return total

    gate_expand_out, up_expand_out, down_shrink_out = scatter_team(team_grads)
    if compact:
        shared = core_rows(jnp.concatenate([own_grads, down_expand_grad[None]], axis=0))
        split = one_adapter(out_shrink_grad).reshape(2, 8, -1)
        split = jnp.pad(split, ((0, 0), (0, 0), (0, width - split.shape[2])))
        found = deliver(jnp.concatenate([shared, split], axis=1))
        gate_shrink_out, up_shrink_out, out_expand_out, down_expand_out = (
            found[4 * i : 4 * i + 4] for i in range(4)
        )
        out_shrink_out = found[16:, : out_shrink_grad.shape[1]]
        expands = [one_adapter(g) for g in (query_expand_grad, key_expand_grad, value_expand_grad)]
        sizes = [g.shape[1] for g in expands]
        split = jnp.concatenate(expands, axis=1).reshape(2, 8, -1)
        split = jnp.pad(split, ((0, 0), (0, 0), (0, width - split.shape[2])))
        found = deliver(jnp.concatenate([core_rows(first_grads), split], axis=1))
        query_shrink_out, key_shrink_out, value_shrink_out = (
            found[4 * i : 4 * i + 4] for i in range(3)
        )
        query_expand_out = found[12:, : sizes[0]]
        key_expand_out = found[12:, sizes[0] : sizes[0] + sizes[1]]
        value_expand_out = found[12:, sizes[0] + sizes[1] : sum(sizes)]
    else:
        (out_shrink_out,) = scatter_split([out_shrink_grad])
        gate_shrink_out, up_shrink_out, out_expand_out, down_expand_out = scatter_shared(
            jnp.concatenate([own_grads, down_expand_grad[None]], axis=0)
        )
        query_expand_out, key_expand_out, value_expand_out = scatter_split(
            [query_expand_grad, key_expand_grad, value_expand_grad]
        )
        query_shrink_out, key_shrink_out, value_shrink_out = scatter_shared(first_grads)

    return (
        both_halves(result_own, other_core(result_own)),
        both_halves(input_own, other_core(input_own)),
        both_halves(layer_input_own, other_core(layer_input_own)),
        query_shrink_out,
        key_shrink_out,
        value_shrink_out,
        gate_shrink_out,
        up_shrink_out,
        out_shrink_out,
        down_shrink_out,
        query_expand_out,
        key_expand_out,
        value_expand_out,
        gate_expand_out,
        up_expand_out,
        out_expand_out,
        down_expand_out,
    )


def solution(mesh):
    in_specs = (
        P("ctx", None),
        P("ctx", None),
        P("ctx", None),
        P(),
        P(),
        P(),
        P(),
        P("ctx", "wt"),
        P("ctx", "wt"),
        P("ctx", "wt"),
        P("ctx", "wt"),
        P("ctx", "wt"),
        P("wt", "ctx"),
        P("wt", "ctx"),
        P(),
        P(),
        P(),
        P(),
        P(),
        P(),
        P(),
        P(),
        P(),
        P(None, "wt"),
        P(None, "wt"),
        P(None, "wt"),
        P(None, "wt"),
        P(None, "wt"),
        P(None, "wt"),
        P(None, "wt"),
        P(),
        P(),
    )
    out_specs = (
        P("ctx", None),
        P("ctx", None),
        P("ctx", None),
        P(("ctx", "wt"), None),
        P(("ctx", "wt"), None),
        P(("ctx", "wt"), None),
        P(("ctx", "wt"), None),
        P(("ctx", "wt"), None),
        P("ctx", "wt"),
        P("ctx", "wt"),
        P("ctx", "wt"),
        P("ctx", "wt"),
        P("ctx", "wt"),
        P("ctx", "wt"),
        P("ctx", "wt"),
        P(("ctx", "wt"), None),
        P(("ctx", "wt"), None),
    )
    return jax.shard_map(local, mesh=mesh, in_specs=in_specs, out_specs=out_specs, check_vma=False)
```

```python
import jax
import jax.numpy as jnp
from jax import lax
from jax.experimental import pallas as pl
from jax.experimental.pallas import tpu as pltpu
from jax.sharding import PartitionSpec as P

QUERY_HEADS = 8
KEY_VALUE_HEADS = 2
ADAPTER_COUNT = 8
ADAPTER_RANK = 16
PROMPT = 2048
CONT = 256

EPS = 1e-06
THETA = 1000000.0
ROOT_HALF = 0.5**0.5
F32 = jnp.float32
BF16 = jnp.bfloat16
SWAP = [(0, 1), (1, 0)]


def normalized(inputs, norm_gain):
    return inputs * lax.rsqrt(jnp.mean(inputs * inputs, axis=-1, keepdims=True) + EPS) * norm_gain


def rotary_applied(inputs, cosine, sine_term):
    half_width = inputs.shape[-1] // 2
    first_half = inputs[..., :half_width]
    second_half = inputs[..., half_width:]
    return jnp.concatenate(
        [
            first_half * cosine - second_half * sine_term,
            second_half * cosine + first_half * sine_term,
        ],
        axis=-1,
    )


def product(left_side, right_side):
    return jnp.dot(left_side, right_side, preferred_element_type=F32)


def against(left_side, right_side):
    return lax.dot_general(
        left_side, right_side, (((1,), (1,)), ((), ())), preferred_element_type=F32
    )


def summed(left_side, right_side):
    return lax.dot_general(
        left_side, right_side, (((0,), (0,)), ((), ())), preferred_element_type=F32
    )


def low(value):
    return value.astype(BF16)


def attend_kernel(count_ref, slot_ref, kslot_ref, vslot_ref, q_ref, kv_ref, o_ref, lse_ref, acc, tot, *, heads, dim):
    group = pl.program_id(0)
    count = count_ref[group]
    rows = q_ref.shape[0]
    fold = tot.shape[-1]
    acc[...] = jnp.zeros_like(acc)
    tot[...] = jnp.zeros_like(tot)

    def step(index, masked):
        keys = kv_ref[slot_ref[group, index], 0, :, :dim]
        values = kv_ref[slot_ref[group, index], 0, :, dim:]
        for head in range(heads):
            lanes = slice(head * dim, (head + 1) * dim)
            scores = against(q_ref[:, lanes], keys)
            weights = jnp.exp(scores)
            if masked:
                row = lax.broadcasted_iota(jnp.int32, scores.shape, 0)
                col = lax.broadcasted_iota(jnp.int32, scores.shape, 1)
                weights = jnp.where(col <= row, weights, 0.0)
            part = weights[:, :fold]
            for start in range(fold, rows, fold):
                part = part + weights[:, start : start + fold]
            tot[head] += part
            acc[:, lanes] += product(low(weights), values)

    def body(index, carry):
        step(index, False)
        return carry

    lax.fori_loop(0, count - 1, body, 0)
    step(count - 1, True)
    lane = lax.broadcasted_iota(jnp.int32, lse_ref.shape, 1)
    lse = jnp.zeros(lse_ref.shape, F32)
    for head in range(heads):
        lanes = slice(head * dim, (head + 1) * dim)
        total = jnp.sum(tot[head], axis=-1, keepdims=True)
        o_ref[:, lanes] = low(acc[:, lanes] / total)
        lse = jnp.where(lane == head, jnp.log(total), lse)
    lse_ref[...] = lse


def attend_back_kernel(
    count_ref, slot_ref, kslot_ref, vslot_ref, q_ref, kv_ref, o_ref, lse_ref, g_ref, dq_ref, dk_near, dk_far, dv_near, dv_far, delta, *, heads, dim
):
    group = pl.program_id(0)
    count = count_ref[group]
    dq_ref[...] = jnp.zeros_like(dq_ref)
    for out_ref in (dk_near, dk_far, dv_near, dv_far):
        out_ref[...] = jnp.zeros_like(out_ref)
    half = dk_near.shape[0]

    def put(near_ref, far_ref, slot, value):
        @pl.when(slot < half)
        def _():
            near_ref[slot, 0] = low(value)

        @pl.when(slot >= half)
        def _():
            far_ref[slot - half, 0] = low(value)

    for head in range(heads):
        lanes = slice(head * dim, (head + 1) * dim)
        delta[head] = jnp.sum(
            o_ref[:, lanes].astype(F32) * g_ref[:, lanes].astype(F32), axis=-1, keepdims=True
        )

    def step(index, masked):
        keys = kv_ref[slot_ref[group, index], 0, :, :dim]
        values = kv_ref[slot_ref[group, index], 0, :, dim:]
        dk = jnp.zeros(keys.shape, F32)
        dv = jnp.zeros(values.shape, F32)
        for head in range(heads):
            lanes = slice(head * dim, (head + 1) * dim)
            queries = q_ref[:, lanes]
            upstream = g_ref[:, lanes]
            scores = against(queries, keys)
            weights = jnp.exp(scores - lse_ref[:, head : head + 1])
            if masked:
                row = lax.broadcasted_iota(jnp.int32, scores.shape, 0)
                col = lax.broadcasted_iota(jnp.int32, scores.shape, 1)
                weights = jnp.where(col <= row, weights, 0.0)
            grad_weights = against(upstream, values)
            grad_scores = low(weights * (grad_weights - delta[head]))
            dq_ref[:, lanes] += product(grad_scores, keys)
            dk += summed(grad_scores, queries)
            dv += summed(low(weights), upstream)
        put(dk_near, dk_far, kslot_ref[group, index], dk)
        put(dv_near, dv_far, vslot_ref[group, index], dv)

    def body(index, carry):
        step(index, False)
        return carry

    lax.fori_loop(0, count - 1, body, 0)
    step(count - 1, True)


def attend(tables, queries, kv_all, groups, heads, dim):
    slots, _, block, _ = kv_all.shape
    rows = queries.shape[0]
    fold = min(128, block)
    whole = pl.BlockSpec((slots, 1, block, 2 * dim), lambda g, *_: (0, g, 0, 0))
    mine = pl.BlockSpec((block, heads * dim), lambda g, *_: (g, 0))
    return pl.pallas_call(
        lambda *refs: attend_kernel(*refs, heads=heads, dim=dim),
        grid_spec=pltpu.PrefetchScalarGridSpec(
            num_scalar_prefetch=4,
            grid=(groups,),
            in_specs=[mine, whole],
            out_specs=[mine, pl.BlockSpec((block, 128), lambda g, *_: (g, 0))],
            scratch_shapes=[
                pltpu.VMEM((block, heads * dim), F32),
                pltpu.VMEM((heads, block, fold), F32),
            ],
        ),
        out_shape=[
            jax.ShapeDtypeStruct((rows, heads * dim), BF16),
            jax.ShapeDtypeStruct((rows, 128), F32),
        ],
        compiler_params=pltpu.CompilerParams(vmem_limit_bytes=40 * 2**20),
        cost_estimate=pl.CostEstimate(
            flops=4 * rows * heads * dim * 2304, bytes_accessed=6 * 2**20, transcendentals=rows * heads * 2304
        ),
    )(*tables, queries, kv_all)


def attend_back(tables, queries, kv_all, heads_low, lse, grads, groups, heads, dim):
    slots, _, block, _ = kv_all.shape
    rows = queries.shape[0]
    whole = pl.BlockSpec((slots, 1, block, 2 * dim), lambda g, *_: (0, g, 0, 0))
    part = pl.BlockSpec((slots // 2, 1, block, dim), lambda g, *_: (0, g, 0, 0))
    mine = pl.BlockSpec((block, heads * dim), lambda g, *_: (g, 0))
    return pl.pallas_call(
        lambda *refs: attend_back_kernel(*refs, heads=heads, dim=dim),
        grid_spec=pltpu.PrefetchScalarGridSpec(
            num_scalar_prefetch=4,
            grid=(groups,),
            in_specs=[mine, whole, mine, pl.BlockSpec((block, 128), lambda g, *_: (g, 0)), mine],
            out_specs=[mine] + [part] * 4,
            scratch_shapes=[pltpu.VMEM((heads, block, 1), F32)],
        ),
        out_shape=[
            jax.ShapeDtypeStruct((rows, heads * dim), F32),
        ]
        + [jax.ShapeDtypeStruct((slots // 2, groups, block, dim), BF16)] * 4,
        compiler_params=pltpu.CompilerParams(vmem_limit_bytes=48 * 2**20),
        cost_estimate=pl.CostEstimate(
            flops=10 * rows * heads * dim * 2304, bytes_accessed=12 * 2**20, transcendentals=rows * heads * 2304
        ),
    )(*tables, queries, kv_all, heads_low, lse, grads)


def gelu_parts(gate):
    slope = 0.7978845608028654
    square = gate * gate
    bend = jnp.tanh(slope * gate * (1.0 + 0.044715 * square))
    half = 0.5 * (1.0 + bend)
    grad = half + 0.5 * gate * (1.0 - bend * bend) * slope * (1.0 + 0.134145 * square)
    return gate * half, grad


def rms_scale(value):
    return lax.rsqrt(jnp.mean(value * value, axis=-1, keepdims=True) + EPS)


def rms_pull(value, scale, weighted):
    return scale * weighted - value * (
        scale * scale * scale * jnp.mean(value * weighted, axis=-1, keepdims=True)
    )


def move_columns(out_ref, in_ref, table_ref, count, block):
    for j in range(count):
        start = pl.multiple_of(table_ref[j] * block, block)
        out_ref[:, j * block : (j + 1) * block] = in_ref[:, pl.ds(start, block)].astype(
            out_ref.dtype
        )


def whole_call(kernel, inputs, outputs, scratch=(), tables=(), specs=None, flops=10**9):
    specs = specs or {}

    def full(array):
        return pl.BlockSpec(array.shape, lambda *_: (0,) * len(array.shape))

    in_specs = [specs.get(i, full(array)) for i, array in enumerate(inputs)]
    size = sum(a.size * a.dtype.itemsize for a in inputs)
    return pl.pallas_call(
        kernel,
        grid_spec=pltpu.PrefetchScalarGridSpec(
            num_scalar_prefetch=len(tables),
            grid=(1,),
            in_specs=in_specs,
            out_specs=[full(array) for array in outputs],
            scratch_shapes=list(scratch),
        ),
        out_shape=list(outputs),
        compiler_params=pltpu.CompilerParams(vmem_limit_bytes=56 * 2**20),
        cost_estimate=pl.CostEstimate(flops=flops, bytes_accessed=size, transcendentals=0),
    )(*tables, *inputs)


def first_kernel(tokens_ref, gains_ref, select_ref, shrink_ref, low_ref, rank_ref):
    tokens = tokens_ref[...].astype(F32)
    first = low(tokens * rms_scale(tokens) * gains_ref[0:1, :])
    low_ref[...] = first
    ranks = against(first, shrink_ref[...])
    select = select_ref[...]
    width = select.shape[1]
    for i in range(3):
        rank_ref[:, i * width : (i + 1) * width] = low(select * ranks[:, i * width : (i + 1) * width])


def middle_kernel(
    half_ref, back_ref, own_ref, other_ref, tokens_ref, gains_ref, expand_ref, left_ref, right_ref,
    total_ref, laurel_ref, mid_ref, second_ref, rank_ref, work, *, count, block, aligned
):
    width = total_ref.shape[1]
    summed_all = own_ref[...] + other_ref[...].astype(F32)
    rank = low(summed_all[:, width:])
    rank_ref[...] = rank
    if aligned:
        work[...] = summed_all[:, :width]
        move_columns(total_ref, work, back_ref, count, block)
        attn = total_ref[...] + product(rank, expand_ref[...])
    else:
        attn = summed_all[:, :width] + product(rank, expand_ref[...])
    total_ref[...] = attn
    tokens = tokens_ref[...].astype(F32)
    first = tokens * rms_scale(tokens) * gains_ref[0:1, :]
    laurel = product(low(product(low(first), left_ref[...])), right_ref[...])
    laurel_ref[...] = laurel
    mid = (
        tokens
        + attn * rms_scale(attn) * gains_ref[1:2, :]
        + first
        + laurel * rms_scale(laurel) * gains_ref[2:3, :]
    ) * ROOT_HALF
    mid_ref[...] = mid
    second_ref[...] = low(mid * rms_scale(mid) * gains_ref[3:4, :])


def keep_rows(out_ref, work_ref, value, pick_ref):
    if out_ref.shape[0] == value.shape[0]:
        out_ref[...] = value.astype(out_ref.dtype)
    else:
        work_ref[...] = value
        rows = out_ref.shape[0]
        start = pl.multiple_of(pick_ref[0] * rows, rows)
        out_ref[...] = work_ref[pl.ds(start, rows), :].astype(out_ref.dtype)


def layer_kernel(
    half_ref, pick_ref, near_ref, y_ref, z_ref, yz_ref, mid_ref, gains_ref, expand_ref, gate_ref, lift_ref, layer_ref, up_ref,
    result_ref, layer_grad_ref, after_ref, grad_ref, expand_grad_ref, kept
):
    width = mid_ref.shape[1]
    joined = near_ref[...].astype(F32) + y_ref[...] + z_ref[...] + yz_ref[...]
    rank = low(joined[:, width:])
    total = joined[:, :width] + product(rank, expand_ref[...])
    scale = rms_scale(total)
    gain = gains_ref[4:5, :]
    after = mid_ref[...] + total * scale * gain
    layer_pre = product(low(after), gate_ref[...])
    layer_in = layer_ref[...].astype(F32)
    act, slope = gelu_parts(layer_pre)
    back = product(low(act * layer_in), lift_ref[...])
    back_scale = rms_scale(back)
    last_gain = gains_ref[5:6, :]
    result_ref[...] = low(after + back * back_scale * last_gain)
    upstream = up_ref[...].astype(F32)
    grad_back = low(rms_pull(back, back_scale, upstream * last_gain))
    grad_gated = against(grad_back, lift_ref[...])
    layer_grad_ref[...] = grad_gated * act
    grad_pre = low(grad_gated * layer_in * slope)
    grad_after = upstream + against(grad_pre, gate_ref[...])
    after_ref[...] = grad_after
    grad_ffn = low(rms_pull(total, scale, grad_after * gain))
    grad_ref[...] = grad_ffn
    keep_rows(expand_grad_ref, kept, summed(rank, grad_ffn), pick_ref)


def turn_kernel(
    order_ref, pick_ref, near_ref, y_ref, z_ref, yz_ref, mid_ref, after_ref, total_ref, laurel_ref, second_ref, gains_ref, gate_ref, up_ref,
    right_ref, left_ref, expand_ref, rank_ref, select_ref,
    sent_ref, scaled_ref, first_ref, grads_ref, work, kept, *, count, block, aligned
):
    width = mid_ref.shape[1]
    ranks = select_ref.shape[1]
    joined = near_ref[...].astype(F32) + y_ref[...] + z_ref[...] + yz_ref[...]
    rank_gate = low(joined[:, width : width + ranks])
    rank_up = low(joined[:, width + ranks :])
    grad_second = joined[:, :width]
    grad_second = grad_second + product(rank_gate, gate_ref[...]) + product(rank_up, up_ref[...])
    keep_rows(grads_ref.at[0], kept, summed(rank_gate, second_ref[...]), pick_ref)
    keep_rows(grads_ref.at[1], kept, summed(rank_up, second_ref[...]), pick_ref)
    mid = mid_ref[...]
    grad_mid = after_ref[...] + rms_pull(mid, rms_scale(mid), grad_second * gains_ref[3:4, :])
    scaled = grad_mid * ROOT_HALF
    scaled_ref[...] = scaled
    attn = total_ref[...]
    grad_attn = rms_pull(attn, rms_scale(attn), scaled * gains_ref[1:2, :])
    laurel = laurel_ref[...]
    grad_laurel = low(rms_pull(laurel, rms_scale(laurel), scaled * gains_ref[2:3, :]))
    grad_rank = low(against(grad_laurel, right_ref[...]))
    first_ref[...] = scaled + against(grad_rank, left_ref[...])
    attn_low = low(grad_attn)
    keep_rows(grads_ref.at[2], kept, summed(rank_ref[...], attn_low), pick_ref)
    sent_ref[:, width:] = low(select_ref[...] * against(attn_low, expand_ref[...]))
    if aligned:
        work[...] = grad_attn
        for j in range(count):
            start = pl.multiple_of(order_ref[j] * block, block)
            sent_ref[:, j * block : (j + 1) * block] = low(work[:, pl.ds(start, block)])
    else:
        sent_ref[:, :width] = attn_low


def last_kernel(
    half_ref, pick_ref, own_ref, other_ref, tokens_ref, gains_ref, scaled_ref, first_ref, shrink_ref,
    input_ref, grads_ref, kept
):
    width = scaled_ref.shape[1]
    joined = own_ref[...] + other_ref[...].astype(F32)
    ranks = low(joined[:, width:])
    each = ranks.shape[1] // 3
    grad_first = joined[:, :width]
    grad_first = grad_first + first_ref[...] + product(ranks, shrink_ref[...])
    tokens = tokens_ref[...].astype(F32)
    scale = rms_scale(tokens)
    gain = gains_ref[0:1, :]
    input_ref[...] = scaled_ref[...] + rms_pull(tokens, scale, grad_first * gain)
    first = low(tokens * scale * gain)
    for i in range(3):
        keep_rows(
            grads_ref.at[i], kept, summed(ranks[:, i * each : (i + 1) * each], first), pick_ref
        )


def gather_parts(out_ref, parts, table_ref, count, width):
    height = parts[0].shape[0]
    block = width // count
    for i, part in enumerate(parts):
        rows = slice(i * height, (i + 1) * height)
        if block % 128 == 0:
            for j in range(count):
                start = pl.multiple_of(table_ref[j] * block, block)
                out_ref[rows, j * block : (j + 1) * block] = part[:, pl.ds(start, block)]
        else:
            out_ref[rows, :] = part[...]


def ranks_of(out_ref, parts, select_ref, maps_ref):
    height = parts[0].shape[0]
    ranks = select_ref.shape[1]
    for i, part in enumerate(parts):
        rows = slice(i * height, (i + 1) * height)
        found = against(part[...], maps_ref[...])
        for start in range(0, out_ref.shape[1], ranks):
            out_ref[rows, start : start + ranks] = low(
                select_ref[rows, :] * found[:, start : start + ranks]
            )


def bring(pieces, space, sems):
    rows = pieces[0].shape[0]
    copies = [
        pltpu.make_async_copy(piece, space.at[pl.ds(i * rows, rows), :], sems.at[i])
        for i, piece in enumerate(pieces)
    ]
    for copy in copies:
        copy.start()
    return copies


def put_columns(out_ref, value, start, table_ref, block):
    size = value.shape[1]
    if block % 128:
        out_ref[:, pl.ds(start, size)] = value.astype(out_ref.dtype)
        return
    for i in range(size // block):
        place = pl.multiple_of(table_ref[start // block + i] * block, block)
        out_ref[:, pl.ds(place, block)] = value[:, i * block : (i + 1) * block].astype(out_ref.dtype)


def feed_kernel(order_ref, *refs, pieces, width, count):
    parts, (select_ref, shrink_ref, gexp_ref, uexp_ref, dshr_ref), refs = refs[:4], refs[4:9], refs[9:]
    gates, ups, downs = refs[:pieces], refs[pieces : 2 * pieces], refs[2 * pieces : 3 * pieces]
    rank_ref, act_ref, slope_ref, hid_ref, part_ref, x_ref, gate_w, up_w, down_w, sems = refs[3 * pieces :]
    arriving = bring(gates, gate_w, sems.at[0]) + bring(ups, up_w, sems.at[1])
    arriving_down = bring(downs, down_w, sems.at[2])
    ranks = select_ref.shape[1]
    hidden_width = gate_w.shape[1]
    chunk = min(1024, hidden_width)
    gather_parts(x_ref, parts, order_ref, count, width)
    ranks_of(rank_ref, parts, select_ref, shrink_ref)
    for copy in arriving:
        copy.wait()

    @pl.loop(0, hidden_width // chunk)
    def _(i):
        lanes = pl.ds(pl.multiple_of(i * chunk, chunk), chunk)
        gate = product(x_ref[...], gate_w[:, lanes]) + product(rank_ref[:, :ranks], gexp_ref[:, lanes])
        up = product(x_ref[...], up_w[:, lanes]) + product(rank_ref[:, ranks:], uexp_ref[:, lanes])
        act, slope = gelu_parts(gate)
        act_ref[:, lanes] = low(act)
        slope_ref[:, lanes] = low(slope * up)
        hid_ref[:, lanes] = low(act * up)

    for copy in arriving_down:
        copy.wait()
    step = 1024

    @pl.loop(0, width // step)
    def _(i):
        start = pl.multiple_of(i * step, step)
        put_columns(
            part_ref, against(hid_ref[...], down_w[pl.ds(start, step), :]), start, order_ref, width // count
        )

    part_ref[:, width:] = (select_ref[...] * against(hid_ref[...], dshr_ref[...])).astype(part_ref.dtype)


def feed_call(kernel, order, parts, inputs, weights, outputs, scratch, flops):
    def full(array):
        return pl.BlockSpec(array.shape, lambda *_: (0,) * len(array.shape))

    pieces = [piece for matrix in weights for piece in matrix]
    matrix = pltpu.VMEM((len(weights[0]) * weights[0][0].shape[0], weights[0][0].shape[1]), BF16)
    width = parts[0].shape[1]
    return pl.pallas_call(
        lambda *refs: kernel(*refs, pieces=len(weights[0]), width=width, count=order.shape[0]),
        grid_spec=pltpu.PrefetchScalarGridSpec(
            num_scalar_prefetch=1,
            grid=(1,),
            in_specs=[full(array) for array in (*parts, *inputs)]
            + [pl.BlockSpec(memory_space=pl.ANY)] * len(pieces),
            out_specs=[full(array) for array in outputs],
            scratch_shapes=list(scratch)
            + [matrix, matrix, matrix, pltpu.SemaphoreType.DMA((3, len(weights[0])))],
        ),
        out_shape=list(outputs),
        compiler_params=pltpu.CompilerParams(vmem_limit_bytes=58 * 2**20),
        cost_estimate=pl.CostEstimate(flops=flops, bytes_accessed=20 * 2**20, transcendentals=0),
    )(order, *parts, *inputs, *pieces)


def feed(order, parts, select, shrink, gexp, uexp, dshr, gates, ups, downs, out_dtype):
    rows, width = 4 * parts[0].shape[0], parts[0].shape[1]
    hidden, ranks = gexp.shape[1], select.shape[1]
    low_hidden = jax.ShapeDtypeStruct((rows, hidden), BF16)
    return feed_call(
        feed_kernel,
        order,
        parts,
        (select, shrink, gexp, uexp, dshr),
        (gates, ups, downs),
        (
            jax.ShapeDtypeStruct((rows, 2 * ranks), BF16),
            low_hidden,
            low_hidden,
            low_hidden,
            jax.ShapeDtypeStruct((rows, width + ranks), out_dtype),
        ),
        (pltpu.VMEM((rows, width), BF16),),
        6 * rows * width * hidden,
    )


def feed_back_kernel(order_ref, *refs, pieces, width, count):
    parts, refs = refs[:4], refs[4:]
    (
        select_ref,
        dexp_ref,
        rank_ref,
        start_ref,
        act_ref,
        slope_ref,
        hid_ref,
        gexp_ref,
        uexp_ref,
        dshr_ref,
    ), refs = refs[:10], refs[10:]
    gates, ups, downs = refs[:pieces], refs[pieces : 2 * pieces], refs[2 * pieces : 3 * pieces]
    part_ref, grads_ref, g_ref, down_rank, gate_grad, up_grad, gate_w, up_w, down_w, sems = refs[3 * pieces :]
    arriving = bring(downs, down_w, sems.at[2])
    arriving_next = bring(gates, gate_w, sems.at[0]) + bring(ups, up_w, sems.at[1])
    ranks = select_ref.shape[1]
    hidden_width = gate_w.shape[1]
    chunk = min(1024, hidden_width)
    gather_parts(g_ref, parts, order_ref, count, width)
    ranks_of(down_rank, parts, select_ref, dexp_ref)
    for copy in arriving:
        copy.wait()

    @pl.loop(0, hidden_width // chunk)
    def _(i):
        lanes = pl.ds(pl.multiple_of(i * chunk, chunk), chunk)
        grad_hidden = product(g_ref[...], down_w[:, lanes]) + product(down_rank[...], dshr_ref[:, lanes])
        grad_gate = low(grad_hidden * slope_ref[:, lanes].astype(F32))
        grad_up = low(grad_hidden * act_ref[:, lanes].astype(F32))
        gate_grad[:, lanes] = grad_gate
        up_grad[:, lanes] = grad_up
        grads_ref[0, :, lanes] = start_ref[0, :, lanes] + summed(rank_ref[:, :ranks], grad_gate)
        grads_ref[1, :, lanes] = start_ref[1, :, lanes] + summed(rank_ref[:, ranks:], grad_up)
        grads_ref[2, :, lanes] = start_ref[2, :, lanes] + summed(down_rank[...], hid_ref[:, lanes])

    for copy in arriving_next:
        copy.wait()
    step = 1024

    @pl.loop(0, width // step)
    def _(i):
        start = pl.multiple_of(i * step, step)
        found = against(gate_grad[...], gate_w[pl.ds(start, step), :]) + against(
            up_grad[...], up_w[pl.ds(start, step), :]
        )
        put_columns(part_ref, found, start, order_ref, width // count)

    select = select_ref[...]
    part_ref[:, width : width + ranks] = (select * against(gate_grad[...], gexp_ref[...])).astype(part_ref.dtype)
    part_ref[:, width + ranks :] = (select * against(up_grad[...], uexp_ref[...])).astype(part_ref.dtype)


def feed_back(order, parts, select, dexp, start, kept, gexp, uexp, dshr, gates, ups, downs, out_dtype):
    rows, width = 4 * parts[0].shape[0], parts[0].shape[1]
    hidden, ranks = gexp.shape[1], select.shape[1]
    low_hidden = pltpu.VMEM((rows, hidden), BF16)
    return feed_call(
        feed_back_kernel,
        order,
        parts,
        (select, dexp, kept[0], start, *kept[1:], gexp, uexp, dshr),
        (gates, ups, downs),
        (
            jax.ShapeDtypeStruct((rows, width + 2 * ranks), out_dtype),
            jax.ShapeDtypeStruct((3, ranks, hidden), F32),
        ),
        (pltpu.VMEM((rows, width), BF16), pltpu.VMEM((rows, ranks), BF16), low_hidden, low_hidden),
        6 * rows * width * hidden,
    )


def local(
    tokens,
    layer_input,
    out_grad,
    block_device,
    adapter_pick,
    norm_gains,
    head_norm_gains,
    query_weight,
    key_matrix,
    value_matrix,
    gate_weight,
    up_weight,
    out_weight,
    down_weight,
    laurel_left,
    laurel_right,
    layer_gate,
    layer_lift,
    query_shrink,
    key_shrink,
    value_shrink,
    gate_shrink,
    up_shrink,
    out_shrink,
    down_shrink,
    query_expand,
    key_widen_maps,
    value_widen_maps,
    gate_expand,
    up_expand,
    out_expand,
    down_expand,
):
    count_ctx = lax.axis_size("ctx")
    bit_count = count_ctx.bit_length() - 1
    groups = block_device.shape[0]
    local_rows, width = tokens.shape
    block_len = local_rows // groups
    half_rows = local_rows // 2
    head_dim = head_norm_gains.shape[1]
    heads_local = query_weight.shape[1] // head_dim
    adapter_width = ADAPTER_COUNT * ADAPTER_RANK
    model_block = width // count_ctx
    hidden_slice = gate_weight.shape[1] // 4
    me = lax.axis_index("ctx")
    core = lax.axis_index("wt")

    spread_bits = list(range(3, bit_count)) + [0]
    team_place = (me >> 1) & 3

    def flip(value, bit):
        return lax.ppermute(value, "ctx", [(i, i ^ (1 << bit)) for i in range(count_ctx)])

    def other_core(value):
        return lax.ppermute(value, "wt", SWAP)

    def own_half(value):
        return lax.dynamic_slice_in_dim(value, core * half_rows, half_rows, 0)

    def other_half(value):
        return lax.dynamic_slice_in_dim(value, (1 - core) * half_rows, half_rows, 0)

    def both_halves(own, other):
        return jnp.where(
            core == 0, jnp.concatenate([own, other], axis=0), jnp.concatenate([other, own], axis=0)
        )

    def column_blocks(value, places):
        return jnp.concatenate(
            [
                lax.dynamic_slice_in_dim(value, place * model_block, model_block, 1)
                for place in places
            ],
            axis=1,
        )

    rest = count_ctx // 4
    rest_bits = list(range(2, bit_count))

    def rest_place(apart):
        return sum(((apart >> bit) & 1) << i for i, bit in enumerate(rest_bits))

    weight_order = [
        me
        ^ (
            (j // (2 * rest)) * 2
            + (j // rest) % 2
            + sum(((j >> i) & 1) << bit for i, bit in enumerate(rest_bits))
        )
        for j in range(count_ctx)
    ]
    weight_back = [
        (((d ^ me) >> 1) & 1) * 2 * rest + ((d ^ me) & 1) * rest + rest_place(d ^ me)
        for d in range(count_ctx)
    ]
    piece_masks = [0]
    for bit in spread_bits:
        piece_masks = piece_masks + [mask | (1 << bit) for mask in piece_masks]
    team_order = [me ^ mask ^ (2 * t) for mask in piece_masks for t in range(4)]
    team_back = [
        4 * sum((((b ^ me) >> bit) & 1) << i for i, bit in enumerate(spread_bits))
        + (((b ^ me) >> 1) & 3)
        for b in range(count_ctx)
    ]

    def to_member(value, member):
        if member == 0:
            return value
        return lax.ppermute(value, "ctx", [(d, d ^ (2 * member)) for d in range(count_ctx)])

    def team_split(shard):
        parts = [
            to_member(
                lax.dynamic_slice_in_dim(
                    shard, (team_place ^ member) * hidden_slice, hidden_slice, 1
                ),
                member,
            )
            for member in range(4)
        ]
        return joined(parts[0], parts[1]), joined(parts[2], parts[3])

    def joined(own, arrived):
        return jnp.concatenate([own, arrived], axis=0)

    prompt_blocks = PROMPT // block_len
    cont_blocks = CONT // block_len
    device_ids = jnp.arange(count_ctx, dtype=jnp.int32)
    block_of = jnp.sum(
        jnp.where(block_device[None] == device_ids[:, None, None], device_ids[None, None, :], 0),
        axis=2,
    )
    cont_of = (block_of - prompt_blocks) // cont_blocks
    pick_of = jnp.sum(
        jnp.where(
            cont_of[:, :, None] == jnp.arange(adapter_pick.shape[1], dtype=jnp.int32),
            adapter_pick[None],
            0,
        ),
        axis=2,
    )
    pick_of = jnp.where(block_of < prompt_blocks, -1, pick_of)
    compact = groups == 1 and count_ctx * 8 == adapter_width
    own_pick = jnp.maximum(jnp.sum(jnp.where(device_ids[:, None] == me, pick_of, 0), axis=0), 0)
    own_pick = own_pick[:1].astype(jnp.int32)
    grad_rows = ADAPTER_RANK if compact else adapter_width
    grad_type = BF16 if compact else F32

    def picks_at(device):
        return jnp.sum(jnp.where(device_ids[:, None] == device, pick_of, 0), axis=0)

    def select_rows(picks):
        rows = jnp.repeat(picks, block_len)
        return (
            jnp.arange(adapter_width, dtype=jnp.int32)[None, :] // ADAPTER_RANK == rows[:, None]
        ).astype(F32)

    select = select_rows(picks_at(me))
    select_own = own_half(select)
    team_select = [select_rows(picks_at(me ^ (2 * t))) for t in range(4)]
    select_near = jnp.concatenate([own_half(part) for part in team_select], axis=0)
    select_far = jnp.concatenate([other_half(part) for part in team_select], axis=0)

    my_block = jnp.sum(jnp.where(device_ids[:, None] == me, block_of, 0), axis=0)
    positions = (
        my_block[:, None] * block_len + jnp.arange(block_len, dtype=jnp.int32)[None, :]
    ).reshape(-1)
    seq_pos = jnp.where(positions < PROMPT, positions, PROMPT + (positions - PROMPT) % CONT)
    frequency = THETA ** (-2.0 * jnp.arange(head_dim // 2, dtype=F32) / head_dim)
    rotary_angles = seq_pos.astype(F32)[:, None] * frequency[None, :]
    cosine = jnp.cos(rotary_angles)[:, None, :]
    sine_term = jnp.sin(rotary_angles)[:, None, :]
    cont_start = prompt_blocks + (my_block - prompt_blocks) // cont_blocks * cont_blocks
    is_prompt = my_block < prompt_blocks
    visible_count = jnp.where(
        is_prompt, my_block + 1, prompt_blocks + my_block - cont_start + 1
    ).astype(jnp.int32)
    entries = jnp.arange(prompt_blocks + cont_blocks, dtype=jnp.int32)
    visible_block = jnp.where(
        is_prompt[:, None] | (entries < prompt_blocks)[None, :],
        entries[None, :],
        cont_start[:, None] + entries[None, :] - prompt_blocks,
    )
    visible_device = jnp.sum(
        jnp.where(
            visible_block[:, :, None] == device_ids[None, None, :], block_device[:, None, :], 0
        ),
        axis=2,
    )
    apart = visible_device ^ me
    key_slot = (((apart >> 1) & 1) * 2 + (apart & 1)) * rest + rest_place(apart)
    value_slot = ((apart & 1) * 2 + ((apart >> 1) & 1)) * rest + rest_place(apart)
    tables = tuple(
        table.astype(jnp.int32) for table in (visible_count, visible_device, key_slot, value_slot)
    )

    gains = norm_gains.astype(F32)
    query_gain = head_norm_gains[0].astype(F32)
    key_gain = head_norm_gains[1].astype(F32)

    def query_piece(projected):
        return (
            rotary_applied(
                normalized(projected.reshape(local_rows, -1, head_dim), query_gain),
                cosine,
                sine_term,
            )
            * head_dim ** (-0.5)
        ).reshape(local_rows, -1)

    def key_piece(projected):
        return rotary_applied(
            normalized(projected.reshape(local_rows, -1, head_dim), key_gain), cosine, sine_term
        ).reshape(local_rows, -1)

    def value_piece(projected):
        return normalized(projected.reshape(local_rows, -1, head_dim), 1.0).reshape(local_rows, -1)

    def slab_product(value, slabs):
        middle = value.shape[1] // 2
        return product(value[:, :middle], slabs[0]) + product(value[:, middle:], slabs[1])

    def slab_against(value, slabs):
        return jnp.concatenate([against(value, slabs[0]), against(value, slabs[1])], axis=1)

    half = jnp.reshape(core, (1,)).astype(jnp.int32)
    aligned = model_block % 128 == 0
    style = dict(count=count_ctx, block=model_block, aligned=aligned)
    weight_order_table = jnp.stack(weight_order).astype(jnp.int32)
    weight_back_table = jnp.stack(weight_back).astype(jnp.int32)
    team_order_table = jnp.stack(team_order).astype(jnp.int32)
    half_spec = pl.BlockSpec((half_rows, width), lambda i, half, *_: (half[0], 0))
    wide_f32 = jax.ShapeDtypeStruct((half_rows, width), F32)
    wide_low = jax.ShapeDtypeStruct((half_rows, width), BF16)
    work_space = pltpu.VMEM((half_rows, width), F32)
    kept_space = pltpu.VMEM((adapter_width, width), F32)

    def moved(value, places):
        return value if aligned else column_blocks(value, places)

    def moved_back(value, places):
        if aligned:
            return value
        flat = value.reshape(-1, value.shape[-1])
        flat = jnp.concatenate([column_blocks(flat[:, :width], places), flat[:, width:]], axis=1)
        return flat.reshape(value.shape)

    first_shrink = jnp.concatenate([query_shrink, key_shrink, value_shrink], axis=0)
    first_low, rank_first = whole_call(
        first_kernel,
        (tokens, gains, select, first_shrink),
        (
            jax.ShapeDtypeStruct(tokens.shape, BF16),
            jax.ShapeDtypeStruct((local_rows, 3 * adapter_width), BF16),
        ),
    )
    rank_query = rank_first[:, :adapter_width]
    rank_key = rank_first[:, adapter_width : 2 * adapter_width]
    rank_value = rank_first[:, 2 * adapter_width :]

    far_bits, near_bit = spread_bits[:-1], spread_bits[-1]
    x_bit, y_bit = 0, 1
    first_bit = rest_bits[0]
    sent_before = {}

    def queued(line, value, move, depth=2):
        earlier = sent_before.setdefault(line, [])
        if len(earlier) >= depth:
            value = lax.optimization_barrier((value, earlier[-depth]))[0]
        result = move(value)
        earlier.append(result)
        return result

    def over_x(value):
        return queued("x", value, lambda v: flip(v, x_bit))

    def over_y(value):
        return queued("y", value, lambda v: flip(v, y_bit))

    def over_rest(value, bits):
        for bit in bits:
            value = joined(value, queued("z", value, lambda v, bit=bit: flip(v, bit)))
        return value

    def spread_far(piece):
        pieces = [piece]
        for bit in far_bits:
            pieces = pieces + [queued("z", other, lambda v, bit=bit: flip(v, bit)) for other in pieces]
        return pieces[1:]

    def near(pieces):
        return [over_x(piece) for piece in pieces]

    step = lax.optimization_barrier
    head_maps = lax.all_gather(
        jnp.concatenate([query_weight, key_matrix, value_matrix], axis=1), "ctx", axis=0, tiled=True
    )
    out_rows = out_weight.T
    gate_a, gate_b = team_split(gate_weight)
    up_a, up_b = team_split(up_weight)
    gate_far_a = spread_far(gate_a)
    gate_far_b = spread_far(gate_b)
    gate_near_a, gate_near_b = near([gate_a]), near([gate_b])
    up_far_a = spread_far(up_a)
    up_near_a, up_near_b = near([up_a]), near([up_b])
    gate_far_near_a = near(gate_far_a)
    head_maps, gate_far_a, gate_far_b, gate_near_a, gate_near_b, up_far_a, up_near_a, up_near_b, gate_far_near_a = step(
        (head_maps, gate_far_a, gate_far_b, gate_near_a, gate_near_b, up_far_a, up_near_a, up_near_b, gate_far_near_a)
    )
    query_width, kv_width = query_weight.shape[1], key_matrix.shape[1]
    query_maps, kv_maps = head_maps[:, :query_width], head_maps[:, query_width:]
    kv_projected = product(first_low, kv_maps)
    key_projected = kv_projected[:, :kv_width] + product(rank_key, key_widen_maps)
    value_projected = kv_projected[:, kv_width:] + product(rank_value, value_widen_maps)
    kv_low = jnp.concatenate([low(key_piece(key_projected)), low(value_piece(value_projected))], axis=1)
    kv_all = lax.all_gather(kv_low, "ctx", axis=0, tiled=True).reshape(
        count_ctx, groups, block_len, 2 * head_dim
    )
    query_proj = product(first_low, query_maps) + product(rank_query, query_expand)
    query_low = low(query_piece(query_proj))
    down_a, down_b = team_split(down_weight.T)
    up_far_b = spread_far(up_b)
    out_part = joined(out_rows, flip(out_rows, first_bit))
    out_part = over_rest(out_part, rest_bits[1:])
    out_slab = joined(out_part, over_x(out_part))
    out_slabs = out_slab, over_y(out_slab)
    gate_far_near_b = near(gate_far_b)
    up_far_near_a = near(up_far_a)
    down_far_a, down_far_b = spread_far(down_a), spread_far(down_b)
    down_near_a, down_near_b = near([down_a]), near([down_b])
    up_far_near_b = near(up_far_b)
    kv_all, down_far_a, up_far_near_a, up_far_b, out_slab, gate_far_near_b, down_near_a = step(
        (kv_all, down_far_a, up_far_near_a, up_far_b, out_slab, gate_far_near_b, down_near_a)
    )
    out_slabs = out_slab, out_slabs[1]
    down_far_near_a = near(down_far_a)
    heads_low, lse = attend(tables, query_low, kv_all, groups, heads_local, head_dim)

    heads_low, out_slabs, down_far_b, up_far_near_b, down_near_b = step(
        (heads_low, out_slabs, down_far_b, up_far_near_b, down_near_b)
    )
    down_far_near_b = near(down_far_b)
    attn_part = jnp.concatenate(
        [slab_against(heads_low, out_slabs), select * against(heads_low, out_shrink)], axis=1
    )
    attn_total, laurel_back, mid_stream, second_low, rank_out = whole_call(
        lambda *refs: middle_kernel(*refs, **style),
        (
            moved_back(own_half(attn_part), weight_back),
            moved_back(other_core(other_half(attn_part)), weight_back),
            tokens,
            gains,
            out_expand,
            laurel_left,
            laurel_right,
        ),
        (
            wide_f32,
            wide_f32,
            wide_f32,
            wide_low,
            jax.ShapeDtypeStruct((half_rows, adapter_width), BF16),
        ),
        scratch=(work_space,),
        tables=(half, weight_back_table),
        specs={2: half_spec},
    )

    def in_order(own, far, near_own, near_far):
        first, second = ([o] + f + n + nf for o, f, n, nf in zip(own, far, near_own, near_far))
        return [piece for pair in zip(first, second) for piece in pair]

    gate_pieces = in_order(
        (gate_a, gate_b),
        (gate_far_a, gate_far_b),
        (gate_near_a, gate_near_b),
        (gate_far_near_a, gate_far_near_b),
    )
    up_pieces = in_order(
        (up_a, up_b), (up_far_a, up_far_b), (up_near_a, up_near_b), (up_far_near_a, up_far_near_b)
    )
    down_pieces = in_order(
        (down_a, down_b),
        (down_far_a, down_far_b),
        (down_near_a, down_near_b),
        (down_far_near_a, down_far_near_b),
    )

    def team_gather(value):
        near_parts = [to_member(value, member) for member in range(4)]
        return near_parts, [other_core(part) for part in near_parts]

    def team_sum(near_part, far_part):
        arrived = other_core(far_part).astype(F32)
        parts = []
        for member in (3, 1, 2, 0):
            rows = slice(member * half_rows, (member + 1) * half_rows)
            parts.append(to_member(low(near_part[rows].astype(F32) + arrived[rows]), member))
        return parts

    def hidden_columns(value):
        return lax.dynamic_slice_in_dim(value, team_place * hidden_slice, hidden_slice, 1)

    feed_maps = moved(jnp.concatenate([gate_shrink, up_shrink], axis=0), team_order)
    down_map = moved(down_expand, team_order)
    slices = tuple(hidden_columns(value) for value in (gate_expand, up_expand, down_shrink))
    pieces = (gate_pieces, up_pieces, down_pieces)

    second_near, second_far = team_gather(moved(second_low, team_order))
    *kept_far, part_far = feed(
        team_order_table, second_far, select_far, feed_maps, *slices, *pieces, BF16
    )
    *kept_near, part_near = feed(
        team_order_table, second_near, select_near, feed_maps, *slices, *pieces, BF16
    )
    ffn_parts = team_sum(part_near, part_far)

    result_own, layer_input_own, grad_after, grad_ffn, down_expand_grad = whole_call(
        layer_kernel,
        (
            *(moved_back(part, team_back) for part in ffn_parts),
            mid_stream,
            gains,
            down_expand,
            layer_gate,
            layer_lift,
            layer_input,
            out_grad,
        ),
        (
            wide_low,
            jax.ShapeDtypeStruct((half_rows, layer_input.shape[1]), F32),
            wide_f32,
            wide_low,
            jax.ShapeDtypeStruct((grad_rows, width), grad_type),
        ),
        scratch=(kept_space,),
        tables=(half, own_pick),
        specs={
            9: pl.BlockSpec((half_rows, layer_input.shape[1]), lambda i, half, *_: (half[0], 0)),
            10: half_spec,
        },
    )

    grad_near, grad_far = team_gather(moved(grad_ffn, team_order))
    nothing = jnp.zeros((3, adapter_width, hidden_slice), F32)
    back_far, team_grads = feed_back(
        team_order_table, grad_far, select_far, down_map, nothing, kept_far, *slices, *pieces, BF16
    )
    back_near, team_grads = feed_back(
        team_order_table, grad_near, select_near, down_map, team_grads, kept_near, *slices, *pieces, BF16
    )
    second_parts = team_sum(back_near, back_far)
    second_parts, team_grads = step((second_parts, team_grads))
    grad_sent, grad_scaled, grad_first, own_grads = whole_call(
        lambda *refs: turn_kernel(*refs, **style),
        (
            *(moved_back(part, team_back) for part in second_parts),
            mid_stream,
            grad_after,
            attn_total,
            laurel_back,
            second_low,
            gains,
            gate_shrink,
            up_shrink,
            laurel_right,
            laurel_left,
            out_expand,
            rank_out,
            select_own,
        ),
        (
            jax.ShapeDtypeStruct((half_rows, width + adapter_width), BF16),
            wide_f32,
            wide_f32,
            jax.ShapeDtypeStruct((3, grad_rows, width), grad_type),
        ),
        scratch=(work_space, kept_space),
        tables=(weight_order_table, own_pick),
    )
    if not aligned:
        grad_sent = jnp.concatenate(
            [column_blocks(grad_sent[:, :width], weight_order), grad_sent[:, width:]], axis=1
        )
    grad_joined = both_halves(grad_sent, other_core(grad_sent))
    grad_attn = grad_joined[:, :width]
    grad_rank_out = grad_joined[:, width:]
    out_shrink_grad = summed(grad_rank_out, heads_low)
    grad_heads = low(slab_product(grad_attn, out_slabs) + product(grad_rank_out, out_shrink))

    grad_queries, keys_near, keys_far, values_near, values_far = attend_back(
        tables, query_low, kv_all, heads_low, lse, grad_heads, groups, heads_local, head_dim
    )

    keys_come, values_come = flip(keys_far, y_bit), flip(values_far, x_bit)
    keep = keys_near.shape[0] // 2

    def sum_of(own, arrived, rows):
        return low(own[rows].astype(F32) + arrived[rows])

    keys_far = flip(sum_of(keys_near, keys_come, slice(keep, None)), x_bit)
    values_far = flip(sum_of(values_near, values_come, slice(keep, None)), y_bit)
    near_rows = slice(None, keep)
    grad_keys = low(keys_near[near_rows].astype(F32) + keys_come[near_rows] + keys_far)
    grad_values = low(values_near[near_rows].astype(F32) + values_come[near_rows] + values_far)

    def collect(value):
        total = value[0].astype(F32)
        for i in range(1, rest):
            mask = sum(((i >> j) & 1) << bit for j, bit in enumerate(rest_bits))
            total = total + lax.ppermute(
                value[i], "ctx", [(d, d ^ mask) for d in range(count_ctx)]
            )
        return total.reshape(local_rows, -1)

    grad_kv_own = jnp.concatenate([collect(grad_keys), collect(grad_values)], axis=1)

    grad_query_proj = low(jax.vjp(query_piece, query_proj)[1](grad_queries)[0])
    grad_key_proj = low(jax.vjp(key_piece, key_projected)[1](grad_kv_own[:, :head_dim])[0])
    grad_value_proj = low(jax.vjp(value_piece, value_projected)[1](grad_kv_own[:, head_dim:])[0])
    query_expand_grad = summed(rank_query, grad_query_proj)
    key_expand_grad = summed(rank_key, grad_key_proj)
    value_expand_grad = summed(rank_value, grad_value_proj)
    grad_kv_proj = jnp.concatenate([grad_key_proj, grad_value_proj], axis=1)
    first_part = jnp.concatenate(
        [
            against(grad_query_proj, query_maps) + against(grad_kv_proj, kv_maps),
            select * against(grad_query_proj, query_expand),
            select * against(grad_key_proj, key_widen_maps),
            select * against(grad_value_proj, value_widen_maps),
        ],
        axis=1,
    )
    input_own, first_grads = whole_call(
        last_kernel,
        (
            own_half(first_part),
            other_core(low(other_half(first_part))),
            tokens,
            gains,
            grad_scaled,
            grad_first,
            first_shrink,
        ),
        (wide_f32, jax.ShapeDtypeStruct((3, grad_rows, width), grad_type)),
        scratch=(kept_space,),
        tables=(half, own_pick),
        specs={2: half_spec},
    )

    def scatter_split(grads):
        rows = adapter_width // count_ctx
        joined = low(jnp.concatenate(grads, axis=1))
        parts = joined.reshape(count_ctx, rows, joined.shape[1])
        parts = lax.all_to_all(parts, "ctx", 0, 0, tiled=True)
        total = jnp.sum(parts.astype(F32), axis=0)
        cuts, start = [], 0
        for grad in grads:
            cuts.append(total[:, start : start + grad.shape[1]])
            start += grad.shape[1]
        return cuts

    def scatter_team(grads):
        rows = adapter_width // count_ctx
        joined = low(grads).reshape(3, count_ctx, rows, hidden_slice)
        parts = joined.transpose(1, 0, 2, 3).reshape(count_ctx, 3 * rows, hidden_slice)
        parts = lax.all_to_all(parts, "ctx", 0, 0, tiled=True)
        teams = [
            sum(parts[i].astype(F32) for i in range(count_ctx) if (i >> 1) & 3 == t)
            for t in range(4)
        ]
        total = jnp.concatenate(teams, axis=1)
        return [total[i * rows : (i + 1) * rows] for i in range(3)]

    def scatter_shared(grads):
        rows = adapter_width // (2 * count_ctx)
        shaped = grads.reshape(grads.shape[0], count_ctx, 2, rows, width)
        keep = lax.dynamic_index_in_dim(shaped, core, 2, keepdims=False)
        send = lax.dynamic_index_in_dim(shaped, 1 - core, 2, keepdims=False)
        joined = low(keep + other_core(low(send)).astype(F32))
        parts = joined.transpose(1, 0, 2, 3).reshape(count_ctx, grads.shape[0] * rows, width)
        parts = lax.all_to_all(parts, "ctx", 0, 0, tiled=True)
        total = jnp.sum(parts.astype(F32), axis=0)
        return [total[i * rows : (i + 1) * rows] for i in range(grads.shape[0])]

    def one_adapter(grad):
        return low(lax.dynamic_slice_in_dim(grad, own_pick[0] * ADAPTER_RANK, ADAPTER_RANK, 0))

    def core_rows(grads):
        shaped = grads.reshape(grads.shape[0], 2, 2, 4, width)
        keep = lax.dynamic_index_in_dim(shaped, core, 2, keepdims=False).astype(F32)
        send = lax.dynamic_index_in_dim(shaped, 1 - core, 2, keepdims=False)
        return low(keep + other_core(send)).transpose(1, 0, 2, 3).reshape(2, -1, width)

    def deliver(load):
        loads = [load] + [
            lax.ppermute(load, "ctx", [(d, d ^ (4 * r)) for d in range(count_ctx)])
            for r in range(1, count_ctx // 4)
        ]
        picks = [
            jnp.sum(jnp.where(device_ids == (me ^ (4 * r)), pick_of[:, 0], 0))
            for r in range(count_ctx // 4)
        ]
        total = 0.0
        for m in (3, 1, 2, 0):
            place = (me & 3) ^ m
            wanted = (me >> 2) * 2 + (place >> 1)
            sent = sum(
                jnp.where(
                    pick == wanted,
                    lax.dynamic_index_in_dim(each, place & 1, 0, keepdims=False).astype(F32),
                    0.0,
                )
                for pick, each in zip(picks, loads)
            )
            if m:
                sent = lax.ppermute(low(sent), "ctx", [(d, d ^ m) for d in range(count_ctx)])
            total = total + sent.astype(F32)
        return total

    gate_expand_out, up_expand_out, down_shrink_out = scatter_team(team_grads)
    if compact:
        shared = core_rows(jnp.concatenate([own_grads, down_expand_grad[None]], axis=0))
        split = one_adapter(out_shrink_grad).reshape(2, 8, -1)
        split = jnp.pad(split, ((0, 0), (0, 0), (0, width - split.shape[2])))
        found = deliver(jnp.concatenate([shared, split], axis=1))
        gate_shrink_out, up_shrink_out, out_expand_out, down_expand_out = (
            found[4 * i : 4 * i + 4] for i in range(4)
        )
        out_shrink_out = found[16:, : out_shrink_grad.shape[1]]
        expands = [one_adapter(g) for g in (query_expand_grad, key_expand_grad, value_expand_grad)]
        sizes = [g.shape[1] for g in expands]
        split = jnp.concatenate(expands, axis=1).reshape(2, 8, -1)
        split = jnp.pad(split, ((0, 0), (0, 0), (0, width - split.shape[2])))
        found = deliver(jnp.concatenate([core_rows(first_grads), split], axis=1))
        query_shrink_out, key_shrink_out, value_shrink_out = (
            found[4 * i : 4 * i + 4] for i in range(3)
        )
        query_expand_out = found[12:, : sizes[0]]
        key_expand_out = found[12:, sizes[0] : sizes[0] + sizes[1]]
        value_expand_out = found[12:, sizes[0] + sizes[1] : sum(sizes)]
    else:
        (out_shrink_out,) = scatter_split([out_shrink_grad])
        gate_shrink_out, up_shrink_out, out_expand_out, down_expand_out = scatter_shared(
            jnp.concatenate([own_grads, down_expand_grad[None]], axis=0)
        )
        query_expand_out, key_expand_out, value_expand_out = scatter_split(
            [query_expand_grad, key_expand_grad, value_expand_grad]
        )
        query_shrink_out, key_shrink_out, value_shrink_out = scatter_shared(first_grads)

    return (
        both_halves(result_own, other_core(result_own)),
        both_halves(input_own, other_core(input_own)),
        both_halves(layer_input_own, other_core(layer_input_own)),
        query_shrink_out,
        key_shrink_out,
        value_shrink_out,
        gate_shrink_out,
        up_shrink_out,
        out_shrink_out,
        down_shrink_out,
        query_expand_out,
        key_expand_out,
        value_expand_out,
        gate_expand_out,
        up_expand_out,
        out_expand_out,
        down_expand_out,
    )


def solution(mesh):
    in_specs = (
        P("ctx", None),
        P("ctx", None),
        P("ctx", None),
        P(),
        P(),
        P(),
        P(),
        P("ctx", "wt"),
        P("ctx", "wt"),
        P("ctx", "wt"),
        P("ctx", "wt"),
        P("ctx", "wt"),
        P("wt", "ctx"),
        P("wt", "ctx"),
        P(),
        P(),
        P(),
        P(),
        P(),
        P(),
        P(),
        P(),
        P(),
        P(None, "wt"),
        P(None, "wt"),
        P(None, "wt"),
        P(None, "wt"),
        P(None, "wt"),
        P(None, "wt"),
        P(None, "wt"),
        P(),
        P(),
    )
    out_specs = (
        P("ctx", None),
        P("ctx", None),
        P("ctx", None),
        P(("ctx", "wt"), None),
        P(("ctx", "wt"), None),
        P(("ctx", "wt"), None),
        P(("ctx", "wt"), None),
        P(("ctx", "wt"), None),
        P("ctx", "wt"),
        P("ctx", "wt"),
        P("ctx", "wt"),
        P("ctx", "wt"),
        P("ctx", "wt"),
        P("ctx", "wt"),
        P("ctx", "wt"),
        P(("ctx", "wt"), None),
        P(("ctx", "wt"), None),
    )
    return jax.shard_map(local, mesh=mesh, in_specs=in_specs, out_specs=out_specs, check_vma=False)
```

```python
import jax
import jax.numpy as jnp
from jax import lax
from jax.experimental import pallas as pl
from jax.experimental.pallas import tpu as pltpu
from jax.sharding import PartitionSpec as P

QUERY_HEADS = 8
KEY_VALUE_HEADS = 2
ADAPTER_COUNT = 8
ADAPTER_RANK = 16
PROMPT = 2048
CONT = 256

EPS = 1e-06
THETA = 1000000.0
ROOT_HALF = 0.5**0.5
F32 = jnp.float32
BF16 = jnp.bfloat16
SWAP = [(0, 1), (1, 0)]


def normalized(inputs, norm_gain):
    return inputs * lax.rsqrt(jnp.mean(inputs * inputs, axis=-1, keepdims=True) + EPS) * norm_gain


def rotary_applied(inputs, cosine, sine_term):
    half_width = inputs.shape[-1] // 2
    first_half = inputs[..., :half_width]
    second_half = inputs[..., half_width:]
    return jnp.concatenate(
        [
            first_half * cosine - second_half * sine_term,
            second_half * cosine + first_half * sine_term,
        ],
        axis=-1,
    )


def product(left_side, right_side):
    return jnp.dot(left_side, right_side, preferred_element_type=F32)


def against(left_side, right_side):
    return lax.dot_general(
        left_side, right_side, (((1,), (1,)), ((), ())), preferred_element_type=F32
    )


def summed(left_side, right_side):
    return lax.dot_general(
        left_side, right_side, (((0,), (0,)), ((), ())), preferred_element_type=F32
    )


def low(value):
    return value.astype(BF16)


def attend_kernel(count_ref, slot_ref, kslot_ref, vslot_ref, q_ref, kv_ref, o_ref, lse_ref, acc, tot, *, heads, dim):
    group = pl.program_id(0)
    count = count_ref[group]
    rows = q_ref.shape[0]
    fold = tot.shape[-1]
    acc[...] = jnp.zeros_like(acc)
    tot[...] = jnp.zeros_like(tot)

    def step(index, masked):
        keys = kv_ref[slot_ref[group, index], 0, :, :dim]
        values = kv_ref[slot_ref[group, index], 0, :, dim:]
        for head in range(heads):
            lanes = slice(head * dim, (head + 1) * dim)
            scores = against(q_ref[:, lanes], keys)
            weights = jnp.exp(scores)
            if masked:
                row = lax.broadcasted_iota(jnp.int32, scores.shape, 0)
                col = lax.broadcasted_iota(jnp.int32, scores.shape, 1)
                weights = jnp.where(col <= row, weights, 0.0)
            part = weights[:, :fold]
            for start in range(fold, rows, fold):
                part = part + weights[:, start : start + fold]
            tot[head] += part
            acc[:, lanes] += product(low(weights), values)

    def body(index, carry):
        step(index, False)
        return carry

    lax.fori_loop(0, count - 1, body, 0)
    step(count - 1, True)
    lane = lax.broadcasted_iota(jnp.int32, lse_ref.shape, 1)
    lse = jnp.zeros(lse_ref.shape, F32)
    for head in range(heads):
        lanes = slice(head * dim, (head + 1) * dim)
        total = jnp.sum(tot[head], axis=-1, keepdims=True)
        o_ref[:, lanes] = low(acc[:, lanes] / total)
        lse = jnp.where(lane == head, jnp.log(total), lse)
    lse_ref[...] = lse


def attend_back_kernel(
    count_ref, slot_ref, kslot_ref, vslot_ref, q_ref, kv_ref, o_ref, lse_ref, g_ref, dq_ref, dk_near, dk_far, dv_near, dv_far, delta, *, heads, dim
):
    group = pl.program_id(0)
    count = count_ref[group]
    dq_ref[...] = jnp.zeros_like(dq_ref)
    for out_ref in (dk_near, dk_far, dv_near, dv_far):
        out_ref[...] = jnp.zeros_like(out_ref)
    half = dk_near.shape[0]

    def put(near_ref, far_ref, slot, value):
        @pl.when(slot < half)
        def _():
            near_ref[slot, 0] = low(value)

        @pl.when(slot >= half)
        def _():
            far_ref[slot - half, 0] = low(value)

    for head in range(heads):
        lanes = slice(head * dim, (head + 1) * dim)
        delta[head] = jnp.sum(
            o_ref[:, lanes].astype(F32) * g_ref[:, lanes].astype(F32), axis=-1, keepdims=True
        )

    def step(index, masked):
        keys = kv_ref[slot_ref[group, index], 0, :, :dim]
        values = kv_ref[slot_ref[group, index], 0, :, dim:]
        dk = jnp.zeros(keys.shape, F32)
        dv = jnp.zeros(values.shape, F32)
        for head in range(heads):
            lanes = slice(head * dim, (head + 1) * dim)
            queries = q_ref[:, lanes]
            upstream = g_ref[:, lanes]
            scores = against(queries, keys)
            weights = jnp.exp(scores - lse_ref[:, head : head + 1])
            if masked:
                row = lax.broadcasted_iota(jnp.int32, scores.shape, 0)
                col = lax.broadcasted_iota(jnp.int32, scores.shape, 1)
                weights = jnp.where(col <= row, weights, 0.0)
            grad_weights = against(upstream, values)
            grad_scores = low(weights * (grad_weights - delta[head]))
            dq_ref[:, lanes] += product(grad_scores, keys)
            dk += summed(grad_scores, queries)
            dv += summed(low(weights), upstream)
        put(dk_near, dk_far, kslot_ref[group, index], dk)
        put(dv_near, dv_far, vslot_ref[group, index], dv)

    def body(index, carry):
        step(index, False)
        return carry

    lax.fori_loop(0, count - 1, body, 0)
    step(count - 1, True)


def attend(tables, queries, kv_all, groups, heads, dim):
    slots, _, block, _ = kv_all.shape
    rows = queries.shape[0]
    fold = min(128, block)
    whole = pl.BlockSpec((slots, 1, block, 2 * dim), lambda g, *_: (0, g, 0, 0))
    mine = pl.BlockSpec((block, heads * dim), lambda g, *_: (g, 0))
    return pl.pallas_call(
        lambda *refs: attend_kernel(*refs, heads=heads, dim=dim),
        grid_spec=pltpu.PrefetchScalarGridSpec(
            num_scalar_prefetch=4,
            grid=(groups,),
            in_specs=[mine, whole],
            out_specs=[mine, pl.BlockSpec((block, 128), lambda g, *_: (g, 0))],
            scratch_shapes=[
                pltpu.VMEM((block, heads * dim), F32),
                pltpu.VMEM((heads, block, fold), F32),
            ],
        ),
        out_shape=[
            jax.ShapeDtypeStruct((rows, heads * dim), BF16),
            jax.ShapeDtypeStruct((rows, 128), F32),
        ],
        compiler_params=pltpu.CompilerParams(vmem_limit_bytes=40 * 2**20),
        cost_estimate=pl.CostEstimate(
            flops=4 * rows * heads * dim * 2304, bytes_accessed=6 * 2**20, transcendentals=rows * heads * 2304
        ),
    )(*tables, queries, kv_all)


def attend_back(tables, queries, kv_all, heads_low, lse, grads, groups, heads, dim):
    slots, _, block, _ = kv_all.shape
    rows = queries.shape[0]
    whole = pl.BlockSpec((slots, 1, block, 2 * dim), lambda g, *_: (0, g, 0, 0))
    part = pl.BlockSpec((slots // 2, 1, block, dim), lambda g, *_: (0, g, 0, 0))
    mine = pl.BlockSpec((block, heads * dim), lambda g, *_: (g, 0))
    return pl.pallas_call(
        lambda *refs: attend_back_kernel(*refs, heads=heads, dim=dim),
        grid_spec=pltpu.PrefetchScalarGridSpec(
            num_scalar_prefetch=4,
            grid=(groups,),
            in_specs=[mine, whole, mine, pl.BlockSpec((block, 128), lambda g, *_: (g, 0)), mine],
            out_specs=[mine] + [part] * 4,
            scratch_shapes=[pltpu.VMEM((heads, block, 1), F32)],
        ),
        out_shape=[
            jax.ShapeDtypeStruct((rows, heads * dim), F32),
        ]
        + [jax.ShapeDtypeStruct((slots // 2, groups, block, dim), BF16)] * 4,
        compiler_params=pltpu.CompilerParams(vmem_limit_bytes=48 * 2**20),
        cost_estimate=pl.CostEstimate(
            flops=10 * rows * heads * dim * 2304, bytes_accessed=12 * 2**20, transcendentals=rows * heads * 2304
        ),
    )(*tables, queries, kv_all, heads_low, lse, grads)


def gelu_parts(gate):
    slope = 0.7978845608028654
    square = gate * gate
    bend = jnp.tanh(slope * gate * (1.0 + 0.044715 * square))
    half = 0.5 * (1.0 + bend)
    grad = half + 0.5 * gate * (1.0 - bend * bend) * slope * (1.0 + 0.134145 * square)
    return gate * half, grad


def rms_scale(value):
    return lax.rsqrt(jnp.mean(value * value, axis=-1, keepdims=True) + EPS)


def rms_pull(value, scale, weighted):
    return scale * weighted - value * (
        scale * scale * scale * jnp.mean(value * weighted, axis=-1, keepdims=True)
    )


def move_columns(out_ref, in_ref, table_ref, count, block):
    for j in range(count):
        start = pl.multiple_of(table_ref[j] * block, block)
        out_ref[:, j * block : (j + 1) * block] = in_ref[:, pl.ds(start, block)].astype(
            out_ref.dtype
        )


def whole_call(kernel, inputs, outputs, scratch=(), tables=(), specs=None, flops=10**9):
    specs = specs or {}

    def full(array):
        return pl.BlockSpec(array.shape, lambda *_: (0,) * len(array.shape))

    in_specs = [specs.get(i, full(array)) for i, array in enumerate(inputs)]
    size = sum(a.size * a.dtype.itemsize for a in inputs)
    return pl.pallas_call(
        kernel,
        grid_spec=pltpu.PrefetchScalarGridSpec(
            num_scalar_prefetch=len(tables),
            grid=(1,),
            in_specs=in_specs,
            out_specs=[full(array) for array in outputs],
            scratch_shapes=list(scratch),
        ),
        out_shape=list(outputs),
        compiler_params=pltpu.CompilerParams(vmem_limit_bytes=56 * 2**20),
        cost_estimate=pl.CostEstimate(flops=flops, bytes_accessed=size, transcendentals=0),
    )(*tables, *inputs)


def first_kernel(tokens_ref, gains_ref, select_ref, shrink_ref, low_ref, rank_ref):
    tokens = tokens_ref[...].astype(F32)
    first = low(tokens * rms_scale(tokens) * gains_ref[0:1, :])
    low_ref[...] = first
    ranks = against(first, shrink_ref[...])
    select = select_ref[...]
    width = select.shape[1]
    for i in range(3):
        rank_ref[:, i * width : (i + 1) * width] = low(select * ranks[:, i * width : (i + 1) * width])


def middle_kernel(
    half_ref, back_ref, own_ref, other_ref, tokens_ref, gains_ref, expand_ref, left_ref, right_ref,
    total_ref, laurel_ref, mid_ref, second_ref, rank_ref, work, *, count, block, aligned
):
    width = total_ref.shape[1]
    summed_all = own_ref[...] + other_ref[...].astype(F32)
    rank = low(summed_all[:, width:])
    rank_ref[...] = rank
    if aligned:
        work[...] = summed_all[:, :width]
        move_columns(total_ref, work, back_ref, count, block)
        attn = total_ref[...] + product(rank, expand_ref[...])
    else:
        attn = summed_all[:, :width] + product(rank, expand_ref[...])
    total_ref[...] = attn
    tokens = tokens_ref[...].astype(F32)
    first = tokens * rms_scale(tokens) * gains_ref[0:1, :]
    laurel = product(low(product(low(first), left_ref[...])), right_ref[...])
    laurel_ref[...] = laurel
    mid = (
        tokens
        + attn * rms_scale(attn) * gains_ref[1:2, :]
        + first
        + laurel * rms_scale(laurel) * gains_ref[2:3, :]
    ) * ROOT_HALF
    mid_ref[...] = mid
    second_ref[...] = low(mid * rms_scale(mid) * gains_ref[3:4, :])


def keep_rows(out_ref, work_ref, value, pick_ref):
    if out_ref.shape[0] == value.shape[0]:
        out_ref[...] = value.astype(out_ref.dtype)
    else:
        work_ref[...] = value
        rows = out_ref.shape[0]
        start = pl.multiple_of(pick_ref[0] * rows, rows)
        out_ref[...] = work_ref[pl.ds(start, rows), :].astype(out_ref.dtype)


def layer_kernel(
    half_ref, pick_ref, near_ref, y_ref, z_ref, yz_ref, mid_ref, gains_ref, expand_ref, gate_ref, lift_ref, layer_ref, up_ref,
    result_ref, layer_grad_ref, after_ref, grad_ref, expand_grad_ref, kept
):
    width = mid_ref.shape[1]
    joined = near_ref[...].astype(F32) + y_ref[...] + z_ref[...] + yz_ref[...]
    rank = low(joined[:, width:])
    total = joined[:, :width] + product(rank, expand_ref[...])
    scale = rms_scale(total)
    gain = gains_ref[4:5, :]
    after = mid_ref[...] + total * scale * gain
    layer_pre = product(low(after), gate_ref[...])
    layer_in = layer_ref[...].astype(F32)
    act, slope = gelu_parts(layer_pre)
    back = product(low(act * layer_in), lift_ref[...])
    back_scale = rms_scale(back)
    last_gain = gains_ref[5:6, :]
    result_ref[...] = low(after + back * back_scale * last_gain)
    upstream = up_ref[...].astype(F32)
    grad_back = low(rms_pull(back, back_scale, upstream * last_gain))
    grad_gated = against(grad_back, lift_ref[...])
    layer_grad_ref[...] = grad_gated * act
    grad_pre = low(grad_gated * layer_in * slope)
    grad_after = upstream + against(grad_pre, gate_ref[...])
    after_ref[...] = grad_after
    grad_ffn = low(rms_pull(total, scale, grad_after * gain))
    grad_ref[...] = grad_ffn
    keep_rows(expand_grad_ref, kept, summed(rank, grad_ffn), pick_ref)


def turn_kernel(
    order_ref, pick_ref, near_ref, y_ref, z_ref, yz_ref, mid_ref, after_ref, total_ref, laurel_ref, second_ref, gains_ref, gate_ref, up_ref,
    right_ref, left_ref, expand_ref, rank_ref, select_ref,
    sent_ref, scaled_ref, first_ref, grads_ref, work, kept, *, count, block, aligned
):
    width = mid_ref.shape[1]
    ranks = select_ref.shape[1]
    joined = near_ref[...].astype(F32) + y_ref[...] + z_ref[...] + yz_ref[...]
    rank_gate = low(joined[:, width : width + ranks])
    rank_up = low(joined[:, width + ranks :])
    grad_second = joined[:, :width]
    grad_second = grad_second + product(rank_gate, gate_ref[...]) + product(rank_up, up_ref[...])
    keep_rows(grads_ref.at[0], kept, summed(rank_gate, second_ref[...]), pick_ref)
    keep_rows(grads_ref.at[1], kept, summed(rank_up, second_ref[...]), pick_ref)
    mid = mid_ref[...]
    grad_mid = after_ref[...] + rms_pull(mid, rms_scale(mid), grad_second * gains_ref[3:4, :])
    scaled = grad_mid * ROOT_HALF
    scaled_ref[...] = scaled
    attn = total_ref[...]
    grad_attn = rms_pull(attn, rms_scale(attn), scaled * gains_ref[1:2, :])
    laurel = laurel_ref[...]
    grad_laurel = low(rms_pull(laurel, rms_scale(laurel), scaled * gains_ref[2:3, :]))
    grad_rank = low(against(grad_laurel, right_ref[...]))
    first_ref[...] = scaled + against(grad_rank, left_ref[...])
    attn_low = low(grad_attn)
    keep_rows(grads_ref.at[2], kept, summed(rank_ref[...], attn_low), pick_ref)
    sent_ref[:, width:] = low(select_ref[...] * against(attn_low, expand_ref[...]))
    if aligned:
        work[...] = grad_attn
        for j in range(count):
            start = pl.multiple_of(order_ref[j] * block, block)
            sent_ref[:, j * block : (j + 1) * block] = low(work[:, pl.ds(start, block)])
    else:
        sent_ref[:, :width] = attn_low


def last_kernel(
    half_ref, pick_ref, own_ref, other_ref, tokens_ref, gains_ref, scaled_ref, first_ref, shrink_ref,
    input_ref, grads_ref, kept
):
    width = scaled_ref.shape[1]
    joined = own_ref[...] + other_ref[...].astype(F32)
    ranks = low(joined[:, width:])
    each = ranks.shape[1] // 3
    grad_first = joined[:, :width]
    grad_first = grad_first + first_ref[...] + product(ranks, shrink_ref[...])
    tokens = tokens_ref[...].astype(F32)
    scale = rms_scale(tokens)
    gain = gains_ref[0:1, :]
    input_ref[...] = scaled_ref[...] + rms_pull(tokens, scale, grad_first * gain)
    first = low(tokens * scale * gain)
    for i in range(3):
        keep_rows(
            grads_ref.at[i], kept, summed(ranks[:, i * each : (i + 1) * each], first), pick_ref
        )


def gather_parts(out_ref, parts, table_ref, count, width):
    height = parts[0].shape[0]
    block = width // count
    for i, part in enumerate(parts):
        rows = slice(i * height, (i + 1) * height)
        if block % 128 == 0:
            for j in range(count):
                start = pl.multiple_of(table_ref[j] * block, block)
                out_ref[rows, j * block : (j + 1) * block] = part[:, pl.ds(start, block)]
        else:
            out_ref[rows, :] = part[...]


def ranks_of(out_ref, parts, select_ref, maps_ref):
    height = parts[0].shape[0]
    ranks = select_ref.shape[1]
    for i, part in enumerate(parts):
        rows = slice(i * height, (i + 1) * height)
        found = against(part[...], maps_ref[...])
        for start in range(0, out_ref.shape[1], ranks):
            out_ref[rows, start : start + ranks] = low(
                select_ref[rows, :] * found[:, start : start + ranks]
            )


def bring(pieces, space, sems):
    rows = pieces[0].shape[0]
    copies = [
        pltpu.make_async_copy(piece, space.at[pl.ds(i * rows, rows), :], sems.at[i])
        for i, piece in enumerate(pieces)
    ]
    for copy in copies:
        copy.start()
    return copies


def put_halves(refs, value, start, table_ref, block):
    half = refs[0].shape[0]
    for i, ref in enumerate(refs):
        put_columns(ref, value[i * half : (i + 1) * half], start, table_ref, block)


def put_columns(out_ref, value, start, table_ref, block):
    size = value.shape[1]
    if block % 128:
        out_ref[:, pl.ds(start, size)] = value.astype(out_ref.dtype)
        return
    for i in range(size // block):
        place = pl.multiple_of(table_ref[start // block + i] * block, block)
        out_ref[:, pl.ds(place, block)] = value[:, i * block : (i + 1) * block].astype(out_ref.dtype)


def feed_kernel(order_ref, *refs, pieces, width, count):
    parts, (select_ref, shrink_ref, gexp_ref, uexp_ref, dshr_ref), refs = refs[:4], refs[4:9], refs[9:]
    gates, ups, downs = refs[:pieces], refs[pieces : 2 * pieces], refs[2 * pieces : 3 * pieces]
    rank_ref, act_ref, slope_ref, hid_ref, near_ref, far_ref, x_ref, gate_w, up_w, down_w, sems = refs[3 * pieces :]
    arriving = bring(gates, gate_w, sems.at[0]) + bring(ups, up_w, sems.at[1])
    arriving_down = bring(downs, down_w, sems.at[2])
    ranks = select_ref.shape[1]
    hidden_width = gate_w.shape[1]
    chunk = min(1024, hidden_width)
    gather_parts(x_ref, parts, order_ref, count, width)
    ranks_of(rank_ref, parts, select_ref, shrink_ref)
    for copy in arriving:
        copy.wait()

    @pl.loop(0, hidden_width // chunk)
    def _(i):
        lanes = pl.ds(pl.multiple_of(i * chunk, chunk), chunk)
        gate = product(x_ref[...], gate_w[:, lanes]) + product(rank_ref[:, :ranks], gexp_ref[:, lanes])
        up = product(x_ref[...], up_w[:, lanes]) + product(rank_ref[:, ranks:], uexp_ref[:, lanes])
        act, slope = gelu_parts(gate)
        act_ref[:, lanes] = low(act)
        slope_ref[:, lanes] = low(slope * up)
        hid_ref[:, lanes] = low(act * up)

    for copy in arriving_down:
        copy.wait()
    step = 1024

    @pl.loop(0, width // step)
    def _(i):
        start = pl.multiple_of(i * step, step)
        found = against(hid_ref[...], down_w[pl.ds(start, step), :])
        put_halves((near_ref, far_ref), found, start, order_ref, width // count)

    found = low(select_ref[...] * against(hid_ref[...], dshr_ref[...]))
    half = near_ref.shape[0]
    near_ref[:, width:] = found[:half]
    far_ref[:, width:] = found[half:]


def feed_call(kernel, order, parts, inputs, weights, outputs, scratch, flops):
    def full(array):
        return pl.BlockSpec(array.shape, lambda *_: (0,) * len(array.shape))

    pieces = [piece for matrix in weights for piece in matrix]
    matrix = pltpu.VMEM((len(weights[0]) * weights[0][0].shape[0], weights[0][0].shape[1]), BF16)
    width = parts[0].shape[1]
    return pl.pallas_call(
        lambda *refs: kernel(*refs, pieces=len(weights[0]), width=width, count=order.shape[0]),
        grid_spec=pltpu.PrefetchScalarGridSpec(
            num_scalar_prefetch=1,
            grid=(1,),
            in_specs=[full(array) for array in (*parts, *inputs)]
            + [pl.BlockSpec(memory_space=pl.ANY)] * len(pieces),
            out_specs=[full(array) for array in outputs],
            scratch_shapes=list(scratch)
            + [matrix, matrix, matrix, pltpu.SemaphoreType.DMA((3, len(weights[0])))],
        ),
        out_shape=list(outputs),
        compiler_params=pltpu.CompilerParams(vmem_limit_bytes=58 * 2**20),
        cost_estimate=pl.CostEstimate(flops=flops, bytes_accessed=20 * 2**20, transcendentals=0),
    )(order, *parts, *inputs, *pieces)


def feed(order, parts, select, shrink, gexp, uexp, dshr, gates, ups, downs):
    rows, width = 4 * parts[0].shape[0], parts[0].shape[1]
    hidden, ranks = gexp.shape[1], select.shape[1]
    low_hidden = jax.ShapeDtypeStruct((rows, hidden), BF16)
    return feed_call(
        feed_kernel,
        order,
        parts,
        (select, shrink, gexp, uexp, dshr),
        (gates, ups, downs),
        (
            jax.ShapeDtypeStruct((rows, 2 * ranks), BF16),
            low_hidden,
            low_hidden,
            low_hidden,
            *[jax.ShapeDtypeStruct((rows // 2, width + ranks), BF16)] * 2,
        ),
        (pltpu.VMEM((rows, width), BF16),),
        6 * rows * width * hidden,
    )


def feed_back_kernel(order_ref, *refs, pieces, width, count):
    parts, refs = refs[:4], refs[4:]
    (
        select_ref,
        dexp_ref,
        rank_ref,
        start_ref,
        act_ref,
        slope_ref,
        hid_ref,
        gexp_ref,
        uexp_ref,
        dshr_ref,
    ), refs = refs[:10], refs[10:]
    gates, ups, downs = refs[:pieces], refs[pieces : 2 * pieces], refs[2 * pieces : 3 * pieces]
    near_ref, far_ref, grads_ref, g_ref, down_rank, gate_grad, up_grad, gate_w, up_w, down_w, sems = refs[3 * pieces :]
    arriving = bring(downs, down_w, sems.at[2])
    arriving_next = bring(gates, gate_w, sems.at[0]) + bring(ups, up_w, sems.at[1])
    ranks = select_ref.shape[1]
    hidden_width = gate_w.shape[1]
    chunk = min(1024, hidden_width)
    gather_parts(g_ref, parts, order_ref, count, width)
    ranks_of(down_rank, parts, select_ref, dexp_ref)
    for copy in arriving:
        copy.wait()

    @pl.loop(0, hidden_width // chunk)
    def _(i):
        lanes = pl.ds(pl.multiple_of(i * chunk, chunk), chunk)
        grad_hidden = product(g_ref[...], down_w[:, lanes]) + product(down_rank[...], dshr_ref[:, lanes])
        grad_gate = low(grad_hidden * slope_ref[:, lanes].astype(F32))
        grad_up = low(grad_hidden * act_ref[:, lanes].astype(F32))
        gate_grad[:, lanes] = grad_gate
        up_grad[:, lanes] = grad_up
        grads_ref[0, :, lanes] = start_ref[0, :, lanes] + summed(rank_ref[:, :ranks], grad_gate)
        grads_ref[1, :, lanes] = start_ref[1, :, lanes] + summed(rank_ref[:, ranks:], grad_up)
        grads_ref[2, :, lanes] = start_ref[2, :, lanes] + summed(down_rank[...], hid_ref[:, lanes])

    for copy in arriving_next:
        copy.wait()
    step = 1024

    @pl.loop(0, width // step)
    def _(i):
        start = pl.multiple_of(i * step, step)
        found = against(gate_grad[...], gate_w[pl.ds(start, step), :]) + against(
            up_grad[...], up_w[pl.ds(start, step), :]
        )
        put_halves((near_ref, far_ref), found, start, order_ref, width // count)

    select = select_ref[...]
    gate_found = low(select * against(gate_grad[...], gexp_ref[...]))
    up_found = low(select * against(up_grad[...], uexp_ref[...]))
    half = near_ref.shape[0]
    for i, ref in enumerate((near_ref, far_ref)):
        ref[:, width : width + ranks] = gate_found[i * half : (i + 1) * half]
        ref[:, width + ranks :] = up_found[i * half : (i + 1) * half]


def feed_back(order, parts, select, dexp, start, kept, gexp, uexp, dshr, gates, ups, downs):
    rows, width = 4 * parts[0].shape[0], parts[0].shape[1]
    hidden, ranks = gexp.shape[1], select.shape[1]
    low_hidden = pltpu.VMEM((rows, hidden), BF16)
    return feed_call(
        feed_back_kernel,
        order,
        parts,
        (select, dexp, kept[0], start, *kept[1:], gexp, uexp, dshr),
        (gates, ups, downs),
        (
            *[jax.ShapeDtypeStruct((rows // 2, width + 2 * ranks), BF16)] * 2,
            jax.ShapeDtypeStruct((3, ranks, hidden), F32),
        ),
        (pltpu.VMEM((rows, width), BF16), pltpu.VMEM((rows, ranks), BF16), low_hidden, low_hidden),
        6 * rows * width * hidden,
    )


def local(
    tokens,
    layer_input,
    out_grad,
    block_device,
    adapter_pick,
    norm_gains,
    head_norm_gains,
    query_weight,
    key_matrix,
    value_matrix,
    gate_weight,
    up_weight,
    out_weight,
    down_weight,
    laurel_left,
    laurel_right,
    layer_gate,
    layer_lift,
    query_shrink,
    key_shrink,
    value_shrink,
    gate_shrink,
    up_shrink,
    out_shrink,
    down_shrink,
    query_expand,
    key_widen_maps,
    value_widen_maps,
    gate_expand,
    up_expand,
    out_expand,
    down_expand,
):
    count_ctx = lax.axis_size("ctx")
    bit_count = count_ctx.bit_length() - 1
    groups = block_device.shape[0]
    local_rows, width = tokens.shape
    block_len = local_rows // groups
    half_rows = local_rows // 2
    head_dim = head_norm_gains.shape[1]
    heads_local = query_weight.shape[1] // head_dim
    adapter_width = ADAPTER_COUNT * ADAPTER_RANK
    model_block = width // count_ctx
    hidden_slice = gate_weight.shape[1] // 4
    me = lax.axis_index("ctx")
    core = lax.axis_index("wt")

    spread_bits = list(range(3, bit_count)) + [0]
    team_place = (me >> 1) & 3

    def flip(value, bit):
        return lax.ppermute(value, "ctx", [(i, i ^ (1 << bit)) for i in range(count_ctx)])

    def other_core(value):
        return lax.ppermute(value, "wt", SWAP)

    def own_half(value):
        return lax.dynamic_slice_in_dim(value, core * half_rows, half_rows, 0)

    def other_half(value):
        return lax.dynamic_slice_in_dim(value, (1 - core) * half_rows, half_rows, 0)

    def both_halves(own, other):
        return jnp.where(
            core == 0, jnp.concatenate([own, other], axis=0), jnp.concatenate([other, own], axis=0)
        )

    def column_blocks(value, places):
        return jnp.concatenate(
            [
                lax.dynamic_slice_in_dim(value, place * model_block, model_block, 1)
                for place in places
            ],
            axis=1,
        )

    rest = count_ctx // 4
    rest_bits = list(range(2, bit_count))

    def rest_place(apart):
        return sum(((apart >> bit) & 1) << i for i, bit in enumerate(rest_bits))

    weight_order = [
        me
        ^ (
            (j // (2 * rest)) * 2
            + (j // rest) % 2
            + sum(((j >> i) & 1) << bit for i, bit in enumerate(rest_bits))
        )
        for j in range(count_ctx)
    ]
    weight_back = [
        (((d ^ me) >> 1) & 1) * 2 * rest + ((d ^ me) & 1) * rest + rest_place(d ^ me)
        for d in range(count_ctx)
    ]
    piece_masks = [0]
    for bit in spread_bits:
        piece_masks = piece_masks + [mask | (1 << bit) for mask in piece_masks]
    team_order = [me ^ mask ^ (2 * t) for mask in piece_masks for t in range(4)]
    team_back = [
        4 * sum((((b ^ me) >> bit) & 1) << i for i, bit in enumerate(spread_bits))
        + (((b ^ me) >> 1) & 3)
        for b in range(count_ctx)
    ]

    def to_member(value, member):
        if member == 0:
            return value
        return lax.ppermute(value, "ctx", [(d, d ^ (2 * member)) for d in range(count_ctx)])

    def team_split(shard):
        parts = [
            to_member(
                lax.dynamic_slice_in_dim(
                    shard, (team_place ^ member) * hidden_slice, hidden_slice, 1
                ),
                member,
            )
            for member in range(4)
        ]
        return joined(parts[0], parts[1]), joined(parts[2], parts[3])

    def joined(own, arrived):
        return jnp.concatenate([own, arrived], axis=0)

    prompt_blocks = PROMPT // block_len
    cont_blocks = CONT // block_len
    device_ids = jnp.arange(count_ctx, dtype=jnp.int32)
    block_of = jnp.sum(
        jnp.where(block_device[None] == device_ids[:, None, None], device_ids[None, None, :], 0),
        axis=2,
    )
    cont_of = (block_of - prompt_blocks) // cont_blocks
    pick_of = jnp.sum(
        jnp.where(
            cont_of[:, :, None] == jnp.arange(adapter_pick.shape[1], dtype=jnp.int32),
            adapter_pick[None],
            0,
        ),
        axis=2,
    )
    pick_of = jnp.where(block_of < prompt_blocks, -1, pick_of)
    compact = groups == 1 and count_ctx * 8 == adapter_width
    own_pick = jnp.maximum(jnp.sum(jnp.where(device_ids[:, None] == me, pick_of, 0), axis=0), 0)
    own_pick = own_pick[:1].astype(jnp.int32)
    grad_rows = ADAPTER_RANK if compact else adapter_width
    grad_type = BF16 if compact else F32

    def picks_at(device):
        return jnp.sum(jnp.where(device_ids[:, None] == device, pick_of, 0), axis=0)

    def select_rows(picks):
        rows = jnp.repeat(picks, block_len)
        return (
            jnp.arange(adapter_width, dtype=jnp.int32)[None, :] // ADAPTER_RANK == rows[:, None]
        ).astype(F32)

    select = select_rows(picks_at(me))
    select_own = own_half(select)
    team_select = [select_rows(picks_at(me ^ (2 * t))) for t in range(4)]

    def select_of(members):
        return jnp.concatenate(
            [own_half(team_select[m]) for m in members] + [other_half(team_select[m]) for m in members],
            axis=0,
        )

    beside, across = (1, 2), (0, 3)
    select_beside, select_across = select_of(beside), select_of(across)

    my_block = jnp.sum(jnp.where(device_ids[:, None] == me, block_of, 0), axis=0)
    positions = (
        my_block[:, None] * block_len + jnp.arange(block_len, dtype=jnp.int32)[None, :]
    ).reshape(-1)
    seq_pos = jnp.where(positions < PROMPT, positions, PROMPT + (positions - PROMPT) % CONT)
    frequency = THETA ** (-2.0 * jnp.arange(head_dim // 2, dtype=F32) / head_dim)
    rotary_angles = seq_pos.astype(F32)[:, None] * frequency[None, :]
    cosine = jnp.cos(rotary_angles)[:, None, :]
    sine_term = jnp.sin(rotary_angles)[:, None, :]
    cont_start = prompt_blocks + (my_block - prompt_blocks) // cont_blocks * cont_blocks
    is_prompt = my_block < prompt_blocks
    visible_count = jnp.where(
        is_prompt, my_block + 1, prompt_blocks + my_block - cont_start + 1
    ).astype(jnp.int32)
    entries = jnp.arange(prompt_blocks + cont_blocks, dtype=jnp.int32)
    visible_block = jnp.where(
        is_prompt[:, None] | (entries < prompt_blocks)[None, :],
        entries[None, :],
        cont_start[:, None] + entries[None, :] - prompt_blocks,
    )
    visible_device = jnp.sum(
        jnp.where(
            visible_block[:, :, None] == device_ids[None, None, :], block_device[:, None, :], 0
        ),
        axis=2,
    )
    apart = visible_device ^ me
    key_slot = (((apart >> 1) & 1) * 2 + (apart & 1)) * rest + rest_place(apart)
    value_slot = ((apart & 1) * 2 + ((apart >> 1) & 1)) * rest + rest_place(apart)
    tables = tuple(
        table.astype(jnp.int32) for table in (visible_count, visible_device, key_slot, value_slot)
    )

    gains = norm_gains.astype(F32)
    query_gain = head_norm_gains[0].astype(F32)
    key_gain = head_norm_gains[1].astype(F32)

    def query_piece(projected):
        return (
            rotary_applied(
                normalized(projected.reshape(local_rows, -1, head_dim), query_gain),
                cosine,
                sine_term,
            )
            * head_dim ** (-0.5)
        ).reshape(local_rows, -1)

    def key_piece(projected):
        return rotary_applied(
            normalized(projected.reshape(local_rows, -1, head_dim), key_gain), cosine, sine_term
        ).reshape(local_rows, -1)

    def value_piece(projected):
        return normalized(projected.reshape(local_rows, -1, head_dim), 1.0).reshape(local_rows, -1)

    def slab_product(value, slabs):
        middle = value.shape[1] // 2
        return product(value[:, :middle], slabs[0]) + product(value[:, middle:], slabs[1])

    def slab_against(value, slabs):
        return jnp.concatenate([against(value, slabs[0]), against(value, slabs[1])], axis=1)

    half = jnp.reshape(core, (1,)).astype(jnp.int32)
    aligned = model_block % 128 == 0
    style = dict(count=count_ctx, block=model_block, aligned=aligned)
    weight_order_table = jnp.stack(weight_order).astype(jnp.int32)
    weight_back_table = jnp.stack(weight_back).astype(jnp.int32)
    team_order_table = jnp.stack(team_order).astype(jnp.int32)
    half_spec = pl.BlockSpec((half_rows, width), lambda i, half, *_: (half[0], 0))
    wide_f32 = jax.ShapeDtypeStruct((half_rows, width), F32)
    wide_low = jax.ShapeDtypeStruct((half_rows, width), BF16)
    work_space = pltpu.VMEM((half_rows, width), F32)
    kept_space = pltpu.VMEM((adapter_width, width), F32)

    def moved(value, places):
        return value if aligned else column_blocks(value, places)

    def moved_back(value, places):
        if aligned:
            return value
        flat = value.reshape(-1, value.shape[-1])
        flat = jnp.concatenate([column_blocks(flat[:, :width], places), flat[:, width:]], axis=1)
        return flat.reshape(value.shape)

    first_shrink = jnp.concatenate([query_shrink, key_shrink, value_shrink], axis=0)
    first_low, rank_first = whole_call(
        first_kernel,
        (tokens, gains, select, first_shrink),
        (
            jax.ShapeDtypeStruct(tokens.shape, BF16),
            jax.ShapeDtypeStruct((local_rows, 3 * adapter_width), BF16),
        ),
    )
    rank_query = rank_first[:, :adapter_width]
    rank_key = rank_first[:, adapter_width : 2 * adapter_width]
    rank_value = rank_first[:, 2 * adapter_width :]

    far_bits, near_bit = spread_bits[:-1], spread_bits[-1]
    x_bit, y_bit = 0, 1
    first_bit = rest_bits[0]
    sent_before = {}

    def queued(line, value, move, depth=2):
        earlier = sent_before.setdefault(line, [])
        if len(earlier) >= depth:
            value = lax.optimization_barrier((value, earlier[-depth]))[0]
        result = move(value)
        earlier.append(result)
        return result

    def over_x(value):
        return queued("x", value, lambda v: flip(v, x_bit))

    def over_y(value):
        return queued("y", value, lambda v: flip(v, y_bit))

    def over_rest(value, bits):
        for bit in bits:
            value = joined(value, queued("z", value, lambda v, bit=bit: flip(v, bit)))
        return value

    def spread_far(piece):
        pieces = [piece]
        for bit in far_bits:
            pieces = pieces + [queued("z", other, lambda v, bit=bit: flip(v, bit)) for other in pieces]
        return pieces[1:]

    def near(pieces):
        return [over_x(piece) for piece in pieces]

    step = lax.optimization_barrier
    head_maps = lax.all_gather(
        jnp.concatenate([query_weight, key_matrix, value_matrix], axis=1), "ctx", axis=0, tiled=True
    )
    out_rows = out_weight.T
    gate_a, gate_b = team_split(gate_weight)
    up_a, up_b = team_split(up_weight)
    gate_far_a = spread_far(gate_a)
    gate_far_b = spread_far(gate_b)
    gate_near_a, gate_near_b = near([gate_a]), near([gate_b])
    up_far_a = spread_far(up_a)
    up_near_a, up_near_b = near([up_a]), near([up_b])
    gate_far_near_a = near(gate_far_a)
    head_maps, gate_far_a, gate_far_b, gate_near_a, gate_near_b, up_far_a, up_near_a, up_near_b, gate_far_near_a = step(
        (head_maps, gate_far_a, gate_far_b, gate_near_a, gate_near_b, up_far_a, up_near_a, up_near_b, gate_far_near_a)
    )
    query_width, kv_width = query_weight.shape[1], key_matrix.shape[1]
    query_maps, kv_maps = head_maps[:, :query_width], head_maps[:, query_width:]
    kv_projected = product(first_low, kv_maps)
    key_projected = kv_projected[:, :kv_width] + product(rank_key, key_widen_maps)
    value_projected = kv_projected[:, kv_width:] + product(rank_value, value_widen_maps)
    kv_low = jnp.concatenate([low(key_piece(key_projected)), low(value_piece(value_projected))], axis=1)
    kv_all = lax.all_gather(kv_low, "ctx", axis=0, tiled=True).reshape(
        count_ctx, groups, block_len, 2 * head_dim
    )
    query_proj = product(first_low, query_maps) + product(rank_query, query_expand)
    query_low = low(query_piece(query_proj))
    down_a, down_b = team_split(down_weight.T)
    up_far_b = spread_far(up_b)
    out_part = joined(out_rows, flip(out_rows, first_bit))
    out_part = over_rest(out_part, rest_bits[1:])
    out_slab = joined(out_part, over_x(out_part))
    out_slabs = out_slab, over_y(out_slab)
    gate_far_near_b = near(gate_far_b)
    up_far_near_a = near(up_far_a)
    down_far_a, down_far_b = spread_far(down_a), spread_far(down_b)
    down_near_a, down_near_b = near([down_a]), near([down_b])
    up_far_near_b = near(up_far_b)
    kv_all, down_far_a, up_far_near_a, up_far_b, out_slab, gate_far_near_b, down_near_a = step(
        (kv_all, down_far_a, up_far_near_a, up_far_b, out_slab, gate_far_near_b, down_near_a)
    )
    out_slabs = out_slab, out_slabs[1]
    down_far_near_a = near(down_far_a)
    heads_low, lse = attend(tables, query_low, kv_all, groups, heads_local, head_dim)

    heads_low, out_slabs, down_far_b, up_far_near_b, down_near_b = step(
        (heads_low, out_slabs, down_far_b, up_far_near_b, down_near_b)
    )
    down_far_near_b = near(down_far_b)
    attn_part = jnp.concatenate(
        [slab_against(heads_low, out_slabs), select * against(heads_low, out_shrink)], axis=1
    )
    attn_total, laurel_back, mid_stream, second_low, rank_out = whole_call(
        lambda *refs: middle_kernel(*refs, **style),
        (
            moved_back(own_half(attn_part), weight_back),
            moved_back(other_core(other_half(attn_part)), weight_back),
            tokens,
            gains,
            out_expand,
            laurel_left,
            laurel_right,
        ),
        (
            wide_f32,
            wide_f32,
            wide_f32,
            wide_low,
            jax.ShapeDtypeStruct((half_rows, adapter_width), BF16),
        ),
        scratch=(work_space,),
        tables=(half, weight_back_table),
        specs={2: half_spec},
    )

    def in_order(own, far, near_own, near_far):
        first, second = ([o] + f + n + nf for o, f, n, nf in zip(own, far, near_own, near_far))
        return [piece for pair in zip(first, second) for piece in pair]

    gate_pieces = in_order(
        (gate_a, gate_b),
        (gate_far_a, gate_far_b),
        (gate_near_a, gate_near_b),
        (gate_far_near_a, gate_far_near_b),
    )
    up_pieces = in_order(
        (up_a, up_b), (up_far_a, up_far_b), (up_near_a, up_near_b), (up_far_near_a, up_far_near_b)
    )
    down_pieces = in_order(
        (down_a, down_b),
        (down_far_a, down_far_b),
        (down_near_a, down_near_b),
        (down_far_near_a, down_far_near_b),
    )

    def in_two_calls(value, call):
        near_parts = [to_member(value, member) for member in (1, 2, 3)]
        first_rows = near_parts[:2] + [other_core(part) for part in near_parts[:2]]
        near_sum, far_sum, *kept_first = call(0, first_rows, None)
        near_sum, far_sum, kept_first, last_part = step(
            (near_sum, far_sum, tuple(kept_first), near_parts[2])
        )
        arrived = other_core(far_sum)
        totals = [
            low(near_sum[i * half_rows : (i + 1) * half_rows].astype(F32) + arrived[i * half_rows : (i + 1) * half_rows])
            for i in range(2)
        ]
        second_rows = [value, last_part, other_core(value), other_core(last_part)]
        totals, second_rows, kept_first = step((totals, second_rows, kept_first))
        beside_parts = [to_member(total, member) for total, member in zip(totals, (1, 2))]
        near_sum, far_sum, *kept_second = call(1, second_rows, kept_first)
        far_sum, beside_parts = step((far_sum, beside_parts))
        arrived = other_core(far_sum)
        over = low(near_sum[half_rows:].astype(F32) + arrived[half_rows:])
        own = low(near_sum[:half_rows].astype(F32) + arrived[:half_rows])
        return [own] + beside_parts + [to_member(over, 3)], kept_first, kept_second

    def hidden_columns(value):
        return lax.dynamic_slice_in_dim(value, team_place * hidden_slice, hidden_slice, 1)

    feed_maps = moved(jnp.concatenate([gate_shrink, up_shrink], axis=0), team_order)
    down_map = moved(down_expand, team_order)
    slices = tuple(hidden_columns(value) for value in (gate_expand, up_expand, down_shrink))
    pieces = (gate_pieces, up_pieces, down_pieces)

    selects = select_beside, select_across

    def forward(index, rows, earlier):
        *kept, near_part, far_part = feed(
            team_order_table, rows, selects[index], feed_maps, *slices, *pieces
        )
        return near_part, far_part, *kept

    ffn_parts, *kept_calls = in_two_calls(moved(second_low, team_order), forward)

    result_own, layer_input_own, grad_after, grad_ffn, down_expand_grad = whole_call(
        layer_kernel,
        (
            *(moved_back(part, team_back) for part in ffn_parts),
            mid_stream,
            gains,
            down_expand,
            layer_gate,
            layer_lift,
            layer_input,
            out_grad,
        ),
        (
            wide_low,
            jax.ShapeDtypeStruct((half_rows, layer_input.shape[1]), F32),
            wide_f32,
            wide_low,
            jax.ShapeDtypeStruct((grad_rows, width), grad_type),
        ),
        scratch=(kept_space,),
        tables=(half, own_pick),
        specs={
            9: pl.BlockSpec((half_rows, layer_input.shape[1]), lambda i, half, *_: (half[0], 0)),
            10: half_spec,
        },
    )

    nothing = jnp.zeros((3, adapter_width, hidden_slice), F32)

    def backward(index, rows, earlier):
        return feed_back(
            team_order_table,
            rows,
            selects[index],
            down_map,
            nothing if earlier is None else earlier[0],
            kept_calls[index],
            *slices,
            *pieces,
        )

    second_parts, _, (team_grads,) = in_two_calls(moved(grad_ffn, team_order), backward)
    second_parts, team_grads = step((second_parts, team_grads))
    grad_sent, grad_scaled, grad_first, own_grads = whole_call(
        lambda *refs: turn_kernel(*refs, **style),
        (
            *(moved_back(part, team_back) for part in second_parts),
            mid_stream,
            grad_after,
            attn_total,
            laurel_back,
            second_low,
            gains,
            gate_shrink,
            up_shrink,
            laurel_right,
            laurel_left,
            out_expand,
            rank_out,
            select_own,
        ),
        (
            jax.ShapeDtypeStruct((half_rows, width + adapter_width), BF16),
            wide_f32,
            wide_f32,
            jax.ShapeDtypeStruct((3, grad_rows, width), grad_type),
        ),
        scratch=(work_space, kept_space),
        tables=(weight_order_table, own_pick),
    )
    if not aligned:
        grad_sent = jnp.concatenate(
            [column_blocks(grad_sent[:, :width], weight_order), grad_sent[:, width:]], axis=1
        )
    grad_joined = both_halves(grad_sent, other_core(grad_sent))
    grad_attn = grad_joined[:, :width]
    grad_rank_out = grad_joined[:, width:]
    out_shrink_grad = summed(grad_rank_out, heads_low)
    grad_heads = low(slab_product(grad_attn, out_slabs) + product(grad_rank_out, out_shrink))

    grad_queries, keys_near, keys_far, values_near, values_far = attend_back(
        tables, query_low, kv_all, heads_low, lse, grad_heads, groups, heads_local, head_dim
    )

    keys_come, values_come = flip(keys_far, y_bit), flip(values_far, x_bit)
    keep = keys_near.shape[0] // 2

    def sum_of(own, arrived, rows):
        return low(own[rows].astype(F32) + arrived[rows])

    keys_far = flip(sum_of(keys_near, keys_come, slice(keep, None)), x_bit)
    values_far = flip(sum_of(values_near, values_come, slice(keep, None)), y_bit)
    near_rows = slice(None, keep)
    grad_keys = low(keys_near[near_rows].astype(F32) + keys_come[near_rows] + keys_far)
    grad_values = low(values_near[near_rows].astype(F32) + values_come[near_rows] + values_far)

    def collect(value):
        total = value[0].astype(F32)
        for i in range(1, rest):
            mask = sum(((i >> j) & 1) << bit for j, bit in enumerate(rest_bits))
            total = total + lax.ppermute(
                value[i], "ctx", [(d, d ^ mask) for d in range(count_ctx)]
            )
        return total.reshape(local_rows, -1)

    grad_kv_own = jnp.concatenate([collect(grad_keys), collect(grad_values)], axis=1)

    grad_query_proj = low(jax.vjp(query_piece, query_proj)[1](grad_queries)[0])
    grad_key_proj = low(jax.vjp(key_piece, key_projected)[1](grad_kv_own[:, :head_dim])[0])
    grad_value_proj = low(jax.vjp(value_piece, value_projected)[1](grad_kv_own[:, head_dim:])[0])
    query_expand_grad = summed(rank_query, grad_query_proj)
    key_expand_grad = summed(rank_key, grad_key_proj)
    value_expand_grad = summed(rank_value, grad_value_proj)
    grad_kv_proj = jnp.concatenate([grad_key_proj, grad_value_proj], axis=1)
    first_part = jnp.concatenate(
        [
            against(grad_query_proj, query_maps) + against(grad_kv_proj, kv_maps),
            select * against(grad_query_proj, query_expand),
            select * against(grad_key_proj, key_widen_maps),
            select * against(grad_value_proj, value_widen_maps),
        ],
        axis=1,
    )
    input_own, first_grads = whole_call(
        last_kernel,
        (
            own_half(first_part),
            other_core(low(other_half(first_part))),
            tokens,
            gains,
            grad_scaled,
            grad_first,
            first_shrink,
        ),
        (wide_f32, jax.ShapeDtypeStruct((3, grad_rows, width), grad_type)),
        scratch=(kept_space,),
        tables=(half, own_pick),
        specs={2: half_spec},
    )

    def scatter_split(grads):
        rows = adapter_width // count_ctx
        joined = low(jnp.concatenate(grads, axis=1))
        parts = joined.reshape(count_ctx, rows, joined.shape[1])
        parts = lax.all_to_all(parts, "ctx", 0, 0, tiled=True)
        total = jnp.sum(parts.astype(F32), axis=0)
        cuts, start = [], 0
        for grad in grads:
            cuts.append(total[:, start : start + grad.shape[1]])
            start += grad.shape[1]
        return cuts

    def scatter_team(grads):
        rows = adapter_width // count_ctx
        joined = low(grads).reshape(3, count_ctx, rows, hidden_slice)
        parts = joined.transpose(1, 0, 2, 3).reshape(count_ctx, 3 * rows, hidden_slice)
        parts = lax.all_to_all(parts, "ctx", 0, 0, tiled=True)
        teams = [
            sum(parts[i].astype(F32) for i in range(count_ctx) if (i >> 1) & 3 == t)
            for t in range(4)
        ]
        total = jnp.concatenate(teams, axis=1)
        return [total[i * rows : (i + 1) * rows] for i in range(3)]

    def scatter_shared(grads):
        rows = adapter_width // (2 * count_ctx)
        shaped = grads.reshape(grads.shape[0], count_ctx, 2, rows, width)
        keep = lax.dynamic_index_in_dim(shaped, core, 2, keepdims=False)
        send = lax.dynamic_index_in_dim(shaped, 1 - core, 2, keepdims=False)
        joined = low(keep + other_core(low(send)).astype(F32))
        parts = joined.transpose(1, 0, 2, 3).reshape(count_ctx, grads.shape[0] * rows, width)
        parts = lax.all_to_all(parts, "ctx", 0, 0, tiled=True)
        total = jnp.sum(parts.astype(F32), axis=0)
        return [total[i * rows : (i + 1) * rows] for i in range(grads.shape[0])]

    def one_adapter(grad):
        return low(lax.dynamic_slice_in_dim(grad, own_pick[0] * ADAPTER_RANK, ADAPTER_RANK, 0))

    def core_rows(grads):
        shaped = grads.reshape(grads.shape[0], 2, 2, 4, width)
        keep = lax.dynamic_index_in_dim(shaped, core, 2, keepdims=False).astype(F32)
        send = lax.dynamic_index_in_dim(shaped, 1 - core, 2, keepdims=False)
        return low(keep + other_core(send)).transpose(1, 0, 2, 3).reshape(2, -1, width)

    def deliver(load):
        loads = [load] + [
            lax.ppermute(load, "ctx", [(d, d ^ (4 * r)) for d in range(count_ctx)])
            for r in range(1, count_ctx // 4)
        ]
        picks = [
            jnp.sum(jnp.where(device_ids == (me ^ (4 * r)), pick_of[:, 0], 0))
            for r in range(count_ctx // 4)
        ]
        total = 0.0
        for m in (3, 1, 2, 0):
            place = (me & 3) ^ m
            wanted = (me >> 2) * 2 + (place >> 1)
            sent = sum(
                jnp.where(
                    pick == wanted,
                    lax.dynamic_index_in_dim(each, place & 1, 0, keepdims=False).astype(F32),
                    0.0,
                )
                for pick, each in zip(picks, loads)
            )
            if m:
                sent = lax.ppermute(low(sent), "ctx", [(d, d ^ m) for d in range(count_ctx)])
            total = total + sent.astype(F32)
        return total

    gate_expand_out, up_expand_out, down_shrink_out = scatter_team(team_grads)
    if compact:
        shared = core_rows(jnp.concatenate([own_grads, down_expand_grad[None]], axis=0))
        split = one_adapter(out_shrink_grad).reshape(2, 8, -1)
        split = jnp.pad(split, ((0, 0), (0, 0), (0, width - split.shape[2])))
        found = deliver(jnp.concatenate([shared, split], axis=1))
        gate_shrink_out, up_shrink_out, out_expand_out, down_expand_out = (
            found[4 * i : 4 * i + 4] for i in range(4)
        )
        out_shrink_out = found[16:, : out_shrink_grad.shape[1]]
        expands = [one_adapter(g) for g in (query_expand_grad, key_expand_grad, value_expand_grad)]
        sizes = [g.shape[1] for g in expands]
        split = jnp.concatenate(expands, axis=1).reshape(2, 8, -1)
        split = jnp.pad(split, ((0, 0), (0, 0), (0, width - split.shape[2])))
        found = deliver(jnp.concatenate([core_rows(first_grads), split], axis=1))
        query_shrink_out, key_shrink_out, value_shrink_out = (
            found[4 * i : 4 * i + 4] for i in range(3)
        )
        query_expand_out = found[12:, : sizes[0]]
        key_expand_out = found[12:, sizes[0] : sizes[0] + sizes[1]]
        value_expand_out = found[12:, sizes[0] + sizes[1] : sum(sizes)]
    else:
        (out_shrink_out,) = scatter_split([out_shrink_grad])
        gate_shrink_out, up_shrink_out, out_expand_out, down_expand_out = scatter_shared(
            jnp.concatenate([own_grads, down_expand_grad[None]], axis=0)
        )
        query_expand_out, key_expand_out, value_expand_out = scatter_split(
            [query_expand_grad, key_expand_grad, value_expand_grad]
        )
        query_shrink_out, key_shrink_out, value_shrink_out = scatter_shared(first_grads)

    return (
        both_halves(result_own, other_core(result_own)),
        both_halves(input_own, other_core(input_own)),
        both_halves(layer_input_own, other_core(layer_input_own)),
        query_shrink_out,
        key_shrink_out,
        value_shrink_out,
        gate_shrink_out,
        up_shrink_out,
        out_shrink_out,
        down_shrink_out,
        query_expand_out,
        key_expand_out,
        value_expand_out,
        gate_expand_out,
        up_expand_out,
        out_expand_out,
        down_expand_out,
    )


def solution(mesh):
    in_specs = (
        P("ctx", None),
        P("ctx", None),
        P("ctx", None),
        P(),
        P(),
        P(),
        P(),
        P("ctx", "wt"),
        P("ctx", "wt"),
        P("ctx", "wt"),
        P("ctx", "wt"),
        P("ctx", "wt"),
        P("wt", "ctx"),
        P("wt", "ctx"),
        P(),
        P(),
        P(),
        P(),
        P(),
        P(),
        P(),
        P(),
        P(),
        P(None, "wt"),
        P(None, "wt"),
        P(None, "wt"),
        P(None, "wt"),
        P(None, "wt"),
        P(None, "wt"),
        P(None, "wt"),
        P(),
        P(),
    )
    out_specs = (
        P("ctx", None),
        P("ctx", None),
        P("ctx", None),
        P(("ctx", "wt"), None),
        P(("ctx", "wt"), None),
        P(("ctx", "wt"), None),
        P(("ctx", "wt"), None),
        P(("ctx", "wt"), None),
        P("ctx", "wt"),
        P("ctx", "wt"),
        P("ctx", "wt"),
        P("ctx", "wt"),
        P("ctx", "wt"),
        P("ctx", "wt"),
        P("ctx", "wt"),
        P(("ctx", "wt"), None),
        P(("ctx", "wt"), None),
    )
    return jax.shard_map(local, mesh=mesh, in_specs=in_specs, out_specs=out_specs, check_vma=False)
```

```python
import jax
import jax.numpy as jnp
from jax import lax
from jax.experimental import pallas as pl
from jax.experimental.pallas import tpu as pltpu
from jax.sharding import PartitionSpec as P

QUERY_HEADS = 8
KEY_VALUE_HEADS = 2
ADAPTER_COUNT = 8
ADAPTER_RANK = 16
PROMPT = 2048
CONT = 256

EPS = 1e-06
THETA = 1000000.0
ROOT_HALF = 0.5**0.5
F32 = jnp.float32
BF16 = jnp.bfloat16
SWAP = [(0, 1), (1, 0)]


def normalized(inputs, norm_gain):
    return inputs * lax.rsqrt(jnp.mean(inputs * inputs, axis=-1, keepdims=True) + EPS) * norm_gain


def rotary_applied(inputs, cosine, sine_term):
    half_width = inputs.shape[-1] // 2
    first_half = inputs[..., :half_width]
    second_half = inputs[..., half_width:]
    return jnp.concatenate(
        [
            first_half * cosine - second_half * sine_term,
            second_half * cosine + first_half * sine_term,
        ],
        axis=-1,
    )


def product(left_side, right_side):
    return jnp.dot(left_side, right_side, preferred_element_type=F32)


def against(left_side, right_side):
    return lax.dot_general(
        left_side, right_side, (((1,), (1,)), ((), ())), preferred_element_type=F32
    )


def summed(left_side, right_side):
    return lax.dot_general(
        left_side, right_side, (((0,), (0,)), ((), ())), preferred_element_type=F32
    )


def low(value):
    return value.astype(BF16)


def attend_kernel(count_ref, slot_ref, kslot_ref, vslot_ref, q_ref, kv_ref, o_ref, lse_ref, acc, tot, *, heads, dim):
    group = pl.program_id(0)
    count = count_ref[group]
    rows = q_ref.shape[0]
    fold = tot.shape[-1]
    acc[...] = jnp.zeros_like(acc)
    tot[...] = jnp.zeros_like(tot)

    def step(index, masked):
        keys = kv_ref[slot_ref[group, index], 0, :, :dim]
        values = kv_ref[slot_ref[group, index], 0, :, dim:]
        for head in range(heads):
            lanes = slice(head * dim, (head + 1) * dim)
            scores = against(q_ref[:, lanes], keys)
            weights = jnp.exp(scores)
            if masked:
                row = lax.broadcasted_iota(jnp.int32, scores.shape, 0)
                col = lax.broadcasted_iota(jnp.int32, scores.shape, 1)
                weights = jnp.where(col <= row, weights, 0.0)
            part = weights[:, :fold]
            for start in range(fold, rows, fold):
                part = part + weights[:, start : start + fold]
            tot[head] += part
            acc[:, lanes] += product(low(weights), values)

    def body(index, carry):
        step(index, False)
        return carry

    lax.fori_loop(0, count - 1, body, 0)
    step(count - 1, True)
    lane = lax.broadcasted_iota(jnp.int32, lse_ref.shape, 1)
    lse = jnp.zeros(lse_ref.shape, F32)
    for head in range(heads):
        lanes = slice(head * dim, (head + 1) * dim)
        total = jnp.sum(tot[head], axis=-1, keepdims=True)
        o_ref[:, lanes] = low(acc[:, lanes] / total)
        lse = jnp.where(lane == head, jnp.log(total), lse)
    lse_ref[...] = lse


def attend_back_kernel(
    count_ref, slot_ref, kslot_ref, vslot_ref, q_ref, kv_ref, o_ref, lse_ref, g_ref, dq_ref, dk_near, dk_far, dv_near, dv_far, delta, *, heads, dim
):
    group = pl.program_id(0)
    count = count_ref[group]
    dq_ref[...] = jnp.zeros_like(dq_ref)
    for out_ref in (dk_near, dk_far, dv_near, dv_far):
        out_ref[...] = jnp.zeros_like(out_ref)
    half = dk_near.shape[0]

    def put(near_ref, far_ref, slot, value):
        @pl.when(slot < half)
        def _():
            near_ref[slot, 0] = low(value)

        @pl.when(slot >= half)
        def _():
            far_ref[slot - half, 0] = low(value)

    for head in range(heads):
        lanes = slice(head * dim, (head + 1) * dim)
        delta[head] = jnp.sum(
            o_ref[:, lanes].astype(F32) * g_ref[:, lanes].astype(F32), axis=-1, keepdims=True
        )

    def step(index, masked):
        keys = kv_ref[slot_ref[group, index], 0, :, :dim]
        values = kv_ref[slot_ref[group, index], 0, :, dim:]
        dk = jnp.zeros(keys.shape, F32)
        dv = jnp.zeros(values.shape, F32)
        for head in range(heads):
            lanes = slice(head * dim, (head + 1) * dim)
            queries = q_ref[:, lanes]
            upstream = g_ref[:, lanes]
            scores = against(queries, keys)
            weights = jnp.exp(scores - lse_ref[:, head : head + 1])
            if masked:
                row = lax.broadcasted_iota(jnp.int32, scores.shape, 0)
                col = lax.broadcasted_iota(jnp.int32, scores.shape, 1)
                weights = jnp.where(col <= row, weights, 0.0)
            grad_weights = against(upstream, values)
            grad_scores = low(weights * (grad_weights - delta[head]))
            dq_ref[:, lanes] += product(grad_scores, keys)
            dk += summed(grad_scores, queries)
            dv += summed(low(weights), upstream)
        put(dk_near, dk_far, kslot_ref[group, index], dk)
        put(dv_near, dv_far, vslot_ref[group, index], dv)

    def body(index, carry):
        step(index, False)
        return carry

    lax.fori_loop(0, count - 1, body, 0)
    step(count - 1, True)


def attend(tables, queries, kv_all, groups, heads, dim):
    slots, _, block, _ = kv_all.shape
    rows = queries.shape[0]
    fold = min(128, block)
    whole = pl.BlockSpec((slots, 1, block, 2 * dim), lambda g, *_: (0, g, 0, 0))
    mine = pl.BlockSpec((block, heads * dim), lambda g, *_: (g, 0))
    return pl.pallas_call(
        lambda *refs: attend_kernel(*refs, heads=heads, dim=dim),
        grid_spec=pltpu.PrefetchScalarGridSpec(
            num_scalar_prefetch=4,
            grid=(groups,),
            in_specs=[mine, whole],
            out_specs=[mine, pl.BlockSpec((block, 128), lambda g, *_: (g, 0))],
            scratch_shapes=[
                pltpu.VMEM((block, heads * dim), F32),
                pltpu.VMEM((heads, block, fold), F32),
            ],
        ),
        out_shape=[
            jax.ShapeDtypeStruct((rows, heads * dim), BF16),
            jax.ShapeDtypeStruct((rows, 128), F32),
        ],
        compiler_params=pltpu.CompilerParams(vmem_limit_bytes=40 * 2**20),
        cost_estimate=pl.CostEstimate(
            flops=4 * rows * heads * dim * 2304, bytes_accessed=6 * 2**20, transcendentals=rows * heads * 2304
        ),
    )(*tables, queries, kv_all)


def attend_back(tables, queries, kv_all, heads_low, lse, grads, groups, heads, dim):
    slots, _, block, _ = kv_all.shape
    rows = queries.shape[0]
    whole = pl.BlockSpec((slots, 1, block, 2 * dim), lambda g, *_: (0, g, 0, 0))
    part = pl.BlockSpec((slots // 2, 1, block, dim), lambda g, *_: (0, g, 0, 0))
    mine = pl.BlockSpec((block, heads * dim), lambda g, *_: (g, 0))
    return pl.pallas_call(
        lambda *refs: attend_back_kernel(*refs, heads=heads, dim=dim),
        grid_spec=pltpu.PrefetchScalarGridSpec(
            num_scalar_prefetch=4,
            grid=(groups,),
            in_specs=[mine, whole, mine, pl.BlockSpec((block, 128), lambda g, *_: (g, 0)), mine],
            out_specs=[mine] + [part] * 4,
            scratch_shapes=[pltpu.VMEM((heads, block, 1), F32)],
        ),
        out_shape=[
            jax.ShapeDtypeStruct((rows, heads * dim), F32),
        ]
        + [jax.ShapeDtypeStruct((slots // 2, groups, block, dim), BF16)] * 4,
        compiler_params=pltpu.CompilerParams(vmem_limit_bytes=48 * 2**20),
        cost_estimate=pl.CostEstimate(
            flops=10 * rows * heads * dim * 2304, bytes_accessed=12 * 2**20, transcendentals=rows * heads * 2304
        ),
    )(*tables, queries, kv_all, heads_low, lse, grads)


def gelu_parts(gate):
    slope = 0.7978845608028654
    square = gate * gate
    bend = jnp.tanh(slope * gate * (1.0 + 0.044715 * square))
    half = 0.5 * (1.0 + bend)
    grad = half + 0.5 * gate * (1.0 - bend * bend) * slope * (1.0 + 0.134145 * square)
    return gate * half, grad


def rms_scale(value):
    return lax.rsqrt(jnp.mean(value * value, axis=-1, keepdims=True) + EPS)


def rms_pull(value, scale, weighted):
    return scale * weighted - value * (
        scale * scale * scale * jnp.mean(value * weighted, axis=-1, keepdims=True)
    )


def move_columns(out_ref, in_ref, table_ref, count, block):
    for j in range(count):
        start = pl.multiple_of(table_ref[j] * block, block)
        out_ref[:, j * block : (j + 1) * block] = in_ref[:, pl.ds(start, block)].astype(
            out_ref.dtype
        )


def whole_call(kernel, inputs, outputs, scratch=(), tables=(), specs=None, flops=10**9):
    specs = specs or {}

    def full(array):
        return pl.BlockSpec(array.shape, lambda *_: (0,) * len(array.shape))

    in_specs = [specs.get(i, full(array)) for i, array in enumerate(inputs)]
    size = sum(a.size * a.dtype.itemsize for a in inputs)
    return pl.pallas_call(
        kernel,
        grid_spec=pltpu.PrefetchScalarGridSpec(
            num_scalar_prefetch=len(tables),
            grid=(1,),
            in_specs=in_specs,
            out_specs=[full(array) for array in outputs],
            scratch_shapes=list(scratch),
        ),
        out_shape=list(outputs),
        compiler_params=pltpu.CompilerParams(vmem_limit_bytes=56 * 2**20),
        cost_estimate=pl.CostEstimate(flops=flops, bytes_accessed=size, transcendentals=0),
    )(*tables, *inputs)


def first_kernel(tokens_ref, gains_ref, select_ref, shrink_ref, low_ref, rank_ref):
    tokens = tokens_ref[...].astype(F32)
    first = low(tokens * rms_scale(tokens) * gains_ref[0:1, :])
    low_ref[...] = first
    ranks = against(first, shrink_ref[...])
    select = select_ref[...]
    width = select.shape[1]
    for i in range(3):
        rank_ref[:, i * width : (i + 1) * width] = low(select * ranks[:, i * width : (i + 1) * width])


def middle_kernel(
    half_ref, back_ref, own_ref, other_ref, tokens_ref, gains_ref, expand_ref, left_ref, right_ref,
    total_ref, laurel_ref, mid_ref, second_ref, rank_ref, work, *, count, block, aligned
):
    width = total_ref.shape[1]
    summed_all = own_ref[...] + other_ref[...].astype(F32)
    rank = low(summed_all[:, width:])
    rank_ref[...] = rank
    if aligned:
        work[...] = summed_all[:, :width]
        move_columns(total_ref, work, back_ref, count, block)
        attn = total_ref[...] + product(rank, expand_ref[...])
    else:
        attn = summed_all[:, :width] + product(rank, expand_ref[...])
    total_ref[...] = attn
    tokens = tokens_ref[...].astype(F32)
    first = tokens * rms_scale(tokens) * gains_ref[0:1, :]
    laurel = product(low(product(low(first), left_ref[...])), right_ref[...])
    laurel_ref[...] = laurel
    mid = (
        tokens
        + attn * rms_scale(attn) * gains_ref[1:2, :]
        + first
        + laurel * rms_scale(laurel) * gains_ref[2:3, :]
    ) * ROOT_HALF
    mid_ref[...] = mid
    second_ref[...] = low(mid * rms_scale(mid) * gains_ref[3:4, :])


def keep_rows(out_ref, work_ref, value, pick_ref):
    if out_ref.shape[0] == value.shape[0]:
        out_ref[...] = value.astype(out_ref.dtype)
    else:
        work_ref[...] = value
        rows = out_ref.shape[0]
        start = pl.multiple_of(pick_ref[0] * rows, rows)
        out_ref[...] = work_ref[pl.ds(start, rows), :].astype(out_ref.dtype)


def layer_kernel(
    half_ref, pick_ref, near_ref, y_ref, z_ref, yz_ref, mid_ref, gains_ref, expand_ref, gate_ref, lift_ref, layer_ref, up_ref,
    result_ref, layer_grad_ref, after_ref, grad_ref, expand_grad_ref, kept
):
    width = mid_ref.shape[1]
    joined = near_ref[...].astype(F32) + y_ref[...] + z_ref[...] + yz_ref[...]
    rank = low(joined[:, width:])
    total = joined[:, :width] + product(rank, expand_ref[...])
    scale = rms_scale(total)
    gain = gains_ref[4:5, :]
    after = mid_ref[...] + total * scale * gain
    layer_pre = product(low(after), gate_ref[...])
    layer_in = layer_ref[...].astype(F32)
    act, slope = gelu_parts(layer_pre)
    back = product(low(act * layer_in), lift_ref[...])
    back_scale = rms_scale(back)
    last_gain = gains_ref[5:6, :]
    result_ref[...] = low(after + back * back_scale * last_gain)
    upstream = up_ref[...].astype(F32)
    grad_back = low(rms_pull(back, back_scale, upstream * last_gain))
    grad_gated = against(grad_back, lift_ref[...])
    layer_grad_ref[...] = grad_gated * act
    grad_pre = low(grad_gated * layer_in * slope)
    grad_after = upstream + against(grad_pre, gate_ref[...])
    after_ref[...] = grad_after
    grad_ffn = low(rms_pull(total, scale, grad_after * gain))
    grad_ref[...] = grad_ffn
    keep_rows(expand_grad_ref, kept, summed(rank, grad_ffn), pick_ref)


def turn_kernel(
    order_ref, pick_ref, near_ref, y_ref, z_ref, yz_ref, mid_ref, after_ref, total_ref, laurel_ref, second_ref, gains_ref, gate_ref, up_ref,
    right_ref, left_ref, expand_ref, rank_ref, select_ref,
    sent_ref, scaled_ref, first_ref, grads_ref, work, kept, *, count, block, aligned
):
    width = mid_ref.shape[1]
    ranks = select_ref.shape[1]
    joined = near_ref[...].astype(F32) + y_ref[...] + z_ref[...] + yz_ref[...]
    rank_gate = low(joined[:, width : width + ranks])
    rank_up = low(joined[:, width + ranks :])
    grad_second = joined[:, :width]
    grad_second = grad_second + product(rank_gate, gate_ref[...]) + product(rank_up, up_ref[...])
    keep_rows(grads_ref.at[0], kept, summed(rank_gate, second_ref[...]), pick_ref)
    keep_rows(grads_ref.at[1], kept, summed(rank_up, second_ref[...]), pick_ref)
    mid = mid_ref[...]
    grad_mid = after_ref[...] + rms_pull(mid, rms_scale(mid), grad_second * gains_ref[3:4, :])
    scaled = grad_mid * ROOT_HALF
    scaled_ref[...] = scaled
    attn = total_ref[...]
    grad_attn = rms_pull(attn, rms_scale(attn), scaled * gains_ref[1:2, :])
    laurel = laurel_ref[...]
    grad_laurel = low(rms_pull(laurel, rms_scale(laurel), scaled * gains_ref[2:3, :]))
    grad_rank = low(against(grad_laurel, right_ref[...]))
    first_ref[...] = scaled + against(grad_rank, left_ref[...])
    attn_low = low(grad_attn)
    keep_rows(grads_ref.at[2], kept, summed(rank_ref[...], attn_low), pick_ref)
    sent_ref[:, width:] = low(select_ref[...] * against(attn_low, expand_ref[...]))
    if aligned:
        work[...] = grad_attn
        for j in range(count):
            start = pl.multiple_of(order_ref[j] * block, block)
            sent_ref[:, j * block : (j + 1) * block] = low(work[:, pl.ds(start, block)])
    else:
        sent_ref[:, :width] = attn_low


def last_kernel(
    half_ref, pick_ref, own_ref, other_ref, tokens_ref, gains_ref, scaled_ref, first_ref, shrink_ref,
    input_ref, grads_ref, kept
):
    width = scaled_ref.shape[1]
    joined = own_ref[...] + other_ref[...].astype(F32)
    ranks = low(joined[:, width:])
    each = ranks.shape[1] // 3
    grad_first = joined[:, :width]
    grad_first = grad_first + first_ref[...] + product(ranks, shrink_ref[...])
    tokens = tokens_ref[...].astype(F32)
    scale = rms_scale(tokens)
    gain = gains_ref[0:1, :]
    input_ref[...] = scaled_ref[...] + rms_pull(tokens, scale, grad_first * gain)
    first = low(tokens * scale * gain)
    for i in range(3):
        keep_rows(
            grads_ref.at[i], kept, summed(ranks[:, i * each : (i + 1) * each], first), pick_ref
        )


def gather_parts(out_ref, parts, table_ref, count, width):
    height = parts[0].shape[0]
    block = width // count
    for i, part in enumerate(parts):
        rows = slice(i * height, (i + 1) * height)
        if block % 128 == 0:
            for j in range(count):
                start = pl.multiple_of(table_ref[j] * block, block)
                out_ref[rows, j * block : (j + 1) * block] = part[:, pl.ds(start, block)]
        else:
            out_ref[rows, :] = part[...]


def ranks_of(out_ref, parts, select_ref, maps_ref):
    height = parts[0].shape[0]
    ranks = select_ref.shape[1]
    for i, part in enumerate(parts):
        rows = slice(i * height, (i + 1) * height)
        found = against(part[...], maps_ref[...])
        for start in range(0, out_ref.shape[1], ranks):
            out_ref[rows, start : start + ranks] = low(
                select_ref[rows, :] * found[:, start : start + ranks]
            )


def bring(pieces, space, sems):
    rows = pieces[0].shape[0]
    copies = [
        pltpu.make_async_copy(piece, space.at[pl.ds(i * rows, rows), :], sems.at[i])
        for i, piece in enumerate(pieces)
    ]
    for copy in copies:
        copy.start()
    return copies


def put_halves(refs, value, start, table_ref, block):
    half = refs[0].shape[0]
    for i, ref in enumerate(refs):
        put_columns(ref, value[i * half : (i + 1) * half], start, table_ref, block)


def put_columns(out_ref, value, start, table_ref, block):
    size = value.shape[1]
    if block % 128:
        out_ref[:, pl.ds(start, size)] = value.astype(out_ref.dtype)
        return
    for i in range(size // block):
        place = pl.multiple_of(table_ref[start // block + i] * block, block)
        out_ref[:, pl.ds(place, block)] = value[:, i * block : (i + 1) * block].astype(out_ref.dtype)


def feed_kernel(order_ref, *refs, pieces, width, count):
    parts, (select_ref, shrink_ref, gexp_ref, uexp_ref, dshr_ref), refs = refs[:4], refs[4:9], refs[9:]
    gates, ups, downs = refs[:pieces], refs[pieces : 2 * pieces], refs[2 * pieces : 3 * pieces]
    rank_ref, act_ref, slope_ref, hid_ref, near_ref, far_ref, x_ref, gate_w, up_w, down_w, sems = refs[3 * pieces :]
    arriving = bring(gates, gate_w, sems.at[0]) + bring(ups, up_w, sems.at[1])
    arriving_down = bring(downs, down_w, sems.at[2])
    ranks = select_ref.shape[1]
    hidden_width = gate_w.shape[1]
    chunk = min(1024, hidden_width)
    gather_parts(x_ref, parts, order_ref, count, width)
    ranks_of(rank_ref, parts, select_ref, shrink_ref)
    for copy in arriving:
        copy.wait()

    @pl.loop(0, hidden_width // chunk)
    def _(i):
        lanes = pl.ds(pl.multiple_of(i * chunk, chunk), chunk)
        gate = product(x_ref[...], gate_w[:, lanes]) + product(rank_ref[:, :ranks], gexp_ref[:, lanes])
        up = product(x_ref[...], up_w[:, lanes]) + product(rank_ref[:, ranks:], uexp_ref[:, lanes])
        act, slope = gelu_parts(gate)
        act_ref[:, lanes] = low(act)
        slope_ref[:, lanes] = low(slope * up)
        hid_ref[:, lanes] = low(act * up)

    for copy in arriving_down:
        copy.wait()
    step = 1024

    @pl.loop(0, width // step)
    def _(i):
        start = pl.multiple_of(i * step, step)
        found = against(hid_ref[...], down_w[pl.ds(start, step), :])
        put_halves((near_ref, far_ref), found, start, order_ref, width // count)

    found = low(select_ref[...] * against(hid_ref[...], dshr_ref[...]))
    half = near_ref.shape[0]
    near_ref[:, width:] = found[:half]
    far_ref[:, width:] = found[half:]


def feed_call(kernel, order, parts, inputs, weights, outputs, scratch, flops):
    def full(array):
        return pl.BlockSpec(array.shape, lambda *_: (0,) * len(array.shape))

    pieces = [piece for matrix in weights for piece in matrix]
    matrix = pltpu.VMEM((len(weights[0]) * weights[0][0].shape[0], weights[0][0].shape[1]), BF16)
    width = parts[0].shape[1]
    return pl.pallas_call(
        lambda *refs: kernel(*refs, pieces=len(weights[0]), width=width, count=order.shape[0]),
        grid_spec=pltpu.PrefetchScalarGridSpec(
            num_scalar_prefetch=1,
            grid=(1,),
            in_specs=[full(array) for array in (*parts, *inputs)]
            + [pl.BlockSpec(memory_space=pl.ANY)] * len(pieces),
            out_specs=[full(array) for array in outputs],
            scratch_shapes=list(scratch)
            + [matrix, matrix, matrix, pltpu.SemaphoreType.DMA((3, len(weights[0])))],
        ),
        out_shape=list(outputs),
        compiler_params=pltpu.CompilerParams(vmem_limit_bytes=58 * 2**20),
        cost_estimate=pl.CostEstimate(flops=flops, bytes_accessed=20 * 2**20, transcendentals=0),
    )(order, *parts, *inputs, *pieces)


def feed(order, parts, select, shrink, gexp, uexp, dshr, gates, ups, downs):
    rows, width = 4 * parts[0].shape[0], parts[0].shape[1]
    hidden, ranks = gexp.shape[1], select.shape[1]
    low_hidden = jax.ShapeDtypeStruct((rows, hidden), BF16)
    return feed_call(
        feed_kernel,
        order,
        parts,
        (select, shrink, gexp, uexp, dshr),
        (gates, ups, downs),
        (
            jax.ShapeDtypeStruct((rows, 2 * ranks), BF16),
            low_hidden,
            low_hidden,
            low_hidden,
            *[jax.ShapeDtypeStruct((rows // 2, width + ranks), BF16)] * 2,
        ),
        (pltpu.VMEM((rows, width), BF16),),
        6 * rows * width * hidden,
    )


def feed_back_kernel(order_ref, *refs, pieces, width, count):
    parts, refs = refs[:4], refs[4:]
    (
        select_ref,
        dexp_ref,
        rank_ref,
        start_ref,
        act_ref,
        slope_ref,
        hid_ref,
        gexp_ref,
        uexp_ref,
        dshr_ref,
    ), refs = refs[:10], refs[10:]
    gates, ups, downs = refs[:pieces], refs[pieces : 2 * pieces], refs[2 * pieces : 3 * pieces]
    near_ref, far_ref, grads_ref, g_ref, down_rank, gate_grad, up_grad, gate_w, up_w, down_w, sems = refs[3 * pieces :]
    arriving = bring(downs, down_w, sems.at[2])
    arriving_next = bring(gates, gate_w, sems.at[0]) + bring(ups, up_w, sems.at[1])
    ranks = select_ref.shape[1]
    hidden_width = gate_w.shape[1]
    chunk = min(1024, hidden_width)
    gather_parts(g_ref, parts, order_ref, count, width)
    ranks_of(down_rank, parts, select_ref, dexp_ref)
    for copy in arriving:
        copy.wait()

    @pl.loop(0, hidden_width // chunk)
    def _(i):
        lanes = pl.ds(pl.multiple_of(i * chunk, chunk), chunk)
        grad_hidden = product(g_ref[...], down_w[:, lanes]) + product(down_rank[...], dshr_ref[:, lanes])
        grad_gate = low(grad_hidden * slope_ref[:, lanes].astype(F32))
        grad_up = low(grad_hidden * act_ref[:, lanes].astype(F32))
        gate_grad[:, lanes] = grad_gate
        up_grad[:, lanes] = grad_up
        grads_ref[0, :, lanes] = start_ref[0, :, lanes] + summed(rank_ref[:, :ranks], grad_gate)
        grads_ref[1, :, lanes] = start_ref[1, :, lanes] + summed(rank_ref[:, ranks:], grad_up)
        grads_ref[2, :, lanes] = start_ref[2, :, lanes] + summed(down_rank[...], hid_ref[:, lanes])

    for copy in arriving_next:
        copy.wait()
    step = 1024

    @pl.loop(0, width // step)
    def _(i):
        start = pl.multiple_of(i * step, step)
        found = against(gate_grad[...], gate_w[pl.ds(start, step), :]) + against(
            up_grad[...], up_w[pl.ds(start, step), :]
        )
        put_halves((near_ref, far_ref), found, start, order_ref, width // count)

    select = select_ref[...]
    gate_found = low(select * against(gate_grad[...], gexp_ref[...]))
    up_found = low(select * against(up_grad[...], uexp_ref[...]))
    half = near_ref.shape[0]
    for i, ref in enumerate((near_ref, far_ref)):
        ref[:, width : width + ranks] = gate_found[i * half : (i + 1) * half]
        ref[:, width + ranks :] = up_found[i * half : (i + 1) * half]


def feed_back(order, parts, select, dexp, start, kept, gexp, uexp, dshr, gates, ups, downs):
    rows, width = 4 * parts[0].shape[0], parts[0].shape[1]
    hidden, ranks = gexp.shape[1], select.shape[1]
    low_hidden = pltpu.VMEM((rows, hidden), BF16)
    return feed_call(
        feed_back_kernel,
        order,
        parts,
        (select, dexp, kept[0], start, *kept[1:], gexp, uexp, dshr),
        (gates, ups, downs),
        (
            *[jax.ShapeDtypeStruct((rows // 2, width + 2 * ranks), BF16)] * 2,
            jax.ShapeDtypeStruct((3, ranks, hidden), F32),
        ),
        (pltpu.VMEM((rows, width), BF16), pltpu.VMEM((rows, ranks), BF16), low_hidden, low_hidden),
        6 * rows * width * hidden,
    )


def local(
    tokens,
    layer_input,
    out_grad,
    block_device,
    adapter_pick,
    norm_gains,
    head_norm_gains,
    query_weight,
    key_matrix,
    value_matrix,
    gate_weight,
    up_weight,
    out_weight,
    down_weight,
    laurel_left,
    laurel_right,
    layer_gate,
    layer_lift,
    query_shrink,
    key_shrink,
    value_shrink,
    gate_shrink,
    up_shrink,
    out_shrink,
    down_shrink,
    query_expand,
    key_widen_maps,
    value_widen_maps,
    gate_expand,
    up_expand,
    out_expand,
    down_expand,
):
    count_ctx = lax.axis_size("ctx")
    bit_count = count_ctx.bit_length() - 1
    groups = block_device.shape[0]
    local_rows, width = tokens.shape
    block_len = local_rows // groups
    half_rows = local_rows // 2
    head_dim = head_norm_gains.shape[1]
    heads_local = query_weight.shape[1] // head_dim
    adapter_width = ADAPTER_COUNT * ADAPTER_RANK
    model_block = width // count_ctx
    hidden_slice = gate_weight.shape[1] // 4
    me = lax.axis_index("ctx")
    core = lax.axis_index("wt")

    spread_bits = list(range(3, bit_count)) + [0]
    team_place = (me >> 1) & 3

    def flip(value, bit):
        return lax.ppermute(value, "ctx", [(i, i ^ (1 << bit)) for i in range(count_ctx)])

    def other_core(value):
        return lax.ppermute(value, "wt", SWAP)

    def own_half(value):
        return lax.dynamic_slice_in_dim(value, core * half_rows, half_rows, 0)

    def other_half(value):
        return lax.dynamic_slice_in_dim(value, (1 - core) * half_rows, half_rows, 0)

    def both_halves(own, other):
        return jnp.where(
            core == 0, jnp.concatenate([own, other], axis=0), jnp.concatenate([other, own], axis=0)
        )

    def column_blocks(value, places):
        return jnp.concatenate(
            [
                lax.dynamic_slice_in_dim(value, place * model_block, model_block, 1)
                for place in places
            ],
            axis=1,
        )

    rest = count_ctx // 4
    rest_bits = list(range(2, bit_count))

    def rest_place(apart):
        return sum(((apart >> bit) & 1) << i for i, bit in enumerate(rest_bits))

    weight_order = [
        me
        ^ (
            (j // (2 * rest)) * 2
            + (j // rest) % 2
            + sum(((j >> i) & 1) << bit for i, bit in enumerate(rest_bits))
        )
        for j in range(count_ctx)
    ]
    weight_back = [
        (((d ^ me) >> 1) & 1) * 2 * rest + ((d ^ me) & 1) * rest + rest_place(d ^ me)
        for d in range(count_ctx)
    ]
    piece_masks = [0]
    for bit in spread_bits:
        piece_masks = piece_masks + [mask | (1 << bit) for mask in piece_masks]
    team_order = [me ^ mask ^ (2 * t) for mask in piece_masks for t in range(4)]
    team_back = [
        4 * sum((((b ^ me) >> bit) & 1) << i for i, bit in enumerate(spread_bits))
        + (((b ^ me) >> 1) & 3)
        for b in range(count_ctx)
    ]

    def to_member(value, member):
        if member == 0:
            return value
        return lax.ppermute(value, "ctx", [(d, d ^ (2 * member)) for d in range(count_ctx)])

    def team_split(shard):
        parts = [
            to_member(
                lax.dynamic_slice_in_dim(
                    shard, (team_place ^ member) * hidden_slice, hidden_slice, 1
                ),
                member,
            )
            for member in range(4)
        ]
        return joined(parts[0], parts[1]), joined(parts[2], parts[3])

    def joined(own, arrived):
        return jnp.concatenate([own, arrived], axis=0)

    prompt_blocks = PROMPT // block_len
    cont_blocks = CONT // block_len
    device_ids = jnp.arange(count_ctx, dtype=jnp.int32)
    block_of = jnp.sum(
        jnp.where(block_device[None] == device_ids[:, None, None], device_ids[None, None, :], 0),
        axis=2,
    )
    cont_of = (block_of - prompt_blocks) // cont_blocks
    pick_of = jnp.sum(
        jnp.where(
            cont_of[:, :, None] == jnp.arange(adapter_pick.shape[1], dtype=jnp.int32),
            adapter_pick[None],
            0,
        ),
        axis=2,
    )
    pick_of = jnp.where(block_of < prompt_blocks, -1, pick_of)
    compact = groups == 1 and count_ctx * 8 == adapter_width
    own_pick = jnp.maximum(jnp.sum(jnp.where(device_ids[:, None] == me, pick_of, 0), axis=0), 0)
    own_pick = own_pick[:1].astype(jnp.int32)
    grad_rows = ADAPTER_RANK if compact else adapter_width
    grad_type = BF16 if compact else F32

    def picks_at(device):
        return jnp.sum(jnp.where(device_ids[:, None] == device, pick_of, 0), axis=0)

    def select_rows(picks):
        rows = jnp.repeat(picks, block_len)
        return (
            jnp.arange(adapter_width, dtype=jnp.int32)[None, :] // ADAPTER_RANK == rows[:, None]
        ).astype(F32)

    select = select_rows(picks_at(me))
    select_own = own_half(select)
    team_select = [select_rows(picks_at(me ^ (2 * t))) for t in range(4)]

    def select_of(members):
        return jnp.concatenate(
            [own_half(team_select[m]) for m in members] + [other_half(team_select[m]) for m in members],
            axis=0,
        )

    beside, across = (1, 2), (0, 3)
    select_beside, select_across = select_of(beside), select_of(across)

    my_block = jnp.sum(jnp.where(device_ids[:, None] == me, block_of, 0), axis=0)
    positions = (
        my_block[:, None] * block_len + jnp.arange(block_len, dtype=jnp.int32)[None, :]
    ).reshape(-1)
    seq_pos = jnp.where(positions < PROMPT, positions, PROMPT + (positions - PROMPT) % CONT)
    frequency = THETA ** (-2.0 * jnp.arange(head_dim // 2, dtype=F32) / head_dim)
    rotary_angles = seq_pos.astype(F32)[:, None] * frequency[None, :]
    cosine = jnp.cos(rotary_angles)[:, None, :]
    sine_term = jnp.sin(rotary_angles)[:, None, :]
    cont_start = prompt_blocks + (my_block - prompt_blocks) // cont_blocks * cont_blocks
    is_prompt = my_block < prompt_blocks
    visible_count = jnp.where(
        is_prompt, my_block + 1, prompt_blocks + my_block - cont_start + 1
    ).astype(jnp.int32)
    entries = jnp.arange(prompt_blocks + cont_blocks, dtype=jnp.int32)
    visible_block = jnp.where(
        is_prompt[:, None] | (entries < prompt_blocks)[None, :],
        entries[None, :],
        cont_start[:, None] + entries[None, :] - prompt_blocks,
    )
    visible_device = jnp.sum(
        jnp.where(
            visible_block[:, :, None] == device_ids[None, None, :], block_device[:, None, :], 0
        ),
        axis=2,
    )
    apart = visible_device ^ me
    key_slot = (((apart >> 1) & 1) * 2 + (apart & 1)) * rest + rest_place(apart)
    value_slot = ((apart & 1) * 2 + ((apart >> 1) & 1)) * rest + rest_place(apart)
    tables = tuple(
        table.astype(jnp.int32) for table in (visible_count, visible_device, key_slot, value_slot)
    )

    gains = norm_gains.astype(F32)
    query_gain = head_norm_gains[0].astype(F32)
    key_gain = head_norm_gains[1].astype(F32)

    def query_piece(projected):
        return (
            rotary_applied(
                normalized(projected.reshape(local_rows, -1, head_dim), query_gain),
                cosine,
                sine_term,
            )
            * head_dim ** (-0.5)
        ).reshape(local_rows, -1)

    def key_piece(projected):
        return rotary_applied(
            normalized(projected.reshape(local_rows, -1, head_dim), key_gain), cosine, sine_term
        ).reshape(local_rows, -1)

    def value_piece(projected):
        return normalized(projected.reshape(local_rows, -1, head_dim), 1.0).reshape(local_rows, -1)

    def slab_product(value, slabs):
        middle = value.shape[1] // 2
        return product(value[:, :middle], slabs[0]) + product(value[:, middle:], slabs[1])

    def slab_against(value, slabs):
        return jnp.concatenate([against(value, slabs[0]), against(value, slabs[1])], axis=1)

    half = jnp.reshape(core, (1,)).astype(jnp.int32)
    aligned = model_block % 128 == 0
    style = dict(count=count_ctx, block=model_block, aligned=aligned)
    weight_order_table = jnp.stack(weight_order).astype(jnp.int32)
    weight_back_table = jnp.stack(weight_back).astype(jnp.int32)
    team_order_table = jnp.stack(team_order).astype(jnp.int32)
    half_spec = pl.BlockSpec((half_rows, width), lambda i, half, *_: (half[0], 0))
    wide_f32 = jax.ShapeDtypeStruct((half_rows, width), F32)
    wide_low = jax.ShapeDtypeStruct((half_rows, width), BF16)
    work_space = pltpu.VMEM((half_rows, width), F32)
    kept_space = pltpu.VMEM((adapter_width, width), F32)

    def moved(value, places):
        return value if aligned else column_blocks(value, places)

    def moved_back(value, places):
        if aligned:
            return value
        flat = value.reshape(-1, value.shape[-1])
        flat = jnp.concatenate([column_blocks(flat[:, :width], places), flat[:, width:]], axis=1)
        return flat.reshape(value.shape)

    first_shrink = jnp.concatenate([query_shrink, key_shrink, value_shrink], axis=0)
    first_low, rank_first = whole_call(
        first_kernel,
        (tokens, gains, select, first_shrink),
        (
            jax.ShapeDtypeStruct(tokens.shape, BF16),
            jax.ShapeDtypeStruct((local_rows, 3 * adapter_width), BF16),
        ),
    )
    rank_query = rank_first[:, :adapter_width]
    rank_key = rank_first[:, adapter_width : 2 * adapter_width]
    rank_value = rank_first[:, 2 * adapter_width :]

    far_bits, near_bit = spread_bits[:-1], spread_bits[-1]
    x_bit, y_bit = 0, 1
    first_bit = rest_bits[0]
    sent_before = {}

    def queued(line, value, move, depth=2):
        earlier = sent_before.setdefault(line, [])
        if len(earlier) >= depth:
            value = lax.optimization_barrier((value, earlier[-depth]))[0]
        result = move(value)
        earlier.append(result)
        return result

    def over_x(value):
        return queued("x", value, lambda v: flip(v, x_bit))

    def over_y(value):
        return queued("y", value, lambda v: flip(v, y_bit))

    def over_rest(value, bits):
        for bit in bits:
            value = joined(value, queued("z", value, lambda v, bit=bit: flip(v, bit)))
        return value

    def spread_far(piece):
        pieces = [piece]
        for bit in far_bits:
            pieces = pieces + [queued("z", other, lambda v, bit=bit: flip(v, bit)) for other in pieces]
        return pieces[1:]

    def near(pieces):
        return [over_x(piece) for piece in pieces]

    step = lax.optimization_barrier
    head_maps = lax.all_gather(
        jnp.concatenate([query_weight, key_matrix, value_matrix], axis=1), "ctx", axis=0, tiled=True
    )
    out_rows = out_weight.T
    gate_a, gate_b = team_split(gate_weight)
    up_a, up_b = team_split(up_weight)
    gate_far_a = spread_far(gate_a)
    gate_far_b = spread_far(gate_b)
    gate_near_a, gate_near_b = near([gate_a]), near([gate_b])
    up_far_a = spread_far(up_a)
    up_near_a, up_near_b = near([up_a]), near([up_b])
    gate_far_near_a = near(gate_far_a)
    head_maps, gate_far_a, gate_far_b, gate_near_a, gate_near_b, up_far_a, up_near_a, up_near_b, gate_far_near_a = step(
        (head_maps, gate_far_a, gate_far_b, gate_near_a, gate_near_b, up_far_a, up_near_a, up_near_b, gate_far_near_a)
    )
    query_width, kv_width = query_weight.shape[1], key_matrix.shape[1]
    query_maps, kv_maps = head_maps[:, :query_width], head_maps[:, query_width:]
    kv_projected = product(first_low, kv_maps)
    key_projected = kv_projected[:, :kv_width] + product(rank_key, key_widen_maps)
    value_projected = kv_projected[:, kv_width:] + product(rank_value, value_widen_maps)
    kv_low = jnp.concatenate([low(key_piece(key_projected)), low(value_piece(value_projected))], axis=1)
    kv_all = lax.all_gather(kv_low, "ctx", axis=0, tiled=True).reshape(
        count_ctx, groups, block_len, 2 * head_dim
    )
    query_proj = product(first_low, query_maps) + product(rank_query, query_expand)
    query_low = low(query_piece(query_proj))
    down_a, down_b = team_split(down_weight.T)
    up_far_b = spread_far(up_b)
    out_part = joined(out_rows, flip(out_rows, first_bit))
    out_part = over_rest(out_part, rest_bits[1:])
    out_slab = joined(out_part, over_x(out_part))
    out_slabs = out_slab, over_y(out_slab)
    gate_far_near_b = near(gate_far_b)
    up_far_near_a = near(up_far_a)
    down_far_a, down_far_b = spread_far(down_a), spread_far(down_b)
    down_near_a, down_near_b = near([down_a]), near([down_b])
    up_far_near_b = near(up_far_b)
    kv_all, down_far_a, up_far_near_a, up_far_b, out_slab, gate_far_near_b, down_near_a = step(
        (kv_all, down_far_a, up_far_near_a, up_far_b, out_slab, gate_far_near_b, down_near_a)
    )
    out_slabs = out_slab, out_slabs[1]
    down_far_near_a = near(down_far_a)
    heads_low, lse = attend(tables, query_low, kv_all, groups, heads_local, head_dim)

    heads_low, out_slabs, down_far_b, up_far_near_b, down_near_b = step(
        (heads_low, out_slabs, down_far_b, up_far_near_b, down_near_b)
    )
    down_far_near_b = near(down_far_b)
    attn_part = jnp.concatenate(
        [slab_against(heads_low, out_slabs), select * against(heads_low, out_shrink)], axis=1
    )
    attn_total, laurel_back, mid_stream, second_low, rank_out = whole_call(
        lambda *refs: middle_kernel(*refs, **style),
        (
            moved_back(attn_part, weight_back),
            moved_back(other_core(other_half(attn_part)), weight_back),
            tokens,
            gains,
            out_expand,
            laurel_left,
            laurel_right,
        ),
        (
            wide_f32,
            wide_f32,
            wide_f32,
            wide_low,
            jax.ShapeDtypeStruct((half_rows, adapter_width), BF16),
        ),
        scratch=(work_space,),
        tables=(half, weight_back_table),
        specs={
            0: pl.BlockSpec((half_rows, width + adapter_width), lambda i, half, *_: (half[0], 0)),
            2: half_spec,
        },
    )

    def in_order(own, far, near_own, near_far):
        first, second = ([o] + f + n + nf for o, f, n, nf in zip(own, far, near_own, near_far))
        return [piece for pair in zip(first, second) for piece in pair]

    gate_pieces = in_order(
        (gate_a, gate_b),
        (gate_far_a, gate_far_b),
        (gate_near_a, gate_near_b),
        (gate_far_near_a, gate_far_near_b),
    )
    up_pieces = in_order(
        (up_a, up_b), (up_far_a, up_far_b), (up_near_a, up_near_b), (up_far_near_a, up_far_near_b)
    )
    down_pieces = in_order(
        (down_a, down_b),
        (down_far_a, down_far_b),
        (down_near_a, down_near_b),
        (down_far_near_a, down_far_near_b),
    )

    def in_two_calls(value, call):
        near_parts = [to_member(value, member) for member in (1, 2, 3)]
        first_rows = near_parts[:2] + [other_core(part) for part in near_parts[:2]]
        near_sum, far_sum, *kept_first = call(0, first_rows, None)
        near_sum, far_sum, kept_first, last_part = step(
            (near_sum, far_sum, tuple(kept_first), near_parts[2])
        )
        arrived = other_core(far_sum)
        totals = [
            low(near_sum[i * half_rows : (i + 1) * half_rows].astype(F32) + arrived[i * half_rows : (i + 1) * half_rows])
            for i in range(2)
        ]
        second_rows = [value, last_part, other_core(value), other_core(last_part)]
        totals, second_rows, kept_first = step((totals, second_rows, kept_first))
        beside_parts = [to_member(total, member) for total, member in zip(totals, (1, 2))]
        near_sum, far_sum, *kept_second = call(1, second_rows, kept_first)
        far_sum, beside_parts = step((far_sum, beside_parts))
        arrived = other_core(far_sum)
        over = low(near_sum[half_rows:].astype(F32) + arrived[half_rows:])
        own = low(near_sum[:half_rows].astype(F32) + arrived[:half_rows])
        return [own] + beside_parts + [to_member(over, 3)], kept_first, kept_second

    def hidden_columns(value):
        return lax.dynamic_slice_in_dim(value, team_place * hidden_slice, hidden_slice, 1)

    feed_maps = moved(jnp.concatenate([gate_shrink, up_shrink], axis=0), team_order)
    down_map = moved(down_expand, team_order)
    slices = tuple(hidden_columns(value) for value in (gate_expand, up_expand, down_shrink))
    pieces = (gate_pieces, up_pieces, down_pieces)

    selects = select_beside, select_across

    def forward(index, rows, earlier):
        *kept, near_part, far_part = feed(
            team_order_table, rows, selects[index], feed_maps, *slices, *pieces
        )
        return near_part, far_part, *kept

    ffn_parts, *kept_calls = in_two_calls(moved(second_low, team_order), forward)

    result_own, layer_input_own, grad_after, grad_ffn, down_expand_grad = whole_call(
        layer_kernel,
        (
            *(moved_back(part, team_back) for part in ffn_parts),
            mid_stream,
            gains,
            down_expand,
            layer_gate,
            layer_lift,
            layer_input,
            out_grad,
        ),
        (
            wide_low,
            jax.ShapeDtypeStruct((half_rows, layer_input.shape[1]), F32),
            wide_f32,
            wide_low,
            jax.ShapeDtypeStruct((grad_rows, width), grad_type),
        ),
        scratch=(kept_space,),
        tables=(half, own_pick),
        specs={
            9: pl.BlockSpec((half_rows, layer_input.shape[1]), lambda i, half, *_: (half[0], 0)),
            10: half_spec,
        },
    )

    nothing = jnp.zeros((3, adapter_width, hidden_slice), F32)

    def backward(index, rows, earlier):
        return feed_back(
            team_order_table,
            rows,
            selects[index],
            down_map,
            nothing if earlier is None else earlier[0],
            kept_calls[index],
            *slices,
            *pieces,
        )

    second_parts, _, (team_grads,) = in_two_calls(moved(grad_ffn, team_order), backward)
    second_parts, team_grads = step((second_parts, team_grads))
    grad_sent, grad_scaled, grad_first, own_grads = whole_call(
        lambda *refs: turn_kernel(*refs, **style),
        (
            *(moved_back(part, team_back) for part in second_parts),
            mid_stream,
            grad_after,
            attn_total,
            laurel_back,
            second_low,
            gains,
            gate_shrink,
            up_shrink,
            laurel_right,
            laurel_left,
            out_expand,
            rank_out,
            select_own,
        ),
        (
            jax.ShapeDtypeStruct((half_rows, width + adapter_width), BF16),
            wide_f32,
            wide_f32,
            jax.ShapeDtypeStruct((3, grad_rows, width), grad_type),
        ),
        scratch=(work_space, kept_space),
        tables=(weight_order_table, own_pick),
    )
    if not aligned:
        grad_sent = jnp.concatenate(
            [column_blocks(grad_sent[:, :width], weight_order), grad_sent[:, width:]], axis=1
        )
    grad_joined = both_halves(grad_sent, other_core(grad_sent))
    grad_attn = grad_joined[:, :width]
    grad_rank_out = grad_joined[:, width:]
    out_shrink_grad = summed(grad_rank_out, heads_low)
    grad_heads = low(slab_product(grad_attn, out_slabs) + product(grad_rank_out, out_shrink))

    grad_queries, keys_near, keys_far, values_near, values_far = attend_back(
        tables, query_low, kv_all, heads_low, lse, grad_heads, groups, heads_local, head_dim
    )

    keys_come, values_come = flip(keys_far, y_bit), flip(values_far, x_bit)
    keep = keys_near.shape[0] // 2

    def sum_of(own, arrived, rows):
        return low(own[rows].astype(F32) + arrived[rows])

    keys_far = flip(sum_of(keys_near, keys_come, slice(keep, None)), x_bit)
    values_far = flip(sum_of(values_near, values_come, slice(keep, None)), y_bit)
    near_rows = slice(None, keep)
    grad_keys = low(keys_near[near_rows].astype(F32) + keys_come[near_rows] + keys_far)
    grad_values = low(values_near[near_rows].astype(F32) + values_come[near_rows] + values_far)

    def collect(value):
        total = value[0].astype(F32)
        for i in range(1, rest):
            mask = sum(((i >> j) & 1) << bit for j, bit in enumerate(rest_bits))
            total = total + lax.ppermute(
                value[i], "ctx", [(d, d ^ mask) for d in range(count_ctx)]
            )
        return total.reshape(local_rows, -1)

    grad_kv_own = jnp.concatenate([collect(grad_keys), collect(grad_values)], axis=1)

    grad_query_proj = low(jax.vjp(query_piece, query_proj)[1](grad_queries)[0])
    grad_key_proj = low(jax.vjp(key_piece, key_projected)[1](grad_kv_own[:, :head_dim])[0])
    grad_value_proj = low(jax.vjp(value_piece, value_projected)[1](grad_kv_own[:, head_dim:])[0])
    query_expand_grad = summed(rank_query, grad_query_proj)
    key_expand_grad = summed(rank_key, grad_key_proj)
    value_expand_grad = summed(rank_value, grad_value_proj)
    grad_kv_proj = jnp.concatenate([grad_key_proj, grad_value_proj], axis=1)
    first_part = jnp.concatenate(
        [
            against(grad_query_proj, query_maps) + against(grad_kv_proj, kv_maps),
            select * against(grad_query_proj, query_expand),
            select * against(grad_key_proj, key_widen_maps),
            select * against(grad_value_proj, value_widen_maps),
        ],
        axis=1,
    )
    input_own, first_grads = whole_call(
        last_kernel,
        (
            first_part,
            other_core(low(other_half(first_part))),
            tokens,
            gains,
            grad_scaled,
            grad_first,
            first_shrink,
        ),
        (wide_f32, jax.ShapeDtypeStruct((3, grad_rows, width), grad_type)),
        scratch=(kept_space,),
        tables=(half, own_pick),
        specs={
            0: pl.BlockSpec((half_rows, width + 3 * adapter_width), lambda i, half, *_: (half[0], 0)),
            2: half_spec,
        },
    )

    def scatter_split(grads):
        rows = adapter_width // count_ctx
        joined = low(jnp.concatenate(grads, axis=1))
        parts = joined.reshape(count_ctx, rows, joined.shape[1])
        parts = lax.all_to_all(parts, "ctx", 0, 0, tiled=True)
        total = jnp.sum(parts.astype(F32), axis=0)
        cuts, start = [], 0
        for grad in grads:
            cuts.append(total[:, start : start + grad.shape[1]])
            start += grad.shape[1]
        return cuts

    def scatter_team(grads):
        rows = adapter_width // count_ctx
        joined = low(grads).reshape(3, count_ctx, rows, hidden_slice)
        parts = joined.transpose(1, 0, 2, 3).reshape(count_ctx, 3 * rows, hidden_slice)
        parts = lax.all_to_all(parts, "ctx", 0, 0, tiled=True)
        teams = [
            sum(parts[i].astype(F32) for i in range(count_ctx) if (i >> 1) & 3 == t)
            for t in range(4)
        ]
        total = jnp.concatenate(teams, axis=1)
        return [total[i * rows : (i + 1) * rows] for i in range(3)]

    def scatter_shared(grads):
        rows = adapter_width // (2 * count_ctx)
        shaped = grads.reshape(grads.shape[0], count_ctx, 2, rows, width)
        keep = lax.dynamic_index_in_dim(shaped, core, 2, keepdims=False)
        send = lax.dynamic_index_in_dim(shaped, 1 - core, 2, keepdims=False)
        joined = low(keep + other_core(low(send)).astype(F32))
        parts = joined.transpose(1, 0, 2, 3).reshape(count_ctx, grads.shape[0] * rows, width)
        parts = lax.all_to_all(parts, "ctx", 0, 0, tiled=True)
        total = jnp.sum(parts.astype(F32), axis=0)
        return [total[i * rows : (i + 1) * rows] for i in range(grads.shape[0])]

    def one_adapter(grad):
        return low(lax.dynamic_slice_in_dim(grad, own_pick[0] * ADAPTER_RANK, ADAPTER_RANK, 0))

    def core_rows(grads):
        shaped = grads.reshape(grads.shape[0], 2, 2, 4, width)
        keep = lax.dynamic_index_in_dim(shaped, core, 2, keepdims=False).astype(F32)
        send = lax.dynamic_index_in_dim(shaped, 1 - core, 2, keepdims=False)
        return low(keep + other_core(send)).transpose(1, 0, 2, 3).reshape(2, -1, width)

    def deliver(load):
        loads = [load] + [
            lax.ppermute(load, "ctx", [(d, d ^ (4 * r)) for d in range(count_ctx)])
            for r in range(1, count_ctx // 4)
        ]
        picks = [
            jnp.sum(jnp.where(device_ids == (me ^ (4 * r)), pick_of[:, 0], 0))
            for r in range(count_ctx // 4)
        ]
        total = 0.0
        for m in (3, 1, 2, 0):
            place = (me & 3) ^ m
            wanted = (me >> 2) * 2 + (place >> 1)
            sent = sum(
                jnp.where(
                    pick == wanted,
                    lax.dynamic_index_in_dim(each, place & 1, 0, keepdims=False).astype(F32),
                    0.0,
                )
                for pick, each in zip(picks, loads)
            )
            if m:
                sent = lax.ppermute(low(sent), "ctx", [(d, d ^ m) for d in range(count_ctx)])
            total = total + sent.astype(F32)
        return total

    gate_expand_out, up_expand_out, down_shrink_out = scatter_team(team_grads)
    if compact:
        shared = core_rows(jnp.concatenate([own_grads, down_expand_grad[None]], axis=0))
        split = one_adapter(out_shrink_grad).reshape(2, 8, -1)
        split = jnp.pad(split, ((0, 0), (0, 0), (0, width - split.shape[2])))
        found = deliver(jnp.concatenate([shared, split], axis=1))
        gate_shrink_out, up_shrink_out, out_expand_out, down_expand_out = (
            found[4 * i : 4 * i + 4] for i in range(4)
        )
        out_shrink_out = found[16:, : out_shrink_grad.shape[1]]
        expands = [one_adapter(g) for g in (query_expand_grad, key_expand_grad, value_expand_grad)]
        sizes = [g.shape[1] for g in expands]
        split = jnp.concatenate(expands, axis=1).reshape(2, 8, -1)
        split = jnp.pad(split, ((0, 0), (0, 0), (0, width - split.shape[2])))
        found = deliver(jnp.concatenate([core_rows(first_grads), split], axis=1))
        query_shrink_out, key_shrink_out, value_shrink_out = (
            found[4 * i : 4 * i + 4] for i in range(3)
        )
        query_expand_out = found[12:, : sizes[0]]
        key_expand_out = found[12:, sizes[0] : sizes[0] + sizes[1]]
        value_expand_out = found[12:, sizes[0] + sizes[1] : sum(sizes)]
    else:
        (out_shrink_out,) = scatter_split([out_shrink_grad])
        gate_shrink_out, up_shrink_out, out_expand_out, down_expand_out = scatter_shared(
            jnp.concatenate([own_grads, down_expand_grad[None]], axis=0)
        )
        query_expand_out, key_expand_out, value_expand_out = scatter_split(
            [query_expand_grad, key_expand_grad, value_expand_grad]
        )
        query_shrink_out, key_shrink_out, value_shrink_out = scatter_shared(first_grads)

    return (
        both_halves(result_own, other_core(result_own)),
        both_halves(input_own, other_core(input_own)),
        both_halves(layer_input_own, other_core(layer_input_own)),
        query_shrink_out,
        key_shrink_out,
        value_shrink_out,
        gate_shrink_out,
        up_shrink_out,
        out_shrink_out,
        down_shrink_out,
        query_expand_out,
        key_expand_out,
        value_expand_out,
        gate_expand_out,
        up_expand_out,
        out_expand_out,
        down_expand_out,
    )


def solution(mesh):
    in_specs = (
        P("ctx", None),
        P("ctx", None),
        P("ctx", None),
        P(),
        P(),
        P(),
        P(),
        P("ctx", "wt"),
        P("ctx", "wt"),
        P("ctx", "wt"),
        P("ctx", "wt"),
        P("ctx", "wt"),
        P("wt", "ctx"),
        P("wt", "ctx"),
        P(),
        P(),
        P(),
        P(),
        P(),
        P(),
        P(),
        P(),
        P(),
        P(None, "wt"),
        P(None, "wt"),
        P(None, "wt"),
        P(None, "wt"),
        P(None, "wt"),
        P(None, "wt"),
        P(None, "wt"),
        P(),
        P(),
    )
    out_specs = (
        P("ctx", None),
        P("ctx", None),
        P("ctx", None),
        P(("ctx", "wt"), None),
        P(("ctx", "wt"), None),
        P(("ctx", "wt"), None),
        P(("ctx", "wt"), None),
        P(("ctx", "wt"), None),
        P("ctx", "wt"),
        P("ctx", "wt"),
        P("ctx", "wt"),
        P("ctx", "wt"),
        P("ctx", "wt"),
        P("ctx", "wt"),
        P("ctx", "wt"),
        P(("ctx", "wt"), None),
        P(("ctx", "wt"), None),
    )
    return jax.shard_map(local, mesh=mesh, in_specs=in_specs, out_specs=out_specs, check_vma=False)
```
